256 devices in a mesh: dp: 8 (over y, core), mp: 32 (over z, x).
Axes of the slice: x: 4, y: 4, z: 8, core: 2. Of those that a mesh axis runs over, the one named last changes fastest.
Arguments:
- tokens: bfloat16 [4096, 12288], P(('dp', 'mp')), may hold values from -6 to 6
- block_weights: float32 [384, 8, 128, 128], P('mp'), may hold values from -0.1875 to 0.1875
- block_rows: int32 [384, 8], P('mp'), may hold values from 0 to 95, all different within a row
- block_owners: int32 [384, 8, 1], P('mp'), may hold values from 0 to 7; in each aligned block of 96 rows (0 to 95, 96 to 191, ..., all dimensions but the last counted through in order) at most 18 rows name the same one
- factor_in: float32 [12288, 128], P('mp'), may hold values from -0.0546875 to 0.0546875
- factor_out: float32 [128, 49152], P(None, 'mp'), may hold values from -0.5 to 0.5
- upstream: bfloat16 [4096, 49152], P('dp', 'mp'), may hold values from -0.09375 to 0.09375
Outputs:
- hidden: bfloat16 [4096, 49152], P('dp', 'mp')
- block_grads: float32 [4608, 128, 128], P(('mp', 'dp'))
- factor_in_grad: float32 [12288, 128], P(('mp', 'dp'))
- factor_out_grad: float32 [128, 49152], P(None, ('mp', 'dp'))
The draws below stay inside these ranges and needn't reach their ends.
Inputs may be any that keep to these rules, and one draw needn't show every extreme that they name: `block_rows`: each column block names 8 different row blocks. `block_owners`: among the 96 active blocks of one index of mp (aligned runs of 12 column blocks), one index of dp owns at most 18; in some runs one owns exactly 18.
All inputs are finite; a program needn't handle non-finite values.
Results may differ from the reference program's by a relative error of at most 0.001.
Values may be sent and summed in bfloat16 or wider, within the bound.
No kernel may reach another device: no remote copies, remote signals or barrier semaphores. Data moves between devices by JAX's collectives and lax.ppermute only.
A program may use at most 128 MiB of HBM per device.

```python
import math
import jax
import jax.numpy as jnp
import numpy as np
from jax import lax

D = 12288
FF = 49152
BS = 128
KB = 8
R = 128
TOKENS = 4096
RB = 96
CBLOCKS = 384
CB_DEV = 12
BLK_MP = 96
CAP = 18
N_DP = 8
N_MP = 32


def level_of(rng, dims, pieces, low, top_value):
    level = 1.0
    for position, parts in pieces:
        draws = jax.random.uniform(jax.random.fold_in(jax.random.fold_in(rng, 6), position), (parts,), jnp.float32, low / len(pieces), top_value / len(pieces))
        level = level * jnp.repeat(jnp.exp(draws), dims[position] // parts).reshape((-1,) + (1,) * (len(dims) - 1 - position))
    return level


def different_ones(stream_key, rows, count, top, lift):
    order = jax.random.permutation(jax.random.fold_in(stream_key, 1), count)
    boost = order
    for power in range(3):
        boost = boost * boost // count
    boost = boost * lift // count
    chance = jax.random.randint(jax.random.fold_in(stream_key, 2), (rows, count), 0, 4096) + boost
    fixed_rows = jax.random.permutation(jax.random.fold_in(stream_key, 3), rows)[jnp.arange(count) % rows]
    chance = jnp.where(jnp.arange(rows)[:, None] == fixed_rows[None, :], 1 << 14, chance)
    priority = chance * count + jnp.arange(count)
    return lax.top_k(priority.astype(jnp.int32), top)[1].astype(jnp.int32)


def routed_block(rng, own, number, rows, amount, top, bound, slope):
    order = jax.random.permutation(rng, amount)
    packed, usual = shares(amount, rows * top, bound, slope, True), shares(amount, rows * top, bound, slope, False)
    places = jnp.arange(amount)

    def named(lengths, rotation):
        used = int((lengths > 0).sum())
        fixed = max(1, used // 4)
        shifted = fixed + (places - fixed + rotation * (used - fixed)) % max(1, amount - fixed)
        return jnp.zeros((amount,), jnp.int32).at[order[jnp.where(places < fixed, places, shifted)]].set(jnp.asarray(lengths, jnp.int32))

    lengths = jnp.where(number % 4 == 0, named(packed, number // 4), named(usual, number - number // 4 - 1))
    mixed = jax.random.permutation(jax.random.fold_in(own, 3), amount)
    donor, receiver = mixed[0:amount // 2 * 2:2], mixed[1:amount // 2 * 2:2]
    slack = jnp.minimum(lengths[donor] - 1, bound - lengths[receiver]) // 2
    slack = jnp.where((donor == order[0]) | (receiver == order[0]) | (lengths[receiver] == 0), 0, jnp.maximum(slack, 0))
    shifted = jax.random.randint(jax.random.fold_in(own, 4), (amount // 2,), 0, 1 << 20) % (slack + 1)
    lengths = lengths.at[donor].add(-shifted).at[receiver].add(shifted)
    members = jnp.searchsorted(jnp.cumsum(lengths), jnp.arange(rows * top), side="right").astype(jnp.int32)
    grid = members.reshape(top, rows).T
    grid = grid[jax.random.permutation(jax.random.fold_in(own, 1), rows)]
    rotation = jax.random.randint(jax.random.fold_in(own, 2), (rows, 1), 0, top)
    return jnp.take_along_axis(grid, (jnp.arange(top)[None, :] + rotation) % top, axis=1)


def shares(amount, total, limit, skew, full):
    weights = [(1 << 20) // math.isqrt(rank ** skew) + 1 for rank in range(1, amount + 1)]
    largest = limit if full else min(limit, max(-(-total // amount), total * weights[0] // sum(weights)))
    least = 1 if total - largest >= amount - 1 else 0
    holding, surplus = [largest] + [least] * (amount - 1), total - largest - least * (amount - 1)
    while surplus > 0:
        movable = [i for i in range(1, amount) if holding[i] < largest] or [i for i in range(1, amount) if holding[i] < limit]
        pool, budget = sum([weights[i] for i in movable]), surplus
        for i in movable:
            addition = min(limit - holding[i], max(1, budget * weights[i] // pool), surplus)
            holding[i] = holding[i] + addition
            surplus = surplus - addition
    return np.array(holding)


def scatter_about(stream_key, dims, spread, most, split=(), kind=jnp.bfloat16):
    values = spread * jax.random.normal(stream_key, dims, jnp.float32)
    if split:
        values = values * level_of(stream_key, dims, split, -0.22, 0.18)
    return jnp.clip(values, -most, most).astype(kind)


def setup_inputs(seed: int = 0) -> dict:
    seeds = jax.random.split(jax.random.key(seed), 8)
    tokens = scatter_about(seeds[0], (TOKENS, D), 1.0, 6.0, ((0, 256),))
    block_weights = scatter_about(seeds[1], (CBLOCKS, KB, BS, BS), (KB * BS) ** -0.5, 0.1875, ((0, 32),), jnp.float32)
    block_rows = different_ones(seeds[2], CBLOCKS, RB, KB, 0)
    block_owners_keys = jax.random.split(jax.random.fold_in(seeds[3], 1), CBLOCKS * KB // BLK_MP)
    block_owners_turns = jax.random.permutation(jax.random.fold_in(seeds[3], 3), CBLOCKS * KB // BLK_MP)
    block_owners = jax.vmap(lambda own, number: routed_block(jax.random.fold_in(seeds[3], 2), own, number, BLK_MP, N_DP, 1, CAP, 2))(block_owners_keys, block_owners_turns).reshape((CBLOCKS, KB, 1))
    factor_in = scatter_about(seeds[4], (D, R), D ** -0.5, 0.0546875, ((0, 32),), jnp.float32)
    factor_out = scatter_about(seeds[5], (R, FF), R ** -0.5, 0.5, ((1, 32),), jnp.float32)
    upstream = scatter_about(seeds[6], (TOKENS, FF), (TOKENS ** -0.5), 0.09375, ((0, 8), (1, 32)))
    return dict(tokens=tokens, block_weights=block_weights, block_rows=block_rows, block_owners=block_owners, factor_in=factor_in, factor_out=factor_out, upstream=upstream)


highest = lax.Precision.HIGHEST

def gelu_tanh(values):
    return jax.nn.gelu(values, approximate=True)

def reference(tokens, block_weights, block_rows, block_owners, factor_in, factor_out, upstream):
    inputs_f = tokens.astype(jnp.float32)
    low_act = jnp.dot(inputs_f, factor_in, precision=highest)
    feature_blocks = inputs_f.reshape(TOKENS, RB, BS)
    col_width = CB_DEV * BS
    weight_groups = block_weights.reshape(N_MP, CB_DEV, KB, BS, BS)
    row_groups = block_rows.reshape(N_MP, CB_DEV * KB)
    out_groups = jnp.transpose(factor_out.reshape(R, N_MP, col_width), (1, 0, 2))
    up_groups = jnp.transpose(upstream.reshape(TOKENS, N_MP, col_width), (1, 0, 2))

    def group_step(back_low, items):
        weights, rows, factor, pulled = items
        panels = jnp.take(feature_blocks, rows, axis=1).reshape(TOKENS, CB_DEV, KB, BS)
        sparse = jnp.einsum('tckb,ckbo->tco', panels, weights, precision=highest).reshape(TOKENS, col_width)
        preact = sparse + jnp.dot(low_act, factor, precision=highest)
        hidden, pullback = jax.vjp(gelu_tanh, preact)
        pre_grad = pullback(pulled.astype(jnp.float32))[0]
        weight_grad = jnp.einsum('tckb,tco->ckbo', panels, pre_grad.reshape(TOKENS, CB_DEV, BS), precision=highest)
        back_low = back_low + jnp.dot(pre_grad, factor.T, precision=highest)
        out_grad = jnp.dot(low_act.T, pre_grad, precision=highest)
        return (back_low, (hidden.astype(jnp.bfloat16), weight_grad, out_grad))
    back_low, outputs = lax.scan(group_step, jnp.zeros((TOKENS, R), jnp.float32), (weight_groups, row_groups, out_groups, up_groups))
    hidden_groups, weight_grads, out_grads = outputs
    hidden = jnp.transpose(hidden_groups, (1, 0, 2)).reshape(TOKENS, FF)
    factor_out_grad = jnp.transpose(out_grads, (1, 0, 2)).reshape(R, FF)
    factor_in_grad = jnp.dot(inputs_f.T, back_low, precision=highest)
    owners = block_owners.reshape(N_MP, BLK_MP)
    owner_marks = (owners[:, :, None] == jnp.arange(N_DP, dtype=jnp.int32)[None, None, :]).astype(jnp.int32)
    earlier = jnp.cumsum(owner_marks, axis=1, dtype=jnp.int32) - owner_marks
    slot_rank = lax.optimization_barrier(jnp.sum(earlier * owner_marks, axis=2, dtype=jnp.int32))
    target = jnp.arange(N_MP, dtype=jnp.int32)[:, None] * (N_DP * CAP) + owners * CAP + slot_rank
    grad_slots = jnp.zeros((N_MP * N_DP * CAP, BS, BS), jnp.float32)
    grad_slots = grad_slots.at[target.reshape(-1)].set(weight_grads.reshape(N_MP * BLK_MP, BS, BS))
    return (hidden, grad_slots, factor_in_grad, factor_out_grad)
```

```python
import functools

import jax
import jax.numpy as jnp
from jax import lax
from jax.experimental import pallas as pl
from jax.experimental.pallas import tpu as pltpu
from jax.sharding import Mesh
from jax.sharding import PartitionSpec as P

highest = lax.Precision.HIGHEST
BS = 128
ROWS = 16
NX, NZ, NY, NC = 4, 8, 4, 2
COLS = 12
KB = 8
RB = 96
CAP = 18
GROUPS = NY * NC
SLOT_ROWS = CAP * BS
FO_ROWS = COLS * BS // GROUPS
CODE_ROWS = SLOT_ROWS + FO_ROWS
PART_ROWS = CODE_ROWS + 32
FINE = 256.0


def shift(axis, size, step):
    pairs = [(i, (i + step) % size) for i in range(size)]
    return lambda value: lax.ppermute(value, axis, pairs)


def split_two(value):
    high = value.astype(jnp.bfloat16)
    low = (value - high.astype(jnp.float32)).astype(jnp.bfloat16)
    return high, low


def level_of(block):
    top = jnp.max(jnp.abs(block), axis=0, keepdims=True)
    return jnp.ceil(jnp.log2(jnp.maximum(top, 1e-30)) * FINE)


def encode(block, level):
    inverse = jnp.exp2(level * (-1.0 / FINE)) * 32700.0
    return jnp.floor(block * inverse + 0.5).astype(jnp.int32).astype(jnp.int16)


def decode(code, level):
    unit = jnp.exp2(level * (1.0 / FINE)) * (1.0 / 32700.0)
    return code.astype(jnp.int32).astype(jnp.float32) * unit


def main_kernel(
    rows_ref, where_ref, place_ref, low_ref, weight_ref, factor_ref, up_ref, *rest
):
    pieces = rest[: NX * NZ]
    hidden_ref, send_ref, keep_ref, back_ref = rest[NX * NZ : NX * NZ + 4]
    tok, wide, low_two, codes, levels, sems = rest[NX * NZ + 4 :]
    c = pl.program_id(0)
    tokens = NX * NZ * ROWS

    @pl.when(c == 0)
    def _():
        for j in range(NX * NZ):
            pltpu.make_async_copy(pieces[j], tok.at[place_ref[j]], sems.at[j]).start()
        high, low = split_two(low_ref[...])
        low_two[:, :BS] = high
        low_two[:, BS:] = low
        wide[(KB + 1) * BS :, BS:] = jnp.zeros((BS, BS), jnp.bfloat16)
        back_ref[...] = jnp.zeros_like(back_ref)
        for j in range(NX * NZ):
            pltpu.make_async_copy(pieces[j], tok.at[place_ref[j]], sems.at[j]).wait()

    for k in range(KB):
        high, low = split_two(weight_ref[0, k])
        wide[k * BS : (k + 1) * BS, :BS] = high
        wide[k * BS : (k + 1) * BS, BS:] = low
    f_high, f_low = split_two(factor_ref[...])
    wide[KB * BS : (KB + 1) * BS, :BS] = f_high
    wide[KB * BS : (KB + 1) * BS, BS:] = f_low
    wide[(KB + 1) * BS :, :BS] = f_high

    panel = jnp.concatenate(
        [tok[:, rows_ref[c * KB + k]].reshape(tokens, BS) for k in range(KB)]
        + [low_two[...]],
        axis=1,
    )
    both = jnp.dot(panel, wide[...], preferred_element_type=jnp.float32)
    v = both[:, :BS] + both[:, BS:]
    root = 0.7978845608028654
    square = v * v
    t = jnp.tanh(root * v * (1.0 + 0.044715 * square))
    half = 0.5 * (1.0 + t)
    hidden_ref[...] = (v * half).astype(jnp.bfloat16)
    slope = half + 0.5 * root * v * (1.0 - t * t) * (1.0 + 3.0 * 0.044715 * square)
    grad = up_ref[...].astype(jnp.float32) * slope

    g_high, g_low = split_two(grad)
    g_two = jnp.concatenate([g_high, g_low], axis=1)
    f_two = jnp.concatenate(
        [
            jnp.concatenate([f_high, f_high], axis=1),
            jnp.concatenate([f_low, jnp.zeros_like(f_low)], axis=1),
        ],
        axis=0,
    )
    back = lax.dot_general(
        g_two, f_two, (((1,), (1,)), ((), ())), preferred_element_type=jnp.float32
    )
    back_ref[...] += back[:, :BS] + back[:, BS:]

    grad_t = grad.T
    t_high, t_low = split_two(grad_t)
    gt_two = jnp.concatenate([t_high, t_low], axis=0)
    product = jnp.dot(gt_two, panel, preferred_element_type=jnp.float32)
    product = product[:BS] + product[BS:]
    for k in range(KB):
        block = product[:, k * BS : (k + 1) * BS]
        level = level_of(block)
        part = where_ref[0, c * KB + k]
        slot = where_ref[1, c * KB + k]
        codes[part, pl.ds(pl.multiple_of(slot * BS, BS), BS)] = encode(block, level)
        levels[part, pl.ds(slot, 1)] = level
    outer = product[:, KB * BS : (KB + 1) * BS] + product[:, (KB + 1) * BS :]
    for h in range(2):
        block = outer[h * 64 : (h + 1) * 64]
        level = level_of(block)
        part = where_ref[2, c * 2 + h]
        slot = where_ref[3, c * 2 + h]
        start = pl.multiple_of(SLOT_ROWS + slot * 64, 64)
        codes[part, pl.ds(start, 64)] = encode(block, level)
        levels[part, pl.ds(CAP + slot, 1)] = level

    @pl.when(c == COLS - 1)
    def _():
        for part in range(2 * NY):
            codes[part, CODE_ROWS:] = levels[part].astype(jnp.int32).astype(jnp.int16)
        send = pltpu.make_async_copy(codes.at[pl.ds(0, NY)], send_ref, sems.at[0])
        keep = pltpu.make_async_copy(codes.at[pl.ds(NY, NY)], keep_ref, sems.at[1])
        send.start()
        keep.start()
        send.wait()
        keep.wait()


def blocks_of():
    spans = [(s * BS, BS, s) for s in range(CAP)]
    return spans + [(SLOT_ROWS + h * 64, 64, CAP + h) for h in range(FO_ROWS // 64)]


def pair_kernel(keep_ref, got_ref, out_ref):
    keep_levels = keep_ref[0, CODE_ROWS:].astype(jnp.int32).astype(jnp.float32)
    got_levels = got_ref[0, CODE_ROWS:].astype(jnp.int32).astype(jnp.float32)
    fresh = []
    for start, size, index in blocks_of():
        span = slice(start, start + size)
        total = decode(keep_ref[0, span], keep_levels[index : index + 1])
        total += decode(got_ref[0, span], got_levels[index : index + 1])
        level = level_of(total)
        out_ref[0, span] = encode(total, level)
        fresh.append(level)
    fresh.append(jnp.zeros((32 - len(fresh), BS), jnp.float32))
    fresh = jnp.concatenate(fresh, axis=0)
    out_ref[0, CODE_ROWS:] = fresh.astype(jnp.int32).astype(jnp.int16)


def final_kernel(count_ref, *refs):
    parts, (slots_ref, outer_ref) = refs[:NY], refs[NY:]
    levels = [p[CODE_ROWS:].astype(jnp.int32).astype(jnp.float32) for p in parts]
    count = count_ref[0]
    for start, size, index in blocks_of():
        span = slice(start, start + size)
        total = decode(parts[0][span], levels[0][index : index + 1])
        for i in range(1, NY):
            total += decode(parts[i][span], levels[i][index : index + 1])
        if index < CAP:
            slots_ref[index] = jnp.where(index < count, total.T, 0.0)
        else:
            h = index - CAP
            outer_ref[:, h * 64 : (h + 1) * 64] = total.T


def gather_tokens(own):
    z_up, z_down = shift("z", NZ, 1), shift("z", NZ, -1)
    x_up, x_down = shift("x", NX, 1), shift("x", NX, -1)
    across = shift("x", NX, 2)
    held = {(0, 0): own}
    held[0, 2] = across(own)
    for b in (0, 2):
        for a in (1, 2, 3):
            held[-a, b] = z_up(held[1 - a, b])
            held[a, b] = z_down(held[a - 1, b])
    held[4, 0] = z_up(held[-3, 0])
    held[4, 2] = z_down(held[3, 2])
    for a in (0, -1, 1, -2, 2, -3, 3, 4):
        for b, move in ((-1, x_up), (1, x_down)):
            if (a, b) in ((1, 1), (-1, -1)):
                held[a, b] = (z_down if a > 0 else z_up)(held[0, b])
            else:
                held[a, b] = move(held[a, 0])
    return held


def per_device(tokens, block_weights, block_rows, block_owners, factor_in, factor_out, upstream):
    own = jnp.transpose(tokens.reshape(ROWS, RB, BS), (1, 0, 2))
    held = gather_tokens(own)
    z, x = lax.axis_index("z"), lax.axis_index("x")
    y, core = lax.axis_index("y"), lax.axis_index("core")
    order = sorted(held)
    place = jnp.stack([((z + a) % NZ) * NX + (x + b) % NX for a, b in order]).astype(jnp.int32)
    pieces = [held[key] for key in order]

    plane = ("z", "x")
    span = NX * NZ
    per = RB // span
    own_cols = lax.all_to_all(own.reshape(span, per, ROWS, BS), plane, 0, 0)
    own_cols = own_cols.astype(jnp.float32)
    factor = factor_in.reshape(per, BS, BS)
    partial = jnp.einsum("sbtf,bfr->str", own_cols, factor, precision=highest)
    low_own = jnp.sum(lax.all_to_all(partial, plane, 0, 0), axis=0)
    low_act = lax.all_to_all(
        jnp.broadcast_to(low_own[None], (span, ROWS, BS)), plane, 0, 0
    ).reshape(span * ROWS, BS)

    owners = block_owners.reshape(-1)
    count_all = owners.shape[0]
    marks = (owners[:, None] == jnp.arange(GROUPS, dtype=jnp.int32)[None, :]).astype(jnp.int32)
    before = (
        jnp.arange(count_all, dtype=jnp.int32)[:, None]
        > jnp.arange(count_all, dtype=jnp.int32)[None, :]
    ) & (owners[:, None] == owners[None, :])
    rank = jnp.sum(before.astype(jnp.int32), axis=1)

    def part_of(owner):
        turn = (owner // NC - y) % NY
        return turn + jnp.where(owner % NC == core, NY, 0)

    halves = jnp.arange(2 * COLS, dtype=jnp.int32)
    per_owner = FO_ROWS // 64
    pad = count_all - 2 * COLS
    where = jnp.stack(
        [
            part_of(owners),
            rank,
            jnp.pad(part_of(halves // per_owner), (0, pad)),
            jnp.pad(halves % per_owner, (0, pad)),
        ]
    ).astype(jnp.int32)
    counts = jnp.sum(marks, axis=0)
    mine = jnp.sum(
        jnp.where(jnp.arange(GROUPS) == y * NC + core, counts, 0), dtype=jnp.int32
    ).reshape(1)

    total = span * ROWS
    anywhere = pl.BlockSpec(memory_space=pl.ANY)
    hidden, send, keep, back = pl.pallas_call(
        main_kernel,
        grid_spec=pltpu.PrefetchScalarGridSpec(
            num_scalar_prefetch=3,
            grid=(COLS,),
            in_specs=[
                pl.BlockSpec((total, BS), lambda c, *_: (0, 0)),
                pl.BlockSpec((1, KB, BS, BS), lambda c, *_: (c, 0, 0, 0)),
                pl.BlockSpec((BS, BS), lambda c, *_: (0, c)),
                pl.BlockSpec((total, BS), lambda c, *_: (0, c)),
            ]
            + [anywhere] * span,
            out_specs=[
                pl.BlockSpec((total, BS), lambda c, *_: (0, c)),
                anywhere,
                anywhere,
                pl.BlockSpec((total, BS), lambda c, *_: (0, 0)),
            ],
            scratch_shapes=[
                pltpu.VMEM((span, RB, ROWS, BS), jnp.bfloat16),
                pltpu.VMEM(((KB + 2) * BS, 2 * BS), jnp.bfloat16),
                pltpu.VMEM((total, 2 * BS), jnp.bfloat16),
                pltpu.VMEM((2 * NY, PART_ROWS, BS), jnp.int16),
                pltpu.VMEM((2 * NY, 32, BS), jnp.float32),
                pltpu.SemaphoreType.DMA((span,)),
            ],
        ),
        out_shape=[
            jax.ShapeDtypeStruct((total, COLS * BS), jnp.bfloat16),
            jax.ShapeDtypeStruct((NY, PART_ROWS, BS), jnp.int16),
            jax.ShapeDtypeStruct((NY, PART_ROWS, BS), jnp.int16),
            jax.ShapeDtypeStruct((total, BS), jnp.float32),
        ],
        compiler_params=pltpu.CompilerParams(vmem_limit_bytes=50 * 1024 * 1024),
        name="columns",
    )(
        block_rows.reshape(-1), where, place,
        low_act, block_weights, factor_out, upstream, *pieces,
    )

    got = shift("core", NC, 1)(send)
    paired = pl.pallas_call(
        pair_kernel,
        grid=(NY,),
        in_specs=[pl.BlockSpec((1, PART_ROWS, BS), lambda i: (i, 0, 0))] * 2,
        out_specs=pl.BlockSpec((1, PART_ROWS, BS), lambda i: (i, 0, 0)),
        out_shape=jax.ShapeDtypeStruct((NY, PART_ROWS, BS), jnp.int16),
        compiler_params=pltpu.CompilerParams(vmem_limit_bytes=50 * 1024 * 1024),
        name="pairs",
    )(keep, got)
    parts = [
        paired[0],
        shift("y", NY, 1)(paired[1]),
        shift("y", NY, 2)(paired[2]),
        shift("y", NY, 3)(paired[3]),
    ]

    back_own = jnp.sum(lax.all_to_all(back.reshape(span, ROWS, BS), plane, 0, 0), axis=0)
    back_all = lax.all_to_all(
        jnp.broadcast_to(back_own[None], (span, ROWS, BS)), plane, 0, 0
    )
    in_part = jnp.einsum("sbtf,str->bfr", own_cols, back_all, precision=highest)
    in_part = in_part.reshape(GROUPS, per * BS // GROUPS, BS)
    in_grad = jnp.sum(lax.all_to_all(in_part, ("y", "core"), 0, 0), axis=0)

    whole = pl.BlockSpec(memory_space=pltpu.VMEM)
    slots, out_grad = pl.pallas_call(
        final_kernel,
        in_specs=[pl.BlockSpec(memory_space=pltpu.SMEM)] + [whole] * NY,
        out_specs=[whole, whole],
        out_shape=[
            jax.ShapeDtypeStruct((CAP, BS, BS), jnp.float32),
            jax.ShapeDtypeStruct((BS, FO_ROWS), jnp.float32),
        ],
        compiler_params=pltpu.CompilerParams(vmem_limit_bytes=50 * 1024 * 1024),
        name="slots",
    )(mine, *parts)
    return hidden, slots, in_grad, out_grad


def solution(mesh):
    split = Mesh(mesh.devices.reshape(NY, NC, NZ, NX), ("y", "core", "z", "x"))
    dp, mp = ("y", "core"), ("z", "x")
    return jax.shard_map(
        per_device,
        mesh=split,
        in_specs=(
            P(dp + mp, None),
            P(mp, None, None, None),
            P(mp, None),
            P(mp, None, None),
            P(mp, None),
            P(None, mp),
            P(dp, mp),
        ),
        out_specs=(
            P(dp, mp),
            P(mp + dp, None, None),
            P(mp + dp, None),
            P(None, mp + dp),
        ),
        check_vma=False,
    )
```

```python
import functools

import jax
import jax.numpy as jnp
from jax import lax
from jax.experimental import pallas as pl
from jax.experimental.pallas import tpu as pltpu
from jax.sharding import Mesh
from jax.sharding import PartitionSpec as P

highest = lax.Precision.HIGHEST
BS = 128
ROWS = 16
NX, NZ, NY, NC = 4, 8, 4, 2
COLS = 12
KB = 8
RB = 96
CAP = 18
GROUPS = NY * NC
SLOT_ROWS = CAP * BS
FO_ROWS = COLS * BS // GROUPS
CODE_ROWS = SLOT_ROWS + FO_ROWS
PART_ROWS = CODE_ROWS + 32
FINE = 256.0


def shift(axis, size, step):
    pairs = [(i, (i + step) % size) for i in range(size)]
    return lambda value: lax.ppermute(value, axis, pairs)


def flip(axis, size, bit):
    pairs = [(i, i ^ bit) for i in range(size)]
    return lambda value: lax.ppermute(value, axis, pairs)


def split_two(value):
    high = value.astype(jnp.bfloat16)
    low = (value - high.astype(jnp.float32)).astype(jnp.bfloat16)
    return high, low


def level_of(block):
    top = jnp.max(jnp.abs(block), axis=0, keepdims=True)
    return jnp.ceil(jnp.log2(jnp.maximum(top, 1e-30)) * FINE)


def encode(block, level):
    inverse = jnp.exp2(level * (-1.0 / FINE)) * 32700.0
    return jnp.floor(block * inverse + 0.5).astype(jnp.int32).astype(jnp.int16)


def decode(code, level):
    unit = jnp.exp2(level * (1.0 / FINE)) * (1.0 / 32700.0)
    return code.astype(jnp.int32).astype(jnp.float32) * unit


def main_kernel(
    rows_ref, where_ref, place_ref, low_ref, weight_ref, factor_ref, up_ref, *rest
):
    pieces = rest[: NX * NZ]
    hidden_ref, send_ref, keep_ref, back_ref, cols_ref = rest[NX * NZ : NX * NZ + 5]
    tok, wide, low_two, codes, levels, sems = rest[NX * NZ + 5 :]
    c = pl.program_id(0)
    tokens = NX * NZ * ROWS

    @pl.when(c == 0)
    def _():
        for j in range(NX * NZ):
            pltpu.make_async_copy(pieces[j], tok.at[place_ref[j]], sems.at[j]).start()
        for g in range(NZ):
            high, low = split_two(low_ref[place_ref[NX * NZ + g]])
            low_two[g * NX * ROWS : (g + 1) * NX * ROWS, :BS] = high
            low_two[g * NX * ROWS : (g + 1) * NX * ROWS, BS:] = low
        wide[(KB + 1) * BS :, BS:] = jnp.zeros((BS, BS), jnp.bfloat16)
        back_ref[...] = jnp.zeros_like(back_ref)
        for j in range(NX * NZ):
            pltpu.make_async_copy(pieces[j], tok.at[place_ref[j]], sems.at[j]).wait()
        for j in range(cols_ref.shape[0]):
            first = place_ref[NX * NZ + NZ]
            cols_ref[j] = tok[:, first + j].reshape(tokens, BS)

    for k in range(KB):
        high, low = split_two(weight_ref[0, k])
        wide[k * BS : (k + 1) * BS, :BS] = high
        wide[k * BS : (k + 1) * BS, BS:] = low
    f_high, f_low = split_two(factor_ref[...])
    wide[KB * BS : (KB + 1) * BS, :BS] = f_high
    wide[KB * BS : (KB + 1) * BS, BS:] = f_low
    wide[(KB + 1) * BS :, :BS] = f_high

    panel = jnp.concatenate(
        [tok[:, rows_ref[c * KB + k]].reshape(tokens, BS) for k in range(KB)]
        + [low_two[...]],
        axis=1,
    )
    both = jnp.dot(panel, wide[...], preferred_element_type=jnp.float32)
    v = both[:, :BS] + both[:, BS:]
    root = 0.7978845608028654
    square = v * v
    t = jnp.tanh(root * v * (1.0 + 0.044715 * square))
    half = 0.5 * (1.0 + t)
    hidden_ref[...] = (v * half).astype(jnp.bfloat16)
    slope = half + 0.5 * root * v * (1.0 - t * t) * (1.0 + 3.0 * 0.044715 * square)
    grad = up_ref[...].astype(jnp.float32) * slope

    g_high, g_low = split_two(grad)
    g_two = jnp.concatenate([g_high, g_low], axis=1)
    f_two = jnp.concatenate(
        [
            jnp.concatenate([f_high, f_high], axis=1),
            jnp.concatenate([f_low, jnp.zeros_like(f_low)], axis=1),
        ],
        axis=0,
    )
    back = lax.dot_general(
        g_two, f_two, (((1,), (1,)), ((), ())), preferred_element_type=jnp.float32
    )
    back_ref[...] += back[:, :BS] + back[:, BS:]

    grad_t = grad.T
    t_high, t_low = split_two(grad_t)
    gt_two = jnp.concatenate([t_high, t_low], axis=0)
    product = jnp.dot(gt_two, panel, preferred_element_type=jnp.float32)
    product = product[:BS] + product[BS:]
    for k in range(KB):
        block = product[:, k * BS : (k + 1) * BS]
        level = level_of(block)
        part = where_ref[0, c * KB + k]
        slot = where_ref[1, c * KB + k]
        codes[part, pl.ds(pl.multiple_of(slot * BS, BS), BS)] = encode(block, level)
        levels[part, pl.ds(slot, 1)] = level
    outer = product[:, KB * BS : (KB + 1) * BS] + product[:, (KB + 1) * BS :]
    for h in range(2):
        block = outer[h * 64 : (h + 1) * 64]
        level = level_of(block)
        part = where_ref[2, c * 2 + h]
        slot = where_ref[3, c * 2 + h]
        start = pl.multiple_of(SLOT_ROWS + slot * 64, 64)
        codes[part, pl.ds(start, 64)] = encode(block, level)
        levels[part, pl.ds(CAP + slot, 1)] = level

    @pl.when(c == COLS - 1)
    def _():
        for part in range(2 * NY):
            codes[part, CODE_ROWS:] = levels[part].astype(jnp.int32).astype(jnp.int16)
        send = pltpu.make_async_copy(codes.at[pl.ds(0, NY)], send_ref, sems.at[0])
        keep = pltpu.make_async_copy(codes.at[pl.ds(NY, NY)], keep_ref, sems.at[1])
        send.start()
        keep.start()
        send.wait()
        keep.wait()


def blocks_of():
    spans = [(s * BS, BS, s) for s in range(CAP)]
    return spans + [(SLOT_ROWS + h * 64, 64, CAP + h) for h in range(FO_ROWS // 64)]


def pair_kernel(keep_ref, got_ref, out_ref):
    keep_levels = keep_ref[0, CODE_ROWS:].astype(jnp.int32).astype(jnp.float32)
    got_levels = got_ref[0, CODE_ROWS:].astype(jnp.int32).astype(jnp.float32)
    fresh = []
    for start, size, index in blocks_of():
        span = slice(start, start + size)
        total = decode(keep_ref[0, span], keep_levels[index : index + 1])
        total += decode(got_ref[0, span], got_levels[index : index + 1])
        level = level_of(total)
        out_ref[0, span] = encode(total, level)
        fresh.append(level)
    fresh.append(jnp.zeros((32 - len(fresh), BS), jnp.float32))
    fresh = jnp.concatenate(fresh, axis=0)
    out_ref[0, CODE_ROWS:] = fresh.astype(jnp.int32).astype(jnp.int16)


def final_kernel(count_ref, *refs):
    parts, (slots_ref, outer_ref) = refs[:NY], refs[NY:]
    levels = [p[CODE_ROWS:].astype(jnp.int32).astype(jnp.float32) for p in parts]
    count = count_ref[0]
    for start, size, index in blocks_of():
        span = slice(start, start + size)
        total = decode(parts[0][span], levels[0][index : index + 1])
        for i in range(1, NY):
            total += decode(parts[i][span], levels[i][index : index + 1])
        if index < CAP:
            slots_ref[index] = jnp.where(index < count, total.T, 0.0)
        else:
            h = index - CAP
            outer_ref[:, h * 64 : (h + 1) * 64] = total.T


def low_kernel(near_ref, factor_ref, *rest):
    pieces, (out_ref, tok, sems) = rest[:NX], rest[NX:]
    per = RB // (NX * NZ)
    copies = []
    for j in range(NX):
        source = pieces[j].at[:, pl.ds(near_ref[0] * per, per)]
        copies.append(pltpu.make_async_copy(source, tok.at[near_ref[j]], sems.at[j]))
        copies[j].start()
    high, low = split_two(factor_ref[...])
    wide = jnp.concatenate([high, low], axis=1)
    for copy in copies:
        copy.wait()
    panel = jnp.concatenate(
        [tok[:, g, j].reshape(NX * ROWS, BS) for g in range(NZ) for j in range(per)], axis=1
    )
    both = jnp.dot(panel, wide, preferred_element_type=jnp.float32)
    out_ref[...] = both[:, :BS] + both[:, BS:]


def low_partial(near, factor, pieces):
    per = RB // (NX * NZ)
    pieces = [p.reshape(NZ, NX * per, ROWS, BS) for p in pieces]
    return pl.pallas_call(
        low_kernel,
        in_specs=[
            pl.BlockSpec(memory_space=pltpu.SMEM),
            pl.BlockSpec(memory_space=pltpu.VMEM),
        ]
        + [pl.BlockSpec(memory_space=pl.ANY)] * NX,
        out_specs=pl.BlockSpec(memory_space=pltpu.VMEM),
        out_shape=jax.ShapeDtypeStruct((NX * ROWS, BS), jnp.float32),
        scratch_shapes=[
            pltpu.VMEM((NX, NZ, per, ROWS, BS), jnp.bfloat16),
            pltpu.SemaphoreType.DMA((NX,)),
        ],
        compiler_params=pltpu.CompilerParams(vmem_limit_bytes=30 * 1024 * 1024),
        name="low",
    )(near, factor, *pieces)


def in_kernel(near_ref, turns_ref, cols_ref, *rest):
    backs, (out_ref, full) = rest[:NX], rest[NX:]
    for j in range(NX):
        for g in range(NZ):
            full[g, near_ref[j]] = backs[j][g]
    total = NZ * NX * ROWS
    high, low = split_two(full[...].reshape(total, BS).T)
    two = jnp.concatenate([high, low], axis=0)
    panel = jnp.concatenate([cols_ref[j] for j in range(cols_ref.shape[0])], axis=1)
    both = jnp.dot(two, panel, preferred_element_type=jnp.float32)
    grad = (both[:BS] + both[BS:]).T
    size = grad.shape[0] // GROUPS
    for d in range(GROUPS):
        out_ref[turns_ref[d]] = grad[d * size : (d + 1) * size]


def in_partial(near, turns, cols, backs):
    small = pl.BlockSpec(memory_space=pltpu.SMEM)
    whole = pl.BlockSpec(memory_space=pltpu.VMEM)
    size = cols.shape[0] * BS // GROUPS
    return pl.pallas_call(
        in_kernel,
        in_specs=[small, small, whole] + [whole] * NX,
        out_specs=whole,
        out_shape=jax.ShapeDtypeStruct((GROUPS, size, BS), jnp.float32),
        scratch_shapes=[pltpu.VMEM((NZ, NX, ROWS, BS), jnp.float32)],
        compiler_params=pltpu.CompilerParams(vmem_limit_bytes=30 * 1024 * 1024),
        name="into",
    )(near, turns, cols, *backs)


def gather_tokens(own):
    z_up, z_down = shift("z", NZ, 1), shift("z", NZ, -1)
    x_up, x_down = shift("x", NX, 1), shift("x", NX, -1)
    across = shift("x", NX, 2)
    held = {(0, 0): own}
    held[0, 2] = across(own)
    for b in (0, 2):
        for a in (1, 2, 3):
            held[-a, b] = z_up(held[1 - a, b])
            held[a, b] = z_down(held[a - 1, b])
    held[4, 0] = z_up(held[-3, 0])
    held[4, 2] = z_down(held[3, 2])
    for a in (0, -1, 1, -2, 2, -3, 3, 4):
        for b, move in ((-1, x_up), (1, x_down)):
            if (a, b) in ((1, 1), (-1, -1)):
                held[a, b] = (z_down if a > 0 else z_up)(held[0, b])
            else:
                held[a, b] = move(held[a, 0])
    return held


def per_device(tokens, block_weights, block_rows, block_owners, factor_in, factor_out, upstream):
    own = jnp.transpose(tokens.reshape(ROWS, RB, BS), (1, 0, 2))
    held = gather_tokens(own)
    z, x = lax.axis_index("z"), lax.axis_index("x")
    y, core = lax.axis_index("y"), lax.axis_index("core")
    order = sorted(held)
    place = [((z + a) % NZ) * NX + (x + b) % NX for a, b in order]
    place += [z ^ g for g in range(NZ)] + [(z * NX + x) * (RB // (NX * NZ))]
    place = jnp.stack(place).astype(jnp.int32)
    pieces = [held[key] for key in order]

    span = NX * NZ
    per = RB // span
    turn_x = lambda step: jnp.asarray((x + step) % NX, jnp.int32)
    x_up, x_down, across = shift("x", NX, 1), shift("x", NX, -1), shift("x", NX, 2)
    factor = lax.all_gather(factor_in, "z", axis=0, tiled=True)
    near = jnp.stack([turn_x(b) for b in (0, -1, 1, 2)])
    low_part = low_partial(near, factor, [held[0, b] for b in (0, -1, 1, 2)])
    low = (low_part + across(low_part)) + (x_up(low_part) + x_down(low_part))
    low = low[None]
    for bit in (1, 2, 4):
        low = jnp.concatenate([low, flip("z", NZ, bit)(low)], axis=0)

    owners = block_owners.reshape(-1)
    count_all = owners.shape[0]
    marks = (owners[:, None] == jnp.arange(GROUPS, dtype=jnp.int32)[None, :]).astype(jnp.int32)
    before = (
        jnp.arange(count_all, dtype=jnp.int32)[:, None]
        > jnp.arange(count_all, dtype=jnp.int32)[None, :]
    ) & (owners[:, None] == owners[None, :])
    rank = jnp.sum(before.astype(jnp.int32), axis=1)

    def part_of(owner):
        turn = (owner // NC - y) % NY
        return turn + jnp.where(owner % NC == core, NY, 0)

    halves = jnp.arange(2 * COLS, dtype=jnp.int32)
    per_owner = FO_ROWS // 64
    pad = count_all - 2 * COLS
    where = jnp.stack(
        [
            part_of(owners),
            rank,
            jnp.pad(part_of(halves // per_owner), (0, pad)),
            jnp.pad(halves % per_owner, (0, pad)),
        ]
    ).astype(jnp.int32)
    counts = jnp.sum(marks, axis=0)
    mine = jnp.sum(
        jnp.where(jnp.arange(GROUPS) == y * NC + core, counts, 0), dtype=jnp.int32
    ).reshape(1)

    total = span * ROWS
    anywhere = pl.BlockSpec(memory_space=pl.ANY)
    hidden, send, keep, back, cols = pl.pallas_call(
        main_kernel,
        grid_spec=pltpu.PrefetchScalarGridSpec(
            num_scalar_prefetch=3,
            grid=(COLS,),
            in_specs=[
                pl.BlockSpec((NZ, NX * ROWS, BS), lambda c, *_: (0, 0, 0)),
                pl.BlockSpec((1, KB, BS, BS), lambda c, *_: (c, 0, 0, 0)),
                pl.BlockSpec((BS, BS), lambda c, *_: (0, c)),
                pl.BlockSpec((total, BS), lambda c, *_: (0, c)),
            ]
            + [anywhere] * span,
            out_specs=[
                pl.BlockSpec((total, BS), lambda c, *_: (0, c)),
                anywhere,
                anywhere,
                pl.BlockSpec((total, BS), lambda c, *_: (0, 0)),
                pl.BlockSpec((per, total, BS), lambda c, *_: (0, 0, 0)),
            ],
            scratch_shapes=[
                pltpu.VMEM((span, RB, ROWS, BS), jnp.bfloat16),
                pltpu.VMEM(((KB + 2) * BS, 2 * BS), jnp.bfloat16),
                pltpu.VMEM((total, 2 * BS), jnp.bfloat16),
                pltpu.VMEM((2 * NY, PART_ROWS, BS), jnp.int16),
                pltpu.VMEM((2 * NY, 32, BS), jnp.float32),
                pltpu.SemaphoreType.DMA((span,)),
            ],
        ),
        out_shape=[
            jax.ShapeDtypeStruct((total, COLS * BS), jnp.bfloat16),
            jax.ShapeDtypeStruct((NY, PART_ROWS, BS), jnp.int16),
            jax.ShapeDtypeStruct((NY, PART_ROWS, BS), jnp.int16),
            jax.ShapeDtypeStruct((total, BS), jnp.float32),
            jax.ShapeDtypeStruct((per, total, BS), jnp.bfloat16),
        ],
        compiler_params=pltpu.CompilerParams(vmem_limit_bytes=50 * 1024 * 1024),
        name="columns",
    )(
        block_rows.reshape(-1), where, place,
        low, block_weights, factor_out, upstream, *pieces,
    )

    got = shift("core", NC, 1)(send)
    paired = pl.pallas_call(
        pair_kernel,
        grid=(NY,),
        in_specs=[pl.BlockSpec((1, PART_ROWS, BS), lambda i: (i, 0, 0))] * 2,
        out_specs=pl.BlockSpec((1, PART_ROWS, BS), lambda i: (i, 0, 0)),
        out_shape=jax.ShapeDtypeStruct((NY, PART_ROWS, BS), jnp.int16),
        compiler_params=pltpu.CompilerParams(vmem_limit_bytes=50 * 1024 * 1024),
        name="pairs",
    )(keep, got)
    parts = [
        paired[0],
        shift("y", NY, 1)(paired[1]),
        shift("y", NY, 2)(paired[2]),
        shift("y", NY, 3)(paired[3]),
    ]

    back = back.reshape(NZ, NX, ROWS, BS)
    pick = lambda step: lax.dynamic_index_in_dim(back, turn_x(step), 1, keepdims=False)
    back_x = (pick(0) + across(pick(2))) + (x_up(pick(1)) + x_down(pick(-1)))
    for bit in (1, 2, 4):
        back_x = back_x + flip("z", NZ, bit)(back_x)
    backs = [back_x, x_up(back_x), x_down(back_x), across(back_x)]
    turns = jnp.stack([part_of(jnp.int32(d)) for d in range(GROUPS)]).astype(jnp.int32)
    in_part = in_partial(near, turns, cols, backs)
    in_sum = in_part[NY:] + shift("core", NC, 1)(in_part[:NY])
    in_grad = in_sum[0]
    for step in (1, 2, 3):
        in_grad = in_grad + shift("y", NY, step)(in_sum[step])

    whole = pl.BlockSpec(memory_space=pltpu.VMEM)
    slots, out_grad = pl.pallas_call(
        final_kernel,
        in_specs=[pl.BlockSpec(memory_space=pltpu.SMEM)] + [whole] * NY,
        out_specs=[whole, whole],
        out_shape=[
            jax.ShapeDtypeStruct((CAP, BS, BS), jnp.float32),
            jax.ShapeDtypeStruct((BS, FO_ROWS), jnp.float32),
        ],
        compiler_params=pltpu.CompilerParams(vmem_limit_bytes=50 * 1024 * 1024),
        name="slots",
    )(mine, *parts)
    return hidden, slots, in_grad, out_grad


def solution(mesh):
    split = Mesh(mesh.devices.reshape(NY, NC, NZ, NX), ("y", "core", "z", "x"))
    dp, mp = ("y", "core"), ("z", "x")
    return jax.shard_map(
        per_device,
        mesh=split,
        in_specs=(
            P(dp + mp, None),
            P(mp, None, None, None),
            P(mp, None),
            P(mp, None, None),
            P(mp, None),
            P(None, mp),
            P(dp, mp),
        ),
        out_specs=(
            P(dp, mp),
            P(mp + dp, None, None),
            P(mp + dp, None),
            P(None, mp + dp),
        ),
        check_vma=False,
    )
```

```python
import functools

import jax
import jax.numpy as jnp
from jax import lax
from jax.experimental import pallas as pl
from jax.experimental.pallas import tpu as pltpu
from jax.sharding import Mesh
from jax.sharding import PartitionSpec as P

highest = lax.Precision.HIGHEST
BS = 128
ROWS = 16
NX, NZ, NY, NC = 4, 8, 4, 2
COLS = 12
PER_STEP = 2
KB = 8
RB = 96
CAP = 18
GROUPS = NY * NC
SLOT_ROWS = CAP * BS
FO_ROWS = COLS * BS // GROUPS
CODE_ROWS = SLOT_ROWS + FO_ROWS
PART_ROWS = CODE_ROWS + 32
FINE = 256.0
CUT = 10 * BS


def shift(axis, size, step):
    pairs = [(i, (i + step) % size) for i in range(size)]
    return lambda value: lax.ppermute(value, axis, pairs)


def flip(axis, size, bit):
    pairs = [(i, i ^ bit) for i in range(size)]
    return lambda value: lax.ppermute(value, axis, pairs)


def split_two(value):
    high = value.astype(jnp.bfloat16)
    low = (value - high.astype(jnp.float32)).astype(jnp.bfloat16)
    return high, low


def level_of(block):
    top = jnp.max(jnp.abs(block), axis=0, keepdims=True)
    return jnp.ceil(jnp.log2(jnp.maximum(top, 1e-30)) * FINE)


def encode(block, level):
    inverse = jnp.exp2(level * (-1.0 / FINE)) * 32700.0
    return jnp.floor(block * inverse + 0.5).astype(jnp.int32).astype(jnp.int16)


def decode(code, level):
    unit = jnp.exp2(level * (1.0 / FINE)) * (1.0 / 32700.0)
    return code.astype(jnp.int32).astype(jnp.float32) * unit


def main_kernel(
    counts, rows_ref, where_ref, place_ref, low_ref, weight_ref, factor_ref, up_ref, *rest
):
    arrays, rest = rest[: len(counts)], rest[len(counts) :]
    pieces = [ref.at[i] for ref, n in zip(arrays, counts) for i in range(n)]
    hidden_ref, send_ref, keep_ref, back_ref, cols_ref = rest[:5]
    tok, wide, low_two, codes, levels, sems = rest[5:]
    c = pl.program_id(0)
    tokens = NX * NZ * ROWS

    @pl.when(c == 0)
    def _():
        for j in range(NX * NZ):
            pltpu.make_async_copy(pieces[j], tok.at[place_ref[j]], sems.at[j]).start()
        for g in range(NZ):
            high, low = split_two(low_ref[place_ref[NX * NZ + g]])
            low_two[g * NX * ROWS : (g + 1) * NX * ROWS, :BS] = high
            low_two[g * NX * ROWS : (g + 1) * NX * ROWS, BS:] = low
        wide[(KB + 1) * BS :, BS:] = jnp.zeros((BS, BS), jnp.bfloat16)
        back_ref[...] = jnp.zeros_like(back_ref)
        for j in range(NX * NZ):
            pltpu.make_async_copy(pieces[j], tok.at[place_ref[j]], sems.at[j]).wait()
        for j in range(cols_ref.shape[0]):
            first = place_ref[NX * NZ + NZ]
            cols_ref[j] = tok[:, first + j].reshape(tokens, BS)

    for i in range(PER_STEP):
        col = c * PER_STEP + i
        here = slice(i * BS, (i + 1) * BS)
        for k in range(KB):
            high, low = split_two(weight_ref[i, k])
            wide[k * BS : (k + 1) * BS, :BS] = high
            wide[k * BS : (k + 1) * BS, BS:] = low
        f_high, f_low = split_two(factor_ref[:, here])
        wide[KB * BS : (KB + 1) * BS, :BS] = f_high
        wide[KB * BS : (KB + 1) * BS, BS:] = f_low
        wide[(KB + 1) * BS :, :BS] = f_high

        panel = jnp.concatenate(
            [tok[:, rows_ref[col * KB + k]].reshape(tokens, BS) for k in range(KB)]
            + [low_two[...]],
            axis=1,
        )
        both = jnp.dot(panel, wide[...], preferred_element_type=jnp.float32)
        v = both[:, :BS] + both[:, BS:]
        root = 0.7978845608028654
        square = v * v
        t = jnp.tanh(root * v * (1.0 + 0.044715 * square))
        half = 0.5 * (1.0 + t)
        hidden_ref[:, here] = (v * half).astype(jnp.bfloat16)
        slope = half + 0.5 * root * v * (1.0 - t * t) * (1.0 + 3.0 * 0.044715 * square)
        grad = up_ref[:, here].astype(jnp.float32) * slope

        g_high, g_low = split_two(grad)
        g_two = jnp.concatenate([g_high, g_low], axis=1)
        f_two = jnp.concatenate(
            [
                jnp.concatenate([f_high, f_high], axis=1),
                jnp.concatenate([f_low, jnp.zeros_like(f_low)], axis=1),
            ],
            axis=0,
        )
        back = lax.dot_general(
            g_two, f_two, (((1,), (1,)), ((), ())), preferred_element_type=jnp.float32
        )
        back_ref[...] += back[:, :BS] + back[:, BS:]

        grad_t = grad.T
        t_high, t_low = split_two(grad_t)
        gt_two = jnp.concatenate([t_high, t_low], axis=0)
        product = jnp.dot(gt_two, panel, preferred_element_type=jnp.float32)
        product = product[:BS] + product[BS:]
        for k in range(KB):
            block = product[:, k * BS : (k + 1) * BS]
            level = level_of(block)
            part = where_ref[0, col * KB + k]
            slot = where_ref[1, col * KB + k]
            codes[part, pl.ds(pl.multiple_of(slot * BS, BS), BS)] = encode(block, level)
            levels[part, pl.ds(slot, 1)] = level
        outer = product[:, KB * BS : (KB + 1) * BS] + product[:, (KB + 1) * BS :]
        for h in range(2):
            block = outer[h * 64 : (h + 1) * 64]
            level = level_of(block)
            part = where_ref[2, col * 2 + h]
            slot = where_ref[3, col * 2 + h]
            start = pl.multiple_of(SLOT_ROWS + slot * 64, 64)
            codes[part, pl.ds(start, 64)] = encode(block, level)
            levels[part, pl.ds(CAP + slot, 1)] = level

    @pl.when(c == COLS // PER_STEP - 1)
    def _():
        for part in range(2 * NY):
            codes[part, CODE_ROWS:] = levels[part].astype(jnp.int32).astype(jnp.int16)
        send = pltpu.make_async_copy(codes.at[pl.ds(0, NY)], send_ref, sems.at[0])
        keep = pltpu.make_async_copy(codes.at[pl.ds(NY, NY)], keep_ref, sems.at[1])
        send.start()
        keep.start()
        send.wait()
        keep.wait()


def blocks_of():
    spans = [(s * BS, BS, s) for s in range(CAP)]
    return spans + [(SLOT_ROWS + h * 64, 64, CAP + h) for h in range(FO_ROWS // 64)]


def pair_kernel(keep_ref, got_ref, out_ref):
    keep_levels = keep_ref[0, CODE_ROWS:].astype(jnp.int32).astype(jnp.float32)
    got_levels = got_ref[0, CODE_ROWS:].astype(jnp.int32).astype(jnp.float32)
    fresh = []
    for start, size, index in blocks_of():
        span = slice(start, start + size)
        total = decode(keep_ref[0, span], keep_levels[index : index + 1])
        total += decode(got_ref[0, span], got_levels[index : index + 1])
        level = level_of(total)
        out_ref[0, span] = encode(total, level)
        fresh.append(level)
    fresh.append(jnp.zeros((32 - len(fresh), BS), jnp.float32))
    fresh = jnp.concatenate(fresh, axis=0)
    out_ref[0, CODE_ROWS:] = fresh.astype(jnp.int32).astype(jnp.int16)


def final_kernel(count_ref, own_ref, *refs):
    firsts, seconds = refs[: NY - 1], refs[NY - 1 : 2 * NY - 2]
    slots_ref, outer_ref = refs[2 * NY - 2 :]
    tails = [own_ref[0, CODE_ROWS:]] + [r[CODE_ROWS - CUT :] for r in seconds]
    levels = [t.astype(jnp.int32).astype(jnp.float32) for t in tails]
    count = count_ref[0]
    for start, size, index in blocks_of():
        total = decode(own_ref[0, start : start + size], levels[0][index : index + 1])
        for i in range(NY - 1):
            if start < CUT:
                code = firsts[i][start : start + size]
            else:
                code = seconds[i][start - CUT : start - CUT + size]
            total += decode(code, levels[i + 1][index : index + 1])
        if index < CAP:
            slots_ref[index] = jnp.where(index < count, total.T, 0.0)
        else:
            h = index - CAP
            outer_ref[:, h * 64 : (h + 1) * 64] = total.T


def low_kernel(near_ref, factor_ref, *rest):
    pieces, (out_ref, tok, sems) = rest[:NX], rest[NX:]
    per = RB // (NX * NZ)
    copies = []
    for j in range(NX):
        source = pieces[j].at[:, pl.ds(near_ref[0] * per, per)]
        copies.append(pltpu.make_async_copy(source, tok.at[near_ref[j]], sems.at[j]))
        copies[j].start()
    high, low = split_two(factor_ref[...])
    wide = jnp.concatenate([high, low], axis=1)
    for copy in copies:
        copy.wait()
    panel = jnp.concatenate(
        [tok[:, g, j].reshape(NX * ROWS, BS) for g in range(NZ) for j in range(per)], axis=1
    )
    both = jnp.dot(panel, wide, preferred_element_type=jnp.float32)
    out_ref[...] = both[:, :BS] + both[:, BS:]


def low_partial(near, factor, pieces):
    per = RB // (NX * NZ)
    pieces = [p.reshape(NZ, NX * per, ROWS, BS) for p in pieces]
    return pl.pallas_call(
        low_kernel,
        in_specs=[
            pl.BlockSpec(memory_space=pltpu.SMEM),
            pl.BlockSpec(memory_space=pltpu.VMEM),
        ]
        + [pl.BlockSpec(memory_space=pl.ANY)] * NX,
        out_specs=pl.BlockSpec(memory_space=pltpu.VMEM),
        out_shape=jax.ShapeDtypeStruct((NX * ROWS, BS), jnp.float32),
        scratch_shapes=[
            pltpu.VMEM((NX, NZ, per, ROWS, BS), jnp.bfloat16),
            pltpu.SemaphoreType.DMA((NX,)),
        ],
        compiler_params=pltpu.CompilerParams(vmem_limit_bytes=30 * 1024 * 1024),
        name="low",
    )(near, factor, *pieces)


def in_kernel(near_ref, turns_ref, cols_ref, *rest):
    backs, (out_ref, full) = rest[:NX], rest[NX:]
    for j in range(NX):
        for g in range(NZ):
            full[g, near_ref[j]] = backs[j][g]
    total = NZ * NX * ROWS
    high, low = split_two(full[...].reshape(total, BS).T)
    two = jnp.concatenate([high, low], axis=0)
    panel = jnp.concatenate([cols_ref[j] for j in range(cols_ref.shape[0])], axis=1)
    both = jnp.dot(two, panel, preferred_element_type=jnp.float32)
    grad = (both[:BS] + both[BS:]).T
    size = grad.shape[0] // GROUPS
    for d in range(GROUPS):
        out_ref[turns_ref[d]] = grad[d * size : (d + 1) * size]


def in_partial(near, turns, cols, backs):
    small = pl.BlockSpec(memory_space=pltpu.SMEM)
    whole = pl.BlockSpec(memory_space=pltpu.VMEM)
    size = cols.shape[0] * BS // GROUPS
    return pl.pallas_call(
        in_kernel,
        in_specs=[small, small, whole] + [whole] * NX,
        out_specs=whole,
        out_shape=jax.ShapeDtypeStruct((GROUPS, size, BS), jnp.float32),
        scratch_shapes=[pltpu.VMEM((NZ, NX, ROWS, BS), jnp.float32)],
        compiler_params=pltpu.CompilerParams(vmem_limit_bytes=30 * 1024 * 1024),
        name="into",
    )(near, turns, cols, *backs)


def gather_tokens(own):
    z_up, z_down = shift("z", NZ, 1), shift("z", NZ, -1)
    x_up, x_down, across = shift("x", NX, 1), shift("x", NX, -1), shift("x", NX, 2)
    far = across(own)
    ring = {0: own}
    sides = {-1: x_up(own), 1: x_down(own)}
    sent = {(0,): (sides[-1][None], sides[1][None])}

    def step(a):
        ring[-a] = z_up(ring[1 - a])
        ring[a] = z_down(ring[a - 1])

    def batch(*which):
        block = jnp.stack([ring[a] for a in which])
        sent[which] = (x_up(block), x_down(block))
        return sent[which]

    step(1)
    first_ring = [ring[1], ring[-1]]
    step(2)
    first = batch(1, -1)
    ring[2], ring[-2], _ = lax.optimization_barrier((ring[2], ring[-2], (far, sides)))
    far_all = lax.all_gather(far, "z", axis=0)
    step(3)
    second = batch(2, -2)
    ring[3], ring[-3], _ = lax.optimization_barrier((ring[3], ring[-3], first))
    ring[4] = z_up(ring[-3])
    ring[4], _ = lax.optimization_barrier((ring[4], second))
    batch(3, -3, 4)
    arrays, keys = [far_all], [[(None, g, 2) for g in range(NZ)]]
    for a in ring:
        arrays.append(ring[a][None])
        keys.append([(a, None, 0)])
    for which, pair in sent.items():
        for b, value in zip((-1, 1), pair):
            arrays.append(value)
            keys.append([(a, None, b) for a in which])
    return arrays, keys, first_ring, [own, sides[-1], sides[1], far]


def per_device(tokens, block_weights, block_rows, block_owners, factor_in, factor_out, upstream):
    own = jnp.transpose(tokens.reshape(ROWS, RB, BS), (1, 0, 2))
    arrays, keys, first_ring, near_pieces = gather_tokens(own)
    z, x = lax.axis_index("z"), lax.axis_index("x")
    y, core = lax.axis_index("y"), lax.axis_index("core")
    place = []
    for group in keys:
        for a, g, b in group:
            row = g if a is None else (z + a) % NZ
            place.append(row * NX + (x + b) % NX)
    place += [z ^ g for g in range(NZ)] + [(z * NX + x) * (RB // (NX * NZ))]
    place = jnp.stack([jnp.asarray(p, jnp.int32) for p in place])

    span = NX * NZ
    per = RB // span
    turn_x = lambda step: jnp.asarray((x + step) % NX, jnp.int32)
    x_up, x_down, across = shift("x", NX, 1), shift("x", NX, -1), shift("x", NX, 2)
    factor_late, _ = lax.optimization_barrier((factor_in, (near_pieces, first_ring)))
    factor = lax.all_gather(factor_late, "z", axis=0, tiled=True)
    near = jnp.stack([turn_x(b) for b in (0, -1, 1, 2)])
    low_part = low_partial(near, factor, near_pieces)
    low = (low_part + across(low_part)) + (x_up(low_part) + x_down(low_part))
    low = low[None]
    for bit in (1, 2, 4):
        low = jnp.concatenate([low, flip("z", NZ, bit)(low)], axis=0)

    owners = block_owners.reshape(-1)
    count_all = owners.shape[0]
    marks = (owners[:, None] == jnp.arange(GROUPS, dtype=jnp.int32)[None, :]).astype(jnp.int32)
    before = (
        jnp.arange(count_all, dtype=jnp.int32)[:, None]
        > jnp.arange(count_all, dtype=jnp.int32)[None, :]
    ) & (owners[:, None] == owners[None, :])
    rank = jnp.sum(before.astype(jnp.int32), axis=1)

    def part_of(owner):
        turn = (owner // NC - y) % NY
        return turn + jnp.where(owner % NC == core, NY, 0)

    halves = jnp.arange(2 * COLS, dtype=jnp.int32)
    per_owner = FO_ROWS // 64
    pad = count_all - 2 * COLS
    where = jnp.stack(
        [
            part_of(owners),
            rank,
            jnp.pad(part_of(halves // per_owner), (0, pad)),
            jnp.pad(halves % per_owner, (0, pad)),
        ]
    ).astype(jnp.int32)
    counts = jnp.sum(marks, axis=0)
    mine = jnp.sum(
        jnp.where(jnp.arange(GROUPS) == y * NC + core, counts, 0), dtype=jnp.int32
    ).reshape(1)

    total = span * ROWS
    anywhere = pl.BlockSpec(memory_space=pl.ANY)
    hidden, send, keep, back, cols = pl.pallas_call(
        functools.partial(main_kernel, [len(g) for g in keys]),
        grid_spec=pltpu.PrefetchScalarGridSpec(
            num_scalar_prefetch=3,
            grid=(COLS // PER_STEP,),
            in_specs=[
                pl.BlockSpec((NZ, NX * ROWS, BS), lambda c, *_: (0, 0, 0)),
                pl.BlockSpec((PER_STEP, KB, BS, BS), lambda c, *_: (c, 0, 0, 0)),
                pl.BlockSpec((BS, PER_STEP * BS), lambda c, *_: (0, c)),
                pl.BlockSpec((total, PER_STEP * BS), lambda c, *_: (0, c)),
            ]
            + [anywhere] * len(arrays),
            out_specs=[
                pl.BlockSpec((total, PER_STEP * BS), lambda c, *_: (0, c)),
                anywhere,
                anywhere,
                pl.BlockSpec((total, BS), lambda c, *_: (0, 0)),
                pl.BlockSpec((per, total, BS), lambda c, *_: (0, 0, 0)),
            ],
            scratch_shapes=[
                pltpu.VMEM((span, RB, ROWS, BS), jnp.bfloat16),
                pltpu.VMEM(((KB + 2) * BS, 2 * BS), jnp.bfloat16),
                pltpu.VMEM((total, 2 * BS), jnp.bfloat16),
                pltpu.VMEM((2 * NY, PART_ROWS, BS), jnp.int16),
                pltpu.VMEM((2 * NY, 32, BS), jnp.float32),
                pltpu.SemaphoreType.DMA((span,)),
            ],
        ),
        out_shape=[
            jax.ShapeDtypeStruct((total, COLS * BS), jnp.bfloat16),
            jax.ShapeDtypeStruct((NY, PART_ROWS, BS), jnp.int16),
            jax.ShapeDtypeStruct((NY, PART_ROWS, BS), jnp.int16),
            jax.ShapeDtypeStruct((total, BS), jnp.float32),
            jax.ShapeDtypeStruct((per, total, BS), jnp.bfloat16),
        ],
        compiler_params=pltpu.CompilerParams(vmem_limit_bytes=50 * 1024 * 1024),
        name="columns",
    )(
        block_rows.reshape(-1), where, place,
        low, block_weights, factor_out, upstream, *arrays,
    )

    got = shift("core", NC, 1)(send)
    paired = pl.pallas_call(
        pair_kernel,
        grid=(NY,),
        in_specs=[pl.BlockSpec((1, PART_ROWS, BS), lambda i: (i, 0, 0))] * 2,
        out_specs=pl.BlockSpec((1, PART_ROWS, BS), lambda i: (i, 0, 0)),
        out_shape=jax.ShapeDtypeStruct((NY, PART_ROWS, BS), jnp.int16),
        compiler_params=pltpu.CompilerParams(vmem_limit_bytes=50 * 1024 * 1024),
        name="pairs",
    )(keep, got)
    first_y = [shift("y", NY, i)(paired[i, :CUT]) for i in (1, 2, 3)]

    back = back.reshape(NZ, NX, ROWS, BS)
    pick = lambda step: lax.dynamic_index_in_dim(back, turn_x(step), 1, keepdims=False)
    back_x = (pick(0) + across(pick(2))) + (x_up(pick(1)) + x_down(pick(-1)))
    back_x, _ = lax.optimization_barrier((back_x, paired))
    for bit in (1, 2, 4):
        back_x = back_x + flip("z", NZ, bit)(back_x)
    back_x, rest, _ = lax.optimization_barrier((back_x, paired[1:, CUT:], first_y))
    second_y = [shift("y", NY, i)(rest[i - 1]) for i in (1, 2, 3)]
    backs = [back_x, x_up(back_x), x_down(back_x), across(back_x)]
    turns = jnp.stack([part_of(jnp.int32(d)) for d in range(GROUPS)]).astype(jnp.int32)
    in_part = in_partial(near, turns, cols, backs)
    in_sum = in_part[NY:] + shift("core", NC, 1)(in_part[:NY])
    in_sum, _ = lax.optimization_barrier((in_sum, second_y))
    in_grad = in_sum[0]
    for step in (1, 2, 3):
        in_grad = in_grad + shift("y", NY, step)(in_sum[step])

    whole = pl.BlockSpec(memory_space=pltpu.VMEM)
    slots, out_grad = pl.pallas_call(
        final_kernel,
        in_specs=[pl.BlockSpec(memory_space=pltpu.SMEM)] + [whole] * (2 * NY - 1),
        out_specs=[whole, whole],
        out_shape=[
            jax.ShapeDtypeStruct((CAP, BS, BS), jnp.float32),
            jax.ShapeDtypeStruct((BS, FO_ROWS), jnp.float32),
        ],
        compiler_params=pltpu.CompilerParams(vmem_limit_bytes=50 * 1024 * 1024),
        name="slots",
    )(mine, paired, *first_y, *second_y)
    return hidden, slots, in_grad, out_grad


def solution(mesh):
    split = Mesh(mesh.devices.reshape(NY, NC, NZ, NX), ("y", "core", "z", "x"))
    dp, mp = ("y", "core"), ("z", "x")
    return jax.shard_map(
        per_device,
        mesh=split,
        in_specs=(
            P(dp + mp, None),
            P(mp, None, None, None),
            P(mp, None),
            P(mp, None, None),
            P(mp, None),
            P(None, mp),
            P(dp, mp),
        ),
        out_specs=(
            P(dp, mp),
            P(mp + dp, None, None),
            P(mp + dp, None),
            P(None, mp + dp),
        ),
        check_vma=False,
    )
```

```python
import functools

import jax
import jax.numpy as jnp
from jax import lax
from jax.experimental import pallas as pl
from jax.experimental.pallas import tpu as pltpu
from jax.sharding import Mesh
from jax.sharding import PartitionSpec as P

highest = lax.Precision.HIGHEST
BS = 128
ROWS = 16
NX, NZ, NY, NC = 4, 8, 4, 2
COLS = 12
PER_STEP = 2
KB = 8
RB = 96
CAP = 18
GROUPS = NY * NC
SLOT_ROWS = CAP * BS
FO_ROWS = COLS * BS // GROUPS
CODE_ROWS = SLOT_ROWS + FO_ROWS
PART_ROWS = CODE_ROWS + 32
FINE = 256.0
CUT = 14 * BS


def shift(axis, size, step):
    pairs = [(i, (i + step) % size) for i in range(size)]
    return lambda value: lax.ppermute(value, axis, pairs)


def flip(axis, size, bit):
    pairs = [(i, i ^ bit) for i in range(size)]
    return lambda value: lax.ppermute(value, axis, pairs)


def split_two(value):
    high = value.astype(jnp.bfloat16)
    low = (value - high.astype(jnp.float32)).astype(jnp.bfloat16)
    return high, low


def level_of(block):
    top = jnp.max(jnp.abs(block), axis=0, keepdims=True)
    return jnp.ceil(jnp.log2(jnp.maximum(top, 1e-30)) * FINE)


def encode(block, level):
    inverse = jnp.exp2(level * (-1.0 / FINE)) * 32700.0
    return jnp.floor(block * inverse + 0.5).astype(jnp.int32).astype(jnp.int16)


def decode(code, level):
    unit = jnp.exp2(level * (1.0 / FINE)) * (1.0 / 32700.0)
    return code.astype(jnp.int32).astype(jnp.float32) * unit


def main_kernel(
    counts, rows_ref, where_ref, place_ref, low_ref, weight_ref, factor_ref, up_ref, *rest
):
    arrays, rest = rest[: len(counts)], rest[len(counts) :]
    pieces = [ref.at[i] for ref, n in zip(arrays, counts) for i in range(n)]
    hidden_ref, send_ref, keep_ref, back_ref = rest[:4]
    tok, wide, low_two, codes, levels, sems = rest[4:]
    c = pl.program_id(0)
    tokens = NX * NZ * ROWS

    @pl.when(c == 0)
    def _():
        for j in range(NX * NZ):
            pltpu.make_async_copy(pieces[j], tok.at[place_ref[j]], sems.at[j]).start()
        high, low = split_two(low_ref[...])
        low_two[:, :BS] = high
        low_two[:, BS:] = low
        wide[(KB + 1) * BS :, BS:] = jnp.zeros((BS, BS), jnp.bfloat16)
        back_ref[...] = jnp.zeros_like(back_ref)
        for j in range(NX * NZ):
            pltpu.make_async_copy(pieces[j], tok.at[place_ref[j]], sems.at[j]).wait()

    for i in range(PER_STEP):
        col = c * PER_STEP + i
        here = slice(i * BS, (i + 1) * BS)
        for k in range(KB):
            high, low = split_two(weight_ref[i, k])
            wide[k * BS : (k + 1) * BS, :BS] = high
            wide[k * BS : (k + 1) * BS, BS:] = low
        f_high, f_low = split_two(factor_ref[:, here])
        wide[KB * BS : (KB + 1) * BS, :BS] = f_high
        wide[KB * BS : (KB + 1) * BS, BS:] = f_low
        wide[(KB + 1) * BS :, :BS] = f_high

        panel = jnp.concatenate(
            [tok[:, rows_ref[col * KB + k]].reshape(tokens, BS) for k in range(KB)]
            + [low_two[...]],
            axis=1,
        )
        both = jnp.dot(panel, wide[...], preferred_element_type=jnp.float32)
        v = both[:, :BS] + both[:, BS:]
        root = 0.7978845608028654
        square = v * v
        t = jnp.tanh(root * v * (1.0 + 0.044715 * square))
        half = 0.5 * (1.0 + t)
        hidden_ref[:, here] = (v * half).astype(jnp.bfloat16)
        slope = half + 0.5 * root * v * (1.0 - t * t) * (1.0 + 3.0 * 0.044715 * square)
        grad = up_ref[:, here].astype(jnp.float32) * slope

        g_high, g_low = split_two(grad)
        g_two = jnp.concatenate([g_high, g_low], axis=1)
        f_two = jnp.concatenate(
            [
                jnp.concatenate([f_high, f_high], axis=1),
                jnp.concatenate([f_low, jnp.zeros_like(f_low)], axis=1),
            ],
            axis=0,
        )
        back = lax.dot_general(
            g_two, f_two, (((1,), (1,)), ((), ())), preferred_element_type=jnp.float32
        )
        back_ref[...] += back[:, :BS] + back[:, BS:]

        grad_t = grad.T
        t_high, t_low = split_two(grad_t)
        gt_two = jnp.concatenate([t_high, t_low], axis=0)
        product = jnp.dot(gt_two, panel, preferred_element_type=jnp.float32)
        product = product[:BS] + product[BS:]
        for k in range(KB):
            block = product[:, k * BS : (k + 1) * BS]
            level = level_of(block)
            part = where_ref[0, col * KB + k]
            slot = where_ref[1, col * KB + k]
            codes[part, pl.ds(pl.multiple_of(slot * BS, BS), BS)] = encode(block, level)
            levels[part, pl.ds(slot, 1)] = level
        outer = product[:, KB * BS : (KB + 1) * BS] + product[:, (KB + 1) * BS :]
        for h in range(2):
            block = outer[h * 64 : (h + 1) * 64]
            level = level_of(block)
            part = where_ref[2, col * 2 + h]
            slot = where_ref[3, col * 2 + h]
            start = pl.multiple_of(SLOT_ROWS + slot * 64, 64)
            codes[part, pl.ds(start, 64)] = encode(block, level)
            levels[part, pl.ds(CAP + slot, 1)] = level

    @pl.when(c == COLS // PER_STEP - 1)
    def _():
        for part in range(2 * NY):
            codes[part, CODE_ROWS:] = levels[part].astype(jnp.int32).astype(jnp.int16)
        send = pltpu.make_async_copy(codes.at[pl.ds(0, NY)], send_ref, sems.at[0])
        keep = pltpu.make_async_copy(codes.at[pl.ds(NY, NY)], keep_ref, sems.at[1])
        send.start()
        keep.start()
        send.wait()
        keep.wait()


def blocks_of():
    spans = [(s * BS, BS, s) for s in range(CAP)]
    return spans + [(SLOT_ROWS + h * 64, 64, CAP + h) for h in range(FO_ROWS // 64)]


def pair_kernel(keep_ref, got_ref, out_ref):
    keep_levels = keep_ref[0, CODE_ROWS:].astype(jnp.int32).astype(jnp.float32)
    got_levels = got_ref[0, CODE_ROWS:].astype(jnp.int32).astype(jnp.float32)
    fresh = []
    for start, size, index in blocks_of():
        span = slice(start, start + size)
        total = decode(keep_ref[0, span], keep_levels[index : index + 1])
        total += decode(got_ref[0, span], got_levels[index : index + 1])
        level = level_of(total)
        out_ref[0, span] = encode(total, level)
        fresh.append(level)
    fresh.append(jnp.zeros((32 - len(fresh), BS), jnp.float32))
    fresh = jnp.concatenate(fresh, axis=0)
    out_ref[0, CODE_ROWS:] = fresh.astype(jnp.int32).astype(jnp.int16)


def final_kernel(count_ref, own_ref, *refs):
    firsts, seconds = refs[: NY - 1], refs[NY - 1 : 2 * NY - 2]
    slots_ref, outer_ref = refs[2 * NY - 2 :]
    tails = [own_ref[0, CODE_ROWS:]] + [r[CODE_ROWS - CUT :] for r in seconds]
    levels = [t.astype(jnp.int32).astype(jnp.float32) for t in tails]
    count = count_ref[0]
    for start, size, index in blocks_of():
        total = decode(own_ref[0, start : start + size], levels[0][index : index + 1])
        for i in range(NY - 1):
            if start < CUT:
                code = firsts[i][start : start + size]
            else:
                code = seconds[i][start - CUT : start - CUT + size]
            total += decode(code, levels[i + 1][index : index + 1])
        if index < CAP:
            slots_ref[index] = jnp.where(index < count, total.T, 0.0)
        else:
            h = index - CAP
            outer_ref[:, h * 64 : (h + 1) * 64] = total.T


def in_kernel(near_ref, turns_ref, cols_ref, *rest):
    backs, (out_ref, full) = rest[:NX], rest[NX:]
    for j in range(NX):
        for g in range(NZ):
            full[g, near_ref[j]] = backs[j][g]
    total = NZ * NX * ROWS
    high, low = split_two(full[...].reshape(total, BS).T)
    two = jnp.concatenate([high, low], axis=0)
    panel = jnp.concatenate(
        [cols_ref[:, j].reshape(total, BS) for j in range(cols_ref.shape[1])], axis=1
    )
    both = jnp.dot(two, panel, preferred_element_type=jnp.float32)
    grad = (both[:BS] + both[BS:]).T
    size = grad.shape[0] // GROUPS
    for d in range(GROUPS):
        out_ref[turns_ref[d]] = grad[d * size : (d + 1) * size]


def in_partial(near, turns, cols, backs):
    small = pl.BlockSpec(memory_space=pltpu.SMEM)
    whole = pl.BlockSpec(memory_space=pltpu.VMEM)
    size = cols.shape[1] * BS // GROUPS
    return pl.pallas_call(
        in_kernel,
        in_specs=[small, small, whole] + [whole] * NX,
        out_specs=whole,
        out_shape=jax.ShapeDtypeStruct((GROUPS, size, BS), jnp.float32),
        scratch_shapes=[pltpu.VMEM((NZ, NX, ROWS, BS), jnp.float32)],
        compiler_params=pltpu.CompilerParams(vmem_limit_bytes=30 * 1024 * 1024),
        name="into",
    )(near, turns, cols, *backs)


def gather_tokens(own, factor):
    z_up, z_down = shift("z", NZ, 1), shift("z", NZ, -1)
    x_up, x_down, across = shift("x", NX, 1), shift("x", NX, -1), shift("x", NX, 2)
    after = lambda value, *others: lax.optimization_barrier((value, others))[0]
    ring, far, sent = {0: own}, {}, {}

    def step(part, a):
        part[-a] = z_up(part[1 - a])
        part[a] = z_down(part[a - 1])

    def batch(*which, later=()):
        block = after(jnp.stack([ring[a] for a in which]), *later)
        sent[which] = (x_up(block), x_down(block))
        return sent[which]

    step(ring, 1)
    far[0] = across(own)
    side = batch(0)
    spread = lax.all_to_all(own.reshape(NX * NZ, -1, ROWS, BS), ("z", "x"), 0, 0)
    step(ring, 2)
    first = batch(1, -1)
    own_cols = after(spread, ring[2], ring[-2]).astype(jnp.float32)
    partial = jnp.einsum("sbtf,bfr->str", own_cols, factor, precision=highest)
    ring[2], ring[-2] = after((ring[2], ring[-2]), far[0], side, partial)
    step(ring, 3)
    step(far, 1)
    second = batch(2, -2)
    low_own = jnp.sum(after(lax.all_to_all(partial, ("z", "x"), 0, 0), first), axis=0)
    ring[3], ring[-3] = after((ring[3], ring[-3]), first, far[1], far[-1], low_own)
    ring[4] = z_up(ring[-3])
    step(far, 2)
    low = lax.all_to_all(
        jnp.broadcast_to(low_own[None], (NX * NZ, ROWS, BS)), ("z", "x"), 0, 0
    )
    batch(3, -3, 4, later=(second, far[2], far[-2]))
    step(far, 3)
    low = after(low, far[3], far[-3])
    far[4] = z_down(far[3])
    arrays, keys = [], []
    for b, part in ((0, ring), (2, far)):
        for a in part:
            arrays.append(part[a][None])
            keys.append([(a, b)])
    for which, pair in sent.items():
        for b, value in zip((-1, 1), pair):
            arrays.append(value)
            keys.append([(a, b) for a in which])
    return arrays, keys, spread, low


def per_device(tokens, block_weights, block_rows, block_owners, factor_in, factor_out, upstream):
    own = jnp.transpose(tokens.reshape(ROWS, RB, BS), (1, 0, 2))
    span = NX * NZ
    per = RB // span
    arrays, keys, spread, low = gather_tokens(own, factor_in.reshape(per, BS, BS))
    z, x = lax.axis_index("z"), lax.axis_index("x")
    y, core = lax.axis_index("y"), lax.axis_index("core")
    place = [((z + a) % NZ) * NX + (x + b) % NX for group in keys for a, b in group]
    place = jnp.stack(place).astype(jnp.int32)
    turn_x = lambda step: jnp.asarray((x + step) % NX, jnp.int32)
    x_up, x_down, across = shift("x", NX, 1), shift("x", NX, -1), shift("x", NX, 2)
    near = jnp.stack([turn_x(b) for b in (0, -1, 1, 2)])
    low = low.reshape(span * ROWS, BS)

    owners = block_owners.reshape(-1)
    count_all = owners.shape[0]
    marks = (owners[:, None] == jnp.arange(GROUPS, dtype=jnp.int32)[None, :]).astype(jnp.int32)
    before = (
        jnp.arange(count_all, dtype=jnp.int32)[:, None]
        > jnp.arange(count_all, dtype=jnp.int32)[None, :]
    ) & (owners[:, None] == owners[None, :])
    rank = jnp.sum(before.astype(jnp.int32), axis=1)

    def part_of(owner):
        turn = (owner // NC - y) % NY
        return turn + jnp.where(owner % NC == core, NY, 0)

    halves = jnp.arange(2 * COLS, dtype=jnp.int32)
    per_owner = FO_ROWS // 64
    pad = count_all - 2 * COLS
    where = jnp.stack(
        [
            part_of(owners),
            rank,
            jnp.pad(part_of(halves // per_owner), (0, pad)),
            jnp.pad(halves % per_owner, (0, pad)),
        ]
    ).astype(jnp.int32)
    counts = jnp.sum(marks, axis=0)
    mine = jnp.sum(
        jnp.where(jnp.arange(GROUPS) == y * NC + core, counts, 0), dtype=jnp.int32
    ).reshape(1)

    total = span * ROWS
    anywhere = pl.BlockSpec(memory_space=pl.ANY)
    hidden, send, keep, back = pl.pallas_call(
        functools.partial(main_kernel, [len(g) for g in keys]),
        grid_spec=pltpu.PrefetchScalarGridSpec(
            num_scalar_prefetch=3,
            grid=(COLS // PER_STEP,),
            in_specs=[
                pl.BlockSpec((total, BS), lambda c, *_: (0, 0)),
                pl.BlockSpec((PER_STEP, KB, BS, BS), lambda c, *_: (c, 0, 0, 0)),
                pl.BlockSpec((BS, PER_STEP * BS), lambda c, *_: (0, c)),
                pl.BlockSpec((total, PER_STEP * BS), lambda c, *_: (0, c)),
            ]
            + [anywhere] * len(arrays),
            out_specs=[
                pl.BlockSpec((total, PER_STEP * BS), lambda c, *_: (0, c)),
                anywhere,
                anywhere,
                pl.BlockSpec((total, BS), lambda c, *_: (0, 0)),
            ],
            scratch_shapes=[
                pltpu.VMEM((span, RB, ROWS, BS), jnp.bfloat16),
                pltpu.VMEM(((KB + 2) * BS, 2 * BS), jnp.bfloat16),
                pltpu.VMEM((total, 2 * BS), jnp.bfloat16),
                pltpu.VMEM((2 * NY, PART_ROWS, BS), jnp.int16),
                pltpu.VMEM((2 * NY, 32, BS), jnp.float32),
                pltpu.SemaphoreType.DMA((span,)),
            ],
        ),
        out_shape=[
            jax.ShapeDtypeStruct((total, COLS * BS), jnp.bfloat16),
            jax.ShapeDtypeStruct((NY, PART_ROWS, BS), jnp.int16),
            jax.ShapeDtypeStruct((NY, PART_ROWS, BS), jnp.int16),
            jax.ShapeDtypeStruct((total, BS), jnp.float32),
        ],
        compiler_params=pltpu.CompilerParams(vmem_limit_bytes=50 * 1024 * 1024),
        name="columns",
    )(
        block_rows.reshape(-1), where, place,
        low, block_weights, factor_out, upstream, *arrays,
    )

    got = shift("core", NC, 1)(send)
    paired = pl.pallas_call(
        pair_kernel,
        grid=(NY,),
        in_specs=[pl.BlockSpec((1, PART_ROWS, BS), lambda i: (i, 0, 0))] * 2,
        out_specs=pl.BlockSpec((1, PART_ROWS, BS), lambda i: (i, 0, 0)),
        out_shape=jax.ShapeDtypeStruct((NY, PART_ROWS, BS), jnp.int16),
        compiler_params=pltpu.CompilerParams(vmem_limit_bytes=50 * 1024 * 1024),
        name="pairs",
    )(keep, got)
    first_y = [shift("y", NY, i)(paired[i, :CUT]) for i in (1, 2, 3)]

    back = back.reshape(NZ, NX, ROWS, BS)
    pick = lambda step: lax.dynamic_index_in_dim(back, turn_x(step), 1, keepdims=False)
    back_x = (pick(0) + across(pick(2))) + (x_up(pick(1)) + x_down(pick(-1)))
    back_x = back_x + flip("z", NZ, 1)(back_x)
    back_x, _ = lax.optimization_barrier((back_x, paired))
    for bit in (2, 4):
        back_x = back_x + flip("z", NZ, bit)(back_x)
    back_x, rest, _ = lax.optimization_barrier((back_x, paired[1:, CUT:], first_y))
    second_y = [shift("y", NY, i)(rest[i - 1]) for i in (1, 2, 3)]
    backs = [back_x, x_up(back_x), x_down(back_x), across(back_x)]
    turns = jnp.stack([part_of(jnp.int32(d)) for d in range(GROUPS)]).astype(jnp.int32)
    in_part = in_partial(near, turns, spread, backs)
    in_sum = in_part[NY:] + shift("core", NC, 1)(in_part[:NY])
    in_sum, _ = lax.optimization_barrier((in_sum, second_y))
    in_grad = in_sum[0]
    for step in (1, 2, 3):
        in_grad = in_grad + shift("y", NY, step)(in_sum[step])

    whole = pl.BlockSpec(memory_space=pltpu.VMEM)
    slots, out_grad = pl.pallas_call(
        final_kernel,
        in_specs=[pl.BlockSpec(memory_space=pltpu.SMEM)] + [whole] * (2 * NY - 1),
        out_specs=[whole, whole],
        out_shape=[
            jax.ShapeDtypeStruct((CAP, BS, BS), jnp.float32),
            jax.ShapeDtypeStruct((BS, FO_ROWS), jnp.float32),
        ],
        compiler_params=pltpu.CompilerParams(vmem_limit_bytes=50 * 1024 * 1024),
        name="slots",
    )(mine, paired, *first_y, *second_y)
    return hidden, slots, in_grad, out_grad


def solution(mesh):
    split = Mesh(mesh.devices.reshape(NY, NC, NZ, NX), ("y", "core", "z", "x"))
    dp, mp = ("y", "core"), ("z", "x")
    return jax.shard_map(
        per_device,
        mesh=split,
        in_specs=(
            P(dp + mp, None),
            P(mp, None, None, None),
            P(mp, None),
            P(mp, None, None),
            P(mp, None),
            P(None, mp),
            P(dp, mp),
        ),
        out_specs=(
            P(dp, mp),
            P(mp + dp, None, None),
            P(mp + dp, None),
            P(None, mp + dp),
        ),
        check_vma=False,
    )
```

```python
import jax
import jax.numpy as jnp
from jax import lax
from jax.experimental import pallas as pl
from jax.experimental.pallas import tpu as pltpu
from jax.sharding import Mesh
from jax.sharding import PartitionSpec as P

highest = lax.Precision.HIGHEST
BS = 128
ROWS = 16
NX, NZ, NY, NC = 4, 8, 4, 2
COLS = 12
PER_STEP = 2
KB = 8
RB = 96
CAP = 18
GROUPS = NY * NC
SLOT_ROWS = CAP * BS
FO_ROWS = COLS * BS // GROUPS
CODE_ROWS = SLOT_ROWS + FO_ROWS
PART_ROWS = CODE_ROWS + 32
FINE = 256.0
CUT = 14 * BS
HALF = 48


def shift(axis, size, step):
    pairs = [(i, (i + step) % size) for i in range(size)]
    return lambda value: lax.ppermute(value, axis, pairs)


def flip(axis, size, bit):
    pairs = [(i, i ^ bit) for i in range(size)]
    return lambda value: lax.ppermute(value, axis, pairs)


def split_two(value):
    high = value.astype(jnp.bfloat16)
    low = (value - high.astype(jnp.float32)).astype(jnp.bfloat16)
    return high, low


def level_of(block):
    top = jnp.max(jnp.abs(block), axis=0, keepdims=True)
    return jnp.ceil(jnp.log2(jnp.maximum(top, 1e-30)) * FINE)


def encode(block, level):
    inverse = jnp.exp2(level * (-1.0 / FINE)) * 32700.0
    return jnp.floor(block * inverse + 0.5).astype(jnp.int32).astype(jnp.int16)


def decode(code, level):
    unit = jnp.exp2(level * (1.0 / FINE)) * (1.0 / 32700.0)
    return code.astype(jnp.int32).astype(jnp.float32) * unit


def main_kernel(
    rows_ref, where_ref, place_ref, low_ref, weight_ref, factor_ref, up_ref, *rest
):
    half_ref, pieces, rest = rest[0], rest[1 : 1 + NX * NZ], rest[1 + NX * NZ :]
    hidden_ref, send_ref, keep_ref, back_ref = rest[:4]
    tok, wide, low_two, codes, levels, sems = rest[4:]
    c = pl.program_id(0)
    tokens = NX * NZ * ROWS

    @pl.when(c == 0)
    def _():
        copies = [pltpu.make_async_copy(half_ref, tok.at[:, pl.ds(0, HALF)], sems.at[NX * NZ])]
        for j in range(NX * NZ):
            target = tok.at[place_ref[j], pl.ds(HALF, RB - HALF)]
            copies.append(pltpu.make_async_copy(pieces[j], target, sems.at[j]))
        for copy in copies:
            copy.start()
        high, low = split_two(low_ref[...])
        low_two[:, :BS] = high
        low_two[:, BS:] = low
        wide[(KB + 1) * BS :, BS:] = jnp.zeros((BS, BS), jnp.bfloat16)
        back_ref[...] = jnp.zeros_like(back_ref)
        for copy in copies:
            copy.wait()

    for i in range(PER_STEP):
        col = c * PER_STEP + i
        here = slice(i * BS, (i + 1) * BS)
        for k in range(KB):
            high, low = split_two(weight_ref[i, k])
            wide[k * BS : (k + 1) * BS, :BS] = high
            wide[k * BS : (k + 1) * BS, BS:] = low
        f_high, f_low = split_two(factor_ref[:, here])
        wide[KB * BS : (KB + 1) * BS, :BS] = f_high
        wide[KB * BS : (KB + 1) * BS, BS:] = f_low
        wide[(KB + 1) * BS :, :BS] = f_high

        panel = jnp.concatenate(
            [tok[:, rows_ref[col * KB + k]].reshape(tokens, BS) for k in range(KB)]
            + [low_two[...]],
            axis=1,
        )
        both = jnp.dot(panel, wide[...], preferred_element_type=jnp.float32)
        v = both[:, :BS] + both[:, BS:]
        root = 0.7978845608028654
        square = v * v
        t = jnp.tanh(root * v * (1.0 + 0.044715 * square))
        half = 0.5 * (1.0 + t)
        hidden_ref[:, here] = (v * half).astype(jnp.bfloat16)
        slope = half + 0.5 * root * v * (1.0 - t * t) * (1.0 + 3.0 * 0.044715 * square)
        grad = up_ref[:, here].astype(jnp.float32) * slope

        g_high, g_low = split_two(grad)
        g_two = jnp.concatenate([g_high, g_low], axis=1)
        f_two = jnp.concatenate(
            [
                jnp.concatenate([f_high, f_high], axis=1),
                jnp.concatenate([f_low, jnp.zeros_like(f_low)], axis=1),
            ],
            axis=0,
        )
        back = lax.dot_general(
            g_two, f_two, (((1,), (1,)), ((), ())), preferred_element_type=jnp.float32
        )
        back_ref[...] += back[:, :BS] + back[:, BS:]

        grad_t = grad.T
        t_high, t_low = split_two(grad_t)
        gt_two = jnp.concatenate([t_high, t_low], axis=0)
        product = jnp.dot(gt_two, panel, preferred_element_type=jnp.float32)
        product = product[:BS] + product[BS:]
        for k in range(KB):
            block = product[:, k * BS : (k + 1) * BS]
            level = level_of(block)
            part = where_ref[0, col * KB + k]
            slot = where_ref[1, col * KB + k]
            codes[part, pl.ds(pl.multiple_of(slot * BS, BS), BS)] = encode(block, level)
            levels[part, pl.ds(slot, 1)] = level
        outer = product[:, KB * BS : (KB + 1) * BS] + product[:, (KB + 1) * BS :]
        for h in range(2):
            block = outer[h * 64 : (h + 1) * 64]
            level = level_of(block)
            part = where_ref[2, col * 2 + h]
            slot = where_ref[3, col * 2 + h]
            start = pl.multiple_of(SLOT_ROWS + slot * 64, 64)
            codes[part, pl.ds(start, 64)] = encode(block, level)
            levels[part, pl.ds(CAP + slot, 1)] = level

    @pl.when(c == COLS // PER_STEP - 1)
    def _():
        for part in range(2 * NY):
            codes[part, CODE_ROWS:] = levels[part].astype(jnp.int32).astype(jnp.int16)
        send = pltpu.make_async_copy(codes.at[pl.ds(0, NY)], send_ref, sems.at[0])
        keep = pltpu.make_async_copy(codes.at[pl.ds(NY, NY)], keep_ref, sems.at[1])
        send.start()
        keep.start()
        send.wait()
        keep.wait()


def blocks_of():
    spans = [(s * BS, BS, s) for s in range(CAP)]
    return spans + [(SLOT_ROWS + h * 64, 64, CAP + h) for h in range(FO_ROWS // 64)]


def pair_kernel(keep_ref, got_ref, out_ref):
    keep_levels = keep_ref[0, CODE_ROWS:].astype(jnp.int32).astype(jnp.float32)
    got_levels = got_ref[0, CODE_ROWS:].astype(jnp.int32).astype(jnp.float32)
    fresh = []
    for start, size, index in blocks_of():
        span = slice(start, start + size)
        total = decode(keep_ref[0, span], keep_levels[index : index + 1])
        total += decode(got_ref[0, span], got_levels[index : index + 1])
        level = level_of(total)
        out_ref[0, span] = encode(total, level)
        fresh.append(level)
    fresh.append(jnp.zeros((32 - len(fresh), BS), jnp.float32))
    fresh = jnp.concatenate(fresh, axis=0)
    out_ref[0, CODE_ROWS:] = fresh.astype(jnp.int32).astype(jnp.int16)


def final_kernel(count_ref, own_ref, *refs):
    firsts, seconds = refs[: NY - 1], refs[NY - 1 : 2 * NY - 2]
    slots_ref, outer_ref = refs[2 * NY - 2 :]
    tails = [own_ref[0, CODE_ROWS:]] + [r[CODE_ROWS - CUT :] for r in seconds]
    levels = [t.astype(jnp.int32).astype(jnp.float32) for t in tails]
    count = count_ref[0]
    for start, size, index in blocks_of():
        total = decode(own_ref[0, start : start + size], levels[0][index : index + 1])
        for i in range(NY - 1):
            if start < CUT:
                code = firsts[i][start : start + size]
            else:
                code = seconds[i][start - CUT : start - CUT + size]
            total += decode(code, levels[i + 1][index : index + 1])
        if index < CAP:
            slots_ref[index] = jnp.where(index < count, total.T, 0.0)
        else:
            h = index - CAP
            outer_ref[:, h * 64 : (h + 1) * 64] = total.T


def in_kernel(near_ref, turns_ref, cols_ref, *rest):
    backs, (out_ref, full) = rest[:NX], rest[NX:]
    for j in range(NX):
        for g in range(NZ):
            full[g, near_ref[j]] = backs[j][g]
    total = NZ * NX * ROWS
    high, low = split_two(full[...].reshape(total, BS).T)
    two = jnp.concatenate([high, low], axis=0)
    panel = jnp.concatenate(
        [cols_ref[:, j].reshape(total, BS) for j in range(cols_ref.shape[1])], axis=1
    )
    both = jnp.dot(two, panel, preferred_element_type=jnp.float32)
    grad = (both[:BS] + both[BS:]).T
    size = grad.shape[0] // GROUPS
    for d in range(GROUPS):
        out_ref[turns_ref[d]] = grad[d * size : (d + 1) * size]


def in_partial(near, turns, cols, backs):
    small = pl.BlockSpec(memory_space=pltpu.SMEM)
    whole = pl.BlockSpec(memory_space=pltpu.VMEM)
    size = cols.shape[1] * BS // GROUPS
    return pl.pallas_call(
        in_kernel,
        in_specs=[small, small, whole] + [whole] * NX,
        out_specs=whole,
        out_shape=jax.ShapeDtypeStruct((GROUPS, size, BS), jnp.float32),
        scratch_shapes=[pltpu.VMEM((NZ, NX, ROWS, BS), jnp.float32)],
        compiler_params=pltpu.CompilerParams(vmem_limit_bytes=30 * 1024 * 1024),
        name="into",
    )(near, turns, cols, *backs)


def gather_tokens(own):
    z_up, z_down = shift("z", NZ, 1), shift("z", NZ, -1)
    x_up, x_down = shift("x", NX, 1), shift("x", NX, -1)
    across = shift("x", NX, 2)
    held = {(0, 0): own}
    held[0, 2] = across(own)
    for b in (0, 2):
        for a in (1, 2, 3):
            held[-a, b] = z_up(held[1 - a, b])
            held[a, b] = z_down(held[a - 1, b])
    held[4, 0] = z_up(held[-3, 0])
    held[4, 2] = z_down(held[3, 2])
    for a in (0, -1, 1, -2, 2, -3, 3, 4):
        for b, move in ((-1, x_up), (1, x_down)):
            if (a, b) in ((1, 1), (-1, -1)):
                held[a, b] = (z_down if a > 0 else z_up)(held[0, b])
            else:
                held[a, b] = move(held[a, 0])
    return held


def per_device(tokens, block_weights, block_rows, block_owners, factor_in, factor_out, upstream):
    own = jnp.transpose(tokens.reshape(ROWS, RB, BS), (1, 0, 2))
    span = NX * NZ
    per = RB // span
    plane = ("z", "x")
    whole_half = lax.all_gather(own[:HALF], plane, axis=0)
    held = gather_tokens(own[HALF:])
    order = sorted(held)
    arrays = [held[key] for key in order]
    spread = lax.all_to_all(own.reshape(span, per, ROWS, BS), plane, 0, 0)
    factor = factor_in.reshape(per, BS, BS)
    partial = jnp.einsum(
        "sbtf,bfr->str", spread.astype(jnp.float32), factor, precision=highest
    )
    low_own = jnp.sum(lax.all_to_all(partial, plane, 0, 0), axis=0)
    low = lax.all_to_all(jnp.broadcast_to(low_own[None], (span, ROWS, BS)), plane, 0, 0)
    z, x = lax.axis_index("z"), lax.axis_index("x")
    y, core = lax.axis_index("y"), lax.axis_index("core")
    place = [((z + a) % NZ) * NX + (x + b) % NX for a, b in order]
    place = jnp.stack(place).astype(jnp.int32)
    turn_x = lambda step: jnp.asarray((x + step) % NX, jnp.int32)
    x_up, x_down, across = shift("x", NX, 1), shift("x", NX, -1), shift("x", NX, 2)
    near = jnp.stack([turn_x(b) for b in (0, -1, 1, 2)])
    low = low.reshape(span * ROWS, BS)

    owners = block_owners.reshape(-1)
    count_all = owners.shape[0]
    marks = (owners[:, None] == jnp.arange(GROUPS, dtype=jnp.int32)[None, :]).astype(jnp.int32)
    before = (
        jnp.arange(count_all, dtype=jnp.int32)[:, None]
        > jnp.arange(count_all, dtype=jnp.int32)[None, :]
    ) & (owners[:, None] == owners[None, :])
    rank = jnp.sum(before.astype(jnp.int32), axis=1)

    def part_of(owner):
        turn = (owner // NC - y) % NY
        return turn + jnp.where(owner % NC == core, NY, 0)

    halves = jnp.arange(2 * COLS, dtype=jnp.int32)
    per_owner = FO_ROWS // 64
    pad = count_all - 2 * COLS
    where = jnp.stack(
        [
            part_of(owners),
            rank,
            jnp.pad(part_of(halves // per_owner), (0, pad)),
            jnp.pad(halves % per_owner, (0, pad)),
        ]
    ).astype(jnp.int32)
    counts = jnp.sum(marks, axis=0)
    mine = jnp.sum(
        jnp.where(jnp.arange(GROUPS) == y * NC + core, counts, 0), dtype=jnp.int32
    ).reshape(1)

    total = span * ROWS
    anywhere = pl.BlockSpec(memory_space=pl.ANY)
    hidden, send, keep, back = pl.pallas_call(
        main_kernel,
        grid_spec=pltpu.PrefetchScalarGridSpec(
            num_scalar_prefetch=3,
            grid=(COLS // PER_STEP,),
            in_specs=[
                pl.BlockSpec((total, BS), lambda c, *_: (0, 0)),
                pl.BlockSpec((PER_STEP, KB, BS, BS), lambda c, *_: (c, 0, 0, 0)),
                pl.BlockSpec((BS, PER_STEP * BS), lambda c, *_: (0, c)),
                pl.BlockSpec((total, PER_STEP * BS), lambda c, *_: (0, c)),
            ]
            + [anywhere] * (span + 1),
            out_specs=[
                pl.BlockSpec((total, PER_STEP * BS), lambda c, *_: (0, c)),
                anywhere,
                anywhere,
                pl.BlockSpec((total, BS), lambda c, *_: (0, 0)),
            ],
            scratch_shapes=[
                pltpu.VMEM((span, RB, ROWS, BS), jnp.bfloat16),
                pltpu.VMEM(((KB + 2) * BS, 2 * BS), jnp.bfloat16),
                pltpu.VMEM((total, 2 * BS), jnp.bfloat16),
                pltpu.VMEM((2 * NY, PART_ROWS, BS), jnp.int16),
                pltpu.VMEM((2 * NY, 32, BS), jnp.float32),
                pltpu.SemaphoreType.DMA((span + 1,)),
            ],
        ),
        out_shape=[
            jax.ShapeDtypeStruct((total, COLS * BS), jnp.bfloat16),
            jax.ShapeDtypeStruct((NY, PART_ROWS, BS), jnp.int16),
            jax.ShapeDtypeStruct((NY, PART_ROWS, BS), jnp.int16),
            jax.ShapeDtypeStruct((total, BS), jnp.float32),
        ],
        compiler_params=pltpu.CompilerParams(vmem_limit_bytes=50 * 1024 * 1024),
        name="columns",
    )(
        block_rows.reshape(-1), where, place,
        low, block_weights, factor_out, upstream, whole_half, *arrays,
    )

    got = shift("core", NC, 1)(send)
    paired = pl.pallas_call(
        pair_kernel,
        grid=(NY,),
        in_specs=[pl.BlockSpec((1, PART_ROWS, BS), lambda i: (i, 0, 0))] * 2,
        out_specs=pl.BlockSpec((1, PART_ROWS, BS), lambda i: (i, 0, 0)),
        out_shape=jax.ShapeDtypeStruct((NY, PART_ROWS, BS), jnp.int16),
        compiler_params=pltpu.CompilerParams(vmem_limit_bytes=50 * 1024 * 1024),
        name="pairs",
    )(keep, got)
    first_y = [shift("y", NY, i)(paired[i, :CUT]) for i in (1, 2, 3)]

    back = back.reshape(NZ, NX, ROWS, BS)
    pick = lambda step: lax.dynamic_index_in_dim(back, turn_x(step), 1, keepdims=False)
    back_x = (pick(0) + across(pick(2))) + (x_up(pick(1)) + x_down(pick(-1)))
    back_x = back_x + flip("z", NZ, 1)(back_x)
    back_x, _ = lax.optimization_barrier((back_x, paired))
    for bit in (2, 4):
        back_x = back_x + flip("z", NZ, bit)(back_x)
    back_x, rest, _ = lax.optimization_barrier((back_x, paired[1:, CUT:], first_y))
    second_y = [shift("y", NY, i)(rest[i - 1]) for i in (1, 2, 3)]
    backs = [back_x, x_up(back_x), x_down(back_x), across(back_x)]
    turns = jnp.stack([part_of(jnp.int32(d)) for d in range(GROUPS)]).astype(jnp.int32)
    in_part = in_partial(near, turns, spread, backs)
    in_part, _ = lax.optimization_barrier((in_part, second_y))
    in_sum = in_part[NY:] + shift("core", NC, 1)(in_part[:NY])
    in_grad = in_sum[0]
    for step in (1, 2, 3):
        in_grad = in_grad + shift("y", NY, step)(in_sum[step])

    whole = pl.BlockSpec(memory_space=pltpu.VMEM)
    slots, out_grad = pl.pallas_call(
        final_kernel,
        in_specs=[pl.BlockSpec(memory_space=pltpu.SMEM)] + [whole] * (2 * NY - 1),
        out_specs=[whole, whole],
        out_shape=[
            jax.ShapeDtypeStruct((CAP, BS, BS), jnp.float32),
            jax.ShapeDtypeStruct((BS, FO_ROWS), jnp.float32),
        ],
        compiler_params=pltpu.CompilerParams(vmem_limit_bytes=50 * 1024 * 1024),
        name="slots",
    )(mine, paired, *first_y, *second_y)
    return hidden, slots, in_grad, out_grad


def solution(mesh):
    split = Mesh(mesh.devices.reshape(NY, NC, NZ, NX), ("y", "core", "z", "x"))
    dp, mp = ("y", "core"), ("z", "x")
    return jax.shard_map(
        per_device,
        mesh=split,
        in_specs=(
            P(dp + mp, None),
            P(mp, None, None, None),
            P(mp, None),
            P(mp, None, None),
            P(mp, None),
            P(None, mp),
            P(dp, mp),
        ),
        out_specs=(
            P(dp, mp),
            P(mp + dp, None, None),
            P(mp + dp, None),
            P(None, mp + dp),
        ),
        check_vma=False,
    )
```

```python
import functools

import jax
import jax.numpy as jnp
from jax import lax
from jax.experimental import pallas as pl
from jax.experimental.pallas import tpu as pltpu
from jax.sharding import Mesh
from jax.sharding import PartitionSpec as P

highest = lax.Precision.HIGHEST
BS = 128
ROWS = 16
NX, NZ, NY, NC = 4, 8, 4, 2
COLS = 12
PER_STEP = 2
KB = 8
RB = 96
CAP = 18
GROUPS = NY * NC
SLOT_ROWS = CAP * BS
FO_ROWS = COLS * BS // GROUPS
CODE_ROWS = SLOT_ROWS + FO_ROWS
PART_ROWS = CODE_ROWS + 32
FINE = 256.0


def shift(axis, size, step):
    pairs = [(i, (i + step) % size) for i in range(size)]
    return lambda value: lax.ppermute(value, axis, pairs)


def split_two(value):
    high = value.astype(jnp.bfloat16)
    low = (value - high.astype(jnp.float32)).astype(jnp.bfloat16)
    return high, low


def level_of(block):
    top = jnp.max(jnp.abs(block), axis=0, keepdims=True)
    return jnp.ceil(jnp.log2(jnp.maximum(top, 1e-30)) * FINE)


def encode(block, level):
    inverse = jnp.exp2(level * (-1.0 / FINE)) * 32700.0
    return jnp.floor(block * inverse + 0.5).astype(jnp.int32).astype(jnp.int16)


def decode(code, level):
    unit = jnp.exp2(level * (1.0 / FINE)) * (1.0 / 32700.0)
    return code.astype(jnp.int32).astype(jnp.float32) * unit


def main_kernel(
    counts, rows_ref, where_ref, place_ref, low_ref, weight_ref, factor_ref, up_ref, *rest
):
    arrays, rest = rest[: len(counts)], rest[len(counts) :]
    pieces = [ref.at[i] for ref, n in zip(arrays, counts) for i in range(n)]
    hidden_ref, send_ref, keep_ref, back_ref = rest[:4]
    tok, wide, low_two, codes, levels, sems = rest[4:]
    c = pl.program_id(0)
    tokens = NX * NZ * ROWS

    @pl.when(c == 0)
    def _():
        copies = [
            pltpu.make_async_copy(pieces[j], tok.at[place_ref[j]], sems.at[j])
            for j in range(NX * NZ)
        ]
        for copy in copies:
            copy.start()
        high, low = split_two(low_ref[...])
        low_two[:, :BS] = high
        low_two[:, BS:] = low
        wide[(KB + 1) * BS :, BS:] = jnp.zeros((BS, BS), jnp.bfloat16)
        back_ref[...] = jnp.zeros_like(back_ref)
        for copy in copies:
            copy.wait()

    for i in range(PER_STEP):
        col = c * PER_STEP + i
        here = slice(i * BS, (i + 1) * BS)
        for k in range(KB):
            high, low = split_two(weight_ref[i, k])
            wide[k * BS : (k + 1) * BS, :BS] = high
            wide[k * BS : (k + 1) * BS, BS:] = low
        f_high, f_low = split_two(factor_ref[:, here])
        wide[KB * BS : (KB + 1) * BS, :BS] = f_high
        wide[KB * BS : (KB + 1) * BS, BS:] = f_low
        wide[(KB + 1) * BS :, :BS] = f_high

        panel = jnp.concatenate(
            [tok[:, rows_ref[col * KB + k]].reshape(tokens, BS) for k in range(KB)]
            + [low_two[...]],
            axis=1,
        )
        both = jnp.dot(panel, wide[...], preferred_element_type=jnp.float32)
        v = both[:, :BS] + both[:, BS:]
        root = 0.7978845608028654
        square = v * v
        t = jnp.tanh(root * v * (1.0 + 0.044715 * square))
        half = 0.5 * (1.0 + t)
        hidden_ref[:, here] = (v * half).astype(jnp.bfloat16)
        slope = half + 0.5 * root * v * (1.0 - t * t) * (1.0 + 3.0 * 0.044715 * square)
        grad = up_ref[:, here].astype(jnp.float32) * slope

        g_high, g_low = split_two(grad)
        g_two = jnp.concatenate([g_high, g_low], axis=1)
        f_two = jnp.concatenate(
            [
                jnp.concatenate([f_high, f_high], axis=1),
                jnp.concatenate([f_low, jnp.zeros_like(f_low)], axis=1),
            ],
            axis=0,
        )
        back = lax.dot_general(
            g_two, f_two, (((1,), (1,)), ((), ())), preferred_element_type=jnp.float32
        )
        back_ref[...] += back[:, :BS] + back[:, BS:]

        grad_t = grad.T
        t_high, t_low = split_two(grad_t)
        gt_two = jnp.concatenate([t_high, t_low], axis=0)
        product = jnp.dot(gt_two, panel, preferred_element_type=jnp.float32)
        product = product[:BS] + product[BS:]
        for k in range(KB):
            block = product[:, k * BS : (k + 1) * BS]
            level = level_of(block)
            part = where_ref[0, col * KB + k]
            slot = where_ref[1, col * KB + k]
            codes[part, pl.ds(pl.multiple_of(slot * BS, BS), BS)] = encode(block, level)
            levels[part, pl.ds(slot, 1)] = level
        outer = product[:, KB * BS : (KB + 1) * BS] + product[:, (KB + 1) * BS :]
        for h in range(2):
            block = outer[h * 64 : (h + 1) * 64]
            level = level_of(block)
            part = where_ref[2, col * 2 + h]
            slot = where_ref[3, col * 2 + h]
            start = pl.multiple_of(SLOT_ROWS + slot * 64, 64)
            codes[part, pl.ds(start, 64)] = encode(block, level)
            levels[part, pl.ds(CAP + slot, 1)] = level

    @pl.when(c == COLS // PER_STEP - 1)
    def _():
        for part in range(2 * NY):
            codes[part, CODE_ROWS:] = levels[part].astype(jnp.int32).astype(jnp.int16)
        send = pltpu.make_async_copy(codes.at[pl.ds(0, NY)], send_ref, sems.at[0])
        keep = pltpu.make_async_copy(codes.at[pl.ds(NY, NY)], keep_ref, sems.at[1])
        send.start()
        keep.start()
        send.wait()
        keep.wait()


def blocks_of():
    spans = [(s * BS, BS, s) for s in range(CAP)]
    return spans + [(SLOT_ROWS + h * 64, 64, CAP + h) for h in range(FO_ROWS // 64)]


def pair_kernel(keep_ref, got_ref, out_ref):
    keep_levels = keep_ref[0, CODE_ROWS:].astype(jnp.int32).astype(jnp.float32)
    got_levels = got_ref[0, CODE_ROWS:].astype(jnp.int32).astype(jnp.float32)
    fresh = []
    for start, size, index in blocks_of():
        span = slice(start, start + size)
        total = decode(keep_ref[0, span], keep_levels[index : index + 1])
        total += decode(got_ref[0, span], got_levels[index : index + 1])
        level = level_of(total)
        out_ref[0, span] = encode(total, level)
        fresh.append(level)
    fresh.append(jnp.zeros((32 - len(fresh), BS), jnp.float32))
    fresh = jnp.concatenate(fresh, axis=0)
    out_ref[0, CODE_ROWS:] = fresh.astype(jnp.int32).astype(jnp.int16)


def final_kernel(count_ref, own_ref, *refs):
    parts, (slots_ref, outer_ref) = refs[: NY - 1], refs[NY - 1 :]
    tails = [own_ref[0, CODE_ROWS:]] + [r[CODE_ROWS:] for r in parts]
    levels = [t.astype(jnp.int32).astype(jnp.float32) for t in tails]
    count = count_ref[0]
    for start, size, index in blocks_of():
        total = decode(own_ref[0, start : start + size], levels[0][index : index + 1])
        for i in range(NY - 1):
            code = parts[i][start : start + size]
            total += decode(code, levels[i + 1][index : index + 1])
        if index < CAP:
            slots_ref[index] = jnp.where(index < count, total.T, 0.0)
        else:
            h = index - CAP
            outer_ref[:, h * 64 : (h + 1) * 64] = total.T


def in_kernel(cols_ref, back_ref, out_ref):
    total = NZ * NX * ROWS
    high, low = split_two(back_ref[...].reshape(total, BS).T)
    two = jnp.concatenate([high, low], axis=0)
    panel = jnp.concatenate(
        [cols_ref[:, j].reshape(total, BS) for j in range(cols_ref.shape[1])], axis=1
    )
    both = jnp.dot(two, panel, preferred_element_type=jnp.float32)
    out_ref[...] = (both[:BS] + both[BS:]).T.reshape(out_ref.shape)


def in_partial(cols, back_all):
    whole = pl.BlockSpec(memory_space=pltpu.VMEM)
    size = cols.shape[1] * BS // GROUPS
    return pl.pallas_call(
        in_kernel,
        in_specs=[whole, whole],
        out_specs=whole,
        out_shape=jax.ShapeDtypeStruct((GROUPS, size, BS), jnp.float32),
        compiler_params=pltpu.CompilerParams(vmem_limit_bytes=30 * 1024 * 1024),
        name="into",
    )(cols, back_all)


def gather_tokens(own):
    z_up, z_down = shift("z", NZ, 1), shift("z", NZ, -1)
    x_up, x_down = shift("x", NX, 1), shift("x", NX, -1)
    across = shift("x", NX, 2)
    held = {(0, 0): own[None]}
    held[0, 2] = across(own[None])
    for b in (0, 2):
        for a in (1, 2, 3):
            held[-a, b] = z_up(held[1 - a, b])
            held[a, b] = z_down(held[a - 1, b])
    held[4, 0] = z_up(held[-3, 0])
    held[4, 2] = z_down(held[3, 2])
    for a in (0, -1, 1, -2, 2, -3, 3, 4):
        for b, move in ((-1, x_up), (1, x_down)):
            if (a, b) in ((1, 1), (-1, -1)):
                held[a, b] = (z_down if a > 0 else z_up)(held[0, b])
            else:
                held[a, b] = move(held[a, 0])
    return list(held.values()), [[key] for key in held]


def per_device(tokens, block_weights, block_rows, block_owners, factor_in, factor_out, upstream):
    own = jnp.transpose(tokens.reshape(ROWS, RB, BS), (1, 0, 2))
    span = NX * NZ
    per = RB // span
    plane = ("z", "x")
    arrays, keys = gather_tokens(own)
    spread = lax.all_to_all(own.reshape(span, per, ROWS, BS), plane, 0, 0)
    factor = factor_in.reshape(per, BS, BS)
    partial = jnp.einsum(
        "sbtf,bfr->str", spread.astype(jnp.float32), factor, precision=highest
    )
    low_own = jnp.sum(lax.all_to_all(partial, plane, 0, 0), axis=0)
    low = lax.all_to_all(jnp.broadcast_to(low_own[None], (span, ROWS, BS)), plane, 0, 0)
    z, x = lax.axis_index("z"), lax.axis_index("x")
    y, core = lax.axis_index("y"), lax.axis_index("core")
    place = [((z + a) % NZ) * NX + (x + b) % NX for group in keys for a, b in group]
    place = jnp.stack(place).astype(jnp.int32)
    low = low.reshape(span * ROWS, BS)

    owners = block_owners.reshape(-1)
    count_all = owners.shape[0]
    marks = (owners[:, None] == jnp.arange(GROUPS, dtype=jnp.int32)[None, :]).astype(jnp.int32)
    before = (
        jnp.arange(count_all, dtype=jnp.int32)[:, None]
        > jnp.arange(count_all, dtype=jnp.int32)[None, :]
    ) & (owners[:, None] == owners[None, :])
    rank = jnp.sum(before.astype(jnp.int32), axis=1)

    def part_of(owner):
        turn = (owner // NC - y) % NY
        return turn + jnp.where(owner % NC == core, NY, 0)

    halves = jnp.arange(2 * COLS, dtype=jnp.int32)
    per_owner = FO_ROWS // 64
    pad = count_all - 2 * COLS
    where = jnp.stack(
        [
            part_of(owners),
            rank,
            jnp.pad(part_of(halves // per_owner), (0, pad)),
            jnp.pad(halves % per_owner, (0, pad)),
        ]
    ).astype(jnp.int32)
    counts = jnp.sum(marks, axis=0)
    mine = jnp.sum(
        jnp.where(jnp.arange(GROUPS) == y * NC + core, counts, 0), dtype=jnp.int32
    ).reshape(1)

    total = span * ROWS
    anywhere = pl.BlockSpec(memory_space=pl.ANY)
    hidden, send, keep, back = pl.pallas_call(
        functools.partial(main_kernel, [len(g) for g in keys]),
        grid_spec=pltpu.PrefetchScalarGridSpec(
            num_scalar_prefetch=3,
            grid=(COLS // PER_STEP,),
            in_specs=[
                pl.BlockSpec((total, BS), lambda c, *_: (0, 0)),
                pl.BlockSpec((PER_STEP, KB, BS, BS), lambda c, *_: (c, 0, 0, 0)),
                pl.BlockSpec((BS, PER_STEP * BS), lambda c, *_: (0, c)),
                pl.BlockSpec((total, PER_STEP * BS), lambda c, *_: (0, c)),
            ]
            + [anywhere] * len(arrays),
            out_specs=[
                pl.BlockSpec((total, PER_STEP * BS), lambda c, *_: (0, c)),
                anywhere,
                anywhere,
                pl.BlockSpec((total, BS), lambda c, *_: (0, 0)),
            ],
            scratch_shapes=[
                pltpu.VMEM((span, RB, ROWS, BS), jnp.bfloat16),
                pltpu.VMEM(((KB + 2) * BS, 2 * BS), jnp.bfloat16),
                pltpu.VMEM((total, 2 * BS), jnp.bfloat16),
                pltpu.VMEM((2 * NY, PART_ROWS, BS), jnp.int16),
                pltpu.VMEM((2 * NY, 32, BS), jnp.float32),
                pltpu.SemaphoreType.DMA((span,)),
            ],
        ),
        out_shape=[
            jax.ShapeDtypeStruct((total, COLS * BS), jnp.bfloat16),
            jax.ShapeDtypeStruct((NY, PART_ROWS, BS), jnp.int16),
            jax.ShapeDtypeStruct((NY, PART_ROWS, BS), jnp.int16),
            jax.ShapeDtypeStruct((total, BS), jnp.float32),
        ],
        compiler_params=pltpu.CompilerParams(vmem_limit_bytes=50 * 1024 * 1024),
        name="columns",
    )(
        block_rows.reshape(-1), where, place,
        low, block_weights, factor_out, upstream, *arrays,
    )

    got = shift("core", NC, 1)(send)
    back = lax.all_to_all(back.reshape(span, ROWS, BS), plane, 0, 0)
    got, _ = lax.optimization_barrier((got, back))
    paired = pl.pallas_call(
        pair_kernel,
        grid=(NY,),
        in_specs=[pl.BlockSpec((1, PART_ROWS, BS), lambda i: (i, 0, 0))] * 2,
        out_specs=pl.BlockSpec((1, PART_ROWS, BS), lambda i: (i, 0, 0)),
        out_shape=jax.ShapeDtypeStruct((NY, PART_ROWS, BS), jnp.int16),
        compiler_params=pltpu.CompilerParams(vmem_limit_bytes=50 * 1024 * 1024),
        name="pairs",
    )(keep, got)
    parts = [shift("y", NY, i)(paired[i]) for i in (1, 2, 3)]

    back, _ = lax.optimization_barrier((back, paired))
    back_own = jnp.sum(back, axis=0)
    back_all = lax.all_to_all(
        jnp.broadcast_to(back_own[None], (span, ROWS, BS)), plane, 0, 0
    )
    in_part = in_partial(spread, back_all)
    in_grad = jnp.sum(lax.all_to_all(in_part, ("y", "core"), 0, 0), axis=0)

    whole = pl.BlockSpec(memory_space=pltpu.VMEM)
    slots, out_grad = pl.pallas_call(
        final_kernel,
        in_specs=[pl.BlockSpec(memory_space=pltpu.SMEM)] + [whole] * NY,
        out_specs=[whole, whole],
        out_shape=[
            jax.ShapeDtypeStruct((CAP, BS, BS), jnp.float32),
            jax.ShapeDtypeStruct((BS, FO_ROWS), jnp.float32),
        ],
        compiler_params=pltpu.CompilerParams(vmem_limit_bytes=50 * 1024 * 1024),
        name="slots",
    )(mine, paired, *parts)
    return hidden, slots, in_grad, out_grad


def solution(mesh):
    split = Mesh(mesh.devices.reshape(NY, NC, NZ, NX), ("y", "core", "z", "x"))
    dp, mp = ("y", "core"), ("z", "x")
    return jax.shard_map(
        per_device,
        mesh=split,
        in_specs=(
            P(dp + mp, None),
            P(mp, None, None, None),
            P(mp, None),
            P(mp, None, None),
            P(mp, None),
            P(None, mp),
            P(dp, mp),
        ),
        out_specs=(
            P(dp, mp),
            P(mp + dp, None, None),
            P(mp + dp, None),
            P(None, mp + dp),
        ),
        check_vma=False,
    )
```

```python
import functools

import jax
import jax.numpy as jnp
from jax import lax
from jax.experimental import pallas as pl
from jax.experimental.pallas import tpu as pltpu
from jax.sharding import Mesh
from jax.sharding import PartitionSpec as P

highest = lax.Precision.HIGHEST
BS = 128
ROWS = 16
NX, NZ, NY, NC = 4, 8, 4, 2
COLS = 12
PER_STEP = 2
KB = 8
RB = 96
CAP = 18
GROUPS = NY * NC
SLOT_ROWS = CAP * BS
FO_ROWS = COLS * BS // GROUPS
CODE_ROWS = SLOT_ROWS + FO_ROWS
PART_ROWS = CODE_ROWS + 32
FINE = 256.0


def shift(axis, size, step):
    pairs = [(i, (i + step) % size) for i in range(size)]
    return lambda value: lax.ppermute(value, axis, pairs)


def split_two(value):
    high = value.astype(jnp.bfloat16)
    low = (value - high.astype(jnp.float32)).astype(jnp.bfloat16)
    return high, low


def level_of(block):
    top = jnp.max(jnp.abs(block), axis=0, keepdims=True)
    return jnp.ceil(jnp.log2(jnp.maximum(top, 1e-30)) * FINE)


def encode(block, level):
    inverse = jnp.exp2(level * (-1.0 / FINE)) * 32700.0
    return jnp.floor(block * inverse + 0.5).astype(jnp.int32).astype(jnp.int16)


def decode(code, level):
    unit = jnp.exp2(level * (1.0 / FINE)) * (1.0 / 32700.0)
    return code.astype(jnp.int32).astype(jnp.float32) * unit


def main_kernel(
    counts, rows_ref, where_ref, place_ref, low_ref, weight_ref, factor_ref, up_ref, *rest
):
    arrays, rest = rest[: len(counts)], rest[len(counts) :]
    pieces = [ref.at[i] for ref, n in zip(arrays, counts) for i in range(n)]
    hidden_ref, send_ref, keep_ref, back_ref = rest[:4]
    tok, wide, low_two, codes, levels, sems = rest[4:]
    c = pl.program_id(0)
    tokens = NX * NZ * ROWS

    @pl.when(c == 0)
    def _():
        copies = [
            pltpu.make_async_copy(pieces[j], tok.at[place_ref[j]], sems.at[j])
            for j in range(NX * NZ)
        ]
        for copy in copies:
            copy.start()
        high, low = split_two(low_ref[...])
        low_two[:, :BS] = high
        low_two[:, BS:] = low
        wide[(KB + 1) * BS :, BS:] = jnp.zeros((BS, BS), jnp.bfloat16)
        back_ref[...] = jnp.zeros_like(back_ref)
        for copy in copies:
            copy.wait()

    for i in range(PER_STEP):
        col = c * PER_STEP + i
        here = slice(i * BS, (i + 1) * BS)
        for k in range(KB):
            high, low = split_two(weight_ref[i, k])
            wide[k * BS : (k + 1) * BS, :BS] = high
            wide[k * BS : (k + 1) * BS, BS:] = low
        f_high, f_low = split_two(factor_ref[:, here])
        wide[KB * BS : (KB + 1) * BS, :BS] = f_high
        wide[KB * BS : (KB + 1) * BS, BS:] = f_low
        wide[(KB + 1) * BS :, :BS] = f_high

        panel = jnp.concatenate(
            [tok[:, rows_ref[col * KB + k]].reshape(tokens, BS) for k in range(KB)]
            + [low_two[...]],
            axis=1,
        )
        both = jnp.dot(panel, wide[...], preferred_element_type=jnp.float32)
        v = both[:, :BS] + both[:, BS:]
        root = 0.7978845608028654
        square = v * v
        t = jnp.tanh(root * v * (1.0 + 0.044715 * square))
        half = 0.5 * (1.0 + t)
        hidden_ref[:, here] = (v * half).astype(jnp.bfloat16)
        slope = half + 0.5 * root * v * (1.0 - t * t) * (1.0 + 3.0 * 0.044715 * square)
        grad = up_ref[:, here].astype(jnp.float32) * slope

        g_high, g_low = split_two(grad)
        g_two = jnp.concatenate([g_high, g_low], axis=1)
        f_two = jnp.concatenate(
            [
                jnp.concatenate([f_high, f_high], axis=1),
                jnp.concatenate([f_low, jnp.zeros_like(f_low)], axis=1),
            ],
            axis=0,
        )
        back = lax.dot_general(
            g_two, f_two, (((1,), (1,)), ((), ())), preferred_element_type=jnp.float32
        )
        back_ref[...] += back[:, :BS] + back[:, BS:]

        grad_t = grad.T
        t_high, t_low = split_two(grad_t)
        gt_two = jnp.concatenate([t_high, t_low], axis=0)
        product = jnp.dot(gt_two, panel, preferred_element_type=jnp.float32)
        product = product[:BS] + product[BS:]
        for k in range(KB):
            block = product[:, k * BS : (k + 1) * BS]
            level = level_of(block)
            part = where_ref[0, col * KB + k]
            slot = where_ref[1, col * KB + k]
            codes[part, pl.ds(pl.multiple_of(slot * BS, BS), BS)] = encode(block, level)
            levels[part, pl.ds(slot, 1)] = level
        outer = product[:, KB * BS : (KB + 1) * BS] + product[:, (KB + 1) * BS :]
        for h in range(2):
            block = outer[h * 64 : (h + 1) * 64]
            level = level_of(block)
            part = where_ref[2, col * 2 + h]
            slot = where_ref[3, col * 2 + h]
            start = pl.multiple_of(SLOT_ROWS + slot * 64, 64)
            codes[part, pl.ds(start, 64)] = encode(block, level)
            levels[part, pl.ds(CAP + slot, 1)] = level

    @pl.when(c == COLS // PER_STEP - 1)
    def _():
        for part in range(2 * NY):
            codes[part, CODE_ROWS:] = levels[part].astype(jnp.int32).astype(jnp.int16)
        send = pltpu.make_async_copy(codes.at[pl.ds(0, NY)], send_ref, sems.at[0])
        keep = pltpu.make_async_copy(codes.at[pl.ds(NY, NY)], keep_ref, sems.at[1])
        send.start()
        keep.start()
        send.wait()
        keep.wait()


def blocks_of():
    spans = [(s * BS, BS, s) for s in range(CAP)]
    return spans + [(SLOT_ROWS + h * 64, 64, CAP + h) for h in range(FO_ROWS // 64)]


def pair_kernel(keep_ref, got_ref, out_ref):
    keep_levels = keep_ref[0, CODE_ROWS:].astype(jnp.int32).astype(jnp.float32)
    got_levels = got_ref[0, CODE_ROWS:].astype(jnp.int32).astype(jnp.float32)
    fresh = []
    for start, size, index in blocks_of():
        span = slice(start, start + size)
        total = decode(keep_ref[0, span], keep_levels[index : index + 1])
        total += decode(got_ref[0, span], got_levels[index : index + 1])
        level = level_of(total)
        out_ref[0, span] = encode(total, level)
        fresh.append(level)
    fresh.append(jnp.zeros((32 - len(fresh), BS), jnp.float32))
    fresh = jnp.concatenate(fresh, axis=0)
    out_ref[0, CODE_ROWS:] = fresh.astype(jnp.int32).astype(jnp.int16)


def final_kernel(count_ref, own_ref, *refs):
    parts, (slots_ref, outer_ref) = refs[: NY - 1], refs[NY - 1 :]
    tails = [own_ref[0, CODE_ROWS:]] + [r[CODE_ROWS:] for r in parts]
    levels = [t.astype(jnp.int32).astype(jnp.float32) for t in tails]
    count = count_ref[0]
    for start, size, index in blocks_of():
        total = decode(own_ref[0, start : start + size], levels[0][index : index + 1])
        for i in range(NY - 1):
            code = parts[i][start : start + size]
            total += decode(code, levels[i + 1][index : index + 1])
        if index < CAP:
            slots_ref[index] = jnp.where(index < count, total.T, 0.0)
        else:
            h = index - CAP
            outer_ref[:, h * 64 : (h + 1) * 64] = total.T


def in_kernel(cols_ref, back_ref, out_ref):
    total = NZ * NX * ROWS
    high, low = split_two(back_ref[...].reshape(total, BS).T)
    two = jnp.concatenate([high, low], axis=0)
    panel = jnp.concatenate(
        [cols_ref[:, j].reshape(total, BS) for j in range(cols_ref.shape[1])], axis=1
    )
    both = jnp.dot(two, panel, preferred_element_type=jnp.float32)
    out_ref[...] = (both[:BS] + both[BS:]).T.reshape(out_ref.shape)


def in_partial(cols, back_all):
    whole = pl.BlockSpec(memory_space=pltpu.VMEM)
    size = cols.shape[1] * BS // GROUPS
    return pl.pallas_call(
        in_kernel,
        in_specs=[whole, whole],
        out_specs=whole,
        out_shape=jax.ShapeDtypeStruct((GROUPS, size, BS), jnp.float32),
        compiler_params=pltpu.CompilerParams(vmem_limit_bytes=30 * 1024 * 1024),
        name="into",
    )(cols, back_all)


def gather_tokens(own):
    z_up, z_down = shift("z", NZ, 1), shift("z", NZ, -1)
    x_up, x_down = shift("x", NX, 1), shift("x", NX, -1)
    across = shift("x", NX, 2)
    held = {(0, 0): own[None]}
    held[0, 2] = across(own[None])
    for b in (0, 2):
        for a in (1, 2, 3):
            held[-a, b] = z_up(held[1 - a, b])
            held[a, b] = z_down(held[a - 1, b])
    held[4, 0] = z_up(held[-3, 0])
    held[4, 2] = z_down(held[3, 2])
    for a in (0, -1, 1, -2, 2, -3, 3, 4):
        for b, move in ((-1, x_up), (1, x_down)):
            if (a, b) in ((1, 1), (-1, -1)):
                held[a, b] = (z_down if a > 0 else z_up)(held[0, b])
            else:
                held[a, b] = move(held[a, 0])
    return list(held.values()), [[key] for key in held]


def per_device(tokens, block_weights, block_rows, block_owners, factor_in, factor_out, upstream):
    own = jnp.transpose(tokens.reshape(ROWS, RB, BS), (1, 0, 2))
    span = NX * NZ
    per = RB // span
    plane = ("z", "x")
    arrays, keys = gather_tokens(own)
    spread = lax.all_to_all(own.reshape(span, per, ROWS, BS), plane, 0, 0)
    factor = factor_in.reshape(per, BS, BS)
    partial = jnp.einsum(
        "sbtf,bfr->str", spread.astype(jnp.float32), factor, precision=highest
    )
    low_own = jnp.sum(lax.all_to_all(partial, plane, 0, 0), axis=0)
    low = lax.all_to_all(jnp.broadcast_to(low_own[None], (span, ROWS, BS)), plane, 0, 0)
    z, x = lax.axis_index("z"), lax.axis_index("x")
    y, core = lax.axis_index("y"), lax.axis_index("core")
    place = [((z + a) % NZ) * NX + (x + b) % NX for group in keys for a, b in group]
    place = jnp.stack(place).astype(jnp.int32)
    low = low.reshape(span * ROWS, BS)

    owners = block_owners.reshape(-1)
    count_all = owners.shape[0]
    marks = (owners[:, None] == jnp.arange(GROUPS, dtype=jnp.int32)[None, :]).astype(jnp.int32)
    before = (
        jnp.arange(count_all, dtype=jnp.int32)[:, None]
        > jnp.arange(count_all, dtype=jnp.int32)[None, :]
    ) & (owners[:, None] == owners[None, :])
    rank = jnp.sum(before.astype(jnp.int32), axis=1)

    def part_of(owner):
        turn = (owner // NC - y) % NY
        return turn + jnp.where(owner % NC == core, NY, 0)

    halves = jnp.arange(2 * COLS, dtype=jnp.int32)
    per_owner = FO_ROWS // 64
    pad = count_all - 2 * COLS
    where = jnp.stack(
        [
            part_of(owners),
            rank,
            jnp.pad(part_of(halves // per_owner), (0, pad)),
            jnp.pad(halves % per_owner, (0, pad)),
        ]
    ).astype(jnp.int32)
    counts = jnp.sum(marks, axis=0)
    mine = jnp.sum(
        jnp.where(jnp.arange(GROUPS) == y * NC + core, counts, 0), dtype=jnp.int32
    ).reshape(1)

    total = span * ROWS
    anywhere = pl.BlockSpec(memory_space=pl.ANY)
    hidden, send, keep, back = pl.pallas_call(
        functools.partial(main_kernel, [len(g) for g in keys]),
        grid_spec=pltpu.PrefetchScalarGridSpec(
            num_scalar_prefetch=3,
            grid=(COLS // PER_STEP,),
            in_specs=[
                pl.BlockSpec((total, BS), lambda c, *_: (0, 0)),
                pl.BlockSpec((PER_STEP, KB, BS, BS), lambda c, *_: (c, 0, 0, 0)),
                pl.BlockSpec((BS, PER_STEP * BS), lambda c, *_: (0, c)),
                pl.BlockSpec((total, PER_STEP * BS), lambda c, *_: (0, c)),
            ]
            + [anywhere] * len(arrays),
            out_specs=[
                pl.BlockSpec((total, PER_STEP * BS), lambda c, *_: (0, c)),
                anywhere,
                anywhere,
                pl.BlockSpec((total, BS), lambda c, *_: (0, 0)),
            ],
            scratch_shapes=[
                pltpu.VMEM((span, RB, ROWS, BS), jnp.bfloat16),
                pltpu.VMEM(((KB + 2) * BS, 2 * BS), jnp.bfloat16),
                pltpu.VMEM((total, 2 * BS), jnp.bfloat16),
                pltpu.VMEM((2 * NY, PART_ROWS, BS), jnp.int16),
                pltpu.VMEM((2 * NY, 32, BS), jnp.float32),
                pltpu.SemaphoreType.DMA((span,)),
            ],
        ),
        out_shape=[
            jax.ShapeDtypeStruct((total, COLS * BS), jnp.bfloat16),
            jax.ShapeDtypeStruct((NY, PART_ROWS, BS), jnp.int16),
            jax.ShapeDtypeStruct((NY, PART_ROWS, BS), jnp.int16),
            jax.ShapeDtypeStruct((total, BS), jnp.float32),
        ],
        compiler_params=pltpu.CompilerParams(vmem_limit_bytes=50 * 1024 * 1024),
        name="columns",
    )(
        block_rows.reshape(-1), where, place,
        low, block_weights, factor_out, upstream, *arrays,
    )

    got = shift("core", NC, 1)(send)
    back = lax.all_to_all(back.reshape(span, ROWS, BS), plane, 0, 0)
    paired = pl.pallas_call(
        pair_kernel,
        grid=(NY,),
        in_specs=[pl.BlockSpec((1, PART_ROWS, BS), lambda i: (i, 0, 0))] * 2,
        out_specs=pl.BlockSpec((1, PART_ROWS, BS), lambda i: (i, 0, 0)),
        out_shape=jax.ShapeDtypeStruct((NY, PART_ROWS, BS), jnp.int16),
        compiler_params=pltpu.CompilerParams(vmem_limit_bytes=50 * 1024 * 1024),
        name="pairs",
    )(keep, got)
    outward = [paired[i] for i in (1, 2, 3)]
    parts = [shift("y", NY, i)(outward[i - 1]) for i in (1, 2, 3)]

    back, _ = lax.optimization_barrier((back, outward))
    back_own = jnp.sum(back, axis=0)
    back_all = lax.all_to_all(
        jnp.broadcast_to(back_own[None], (span, ROWS, BS)), plane, 0, 0
    )
    in_part = in_partial(spread, back_all)
    in_grad = jnp.sum(lax.all_to_all(in_part, ("y", "core"), 0, 0), axis=0)

    whole = pl.BlockSpec(memory_space=pltpu.VMEM)
    slots, out_grad = pl.pallas_call(
        final_kernel,
        in_specs=[pl.BlockSpec(memory_space=pltpu.SMEM)] + [whole] * NY,
        out_specs=[whole, whole],
        out_shape=[
            jax.ShapeDtypeStruct((CAP, BS, BS), jnp.float32),
            jax.ShapeDtypeStruct((BS, FO_ROWS), jnp.float32),
        ],
        compiler_params=pltpu.CompilerParams(vmem_limit_bytes=50 * 1024 * 1024),
        name="slots",
    )(mine, paired, *parts)
    return hidden, slots, in_grad, out_grad


def solution(mesh):
    split = Mesh(mesh.devices.reshape(NY, NC, NZ, NX), ("y", "core", "z", "x"))
    dp, mp = ("y", "core"), ("z", "x")
    return jax.shard_map(
        per_device,
        mesh=split,
        in_specs=(
            P(dp + mp, None),
            P(mp, None, None, None),
            P(mp, None),
            P(mp, None, None),
            P(mp, None),
            P(None, mp),
            P(dp, mp),
        ),
        out_specs=(
            P(dp, mp),
            P(mp + dp, None, None),
            P(mp + dp, None),
            P(None, mp + dp),
        ),
        check_vma=False,
    )
```

```python
import functools

import jax
import jax.numpy as jnp
from jax import lax
from jax.experimental import pallas as pl
from jax.experimental.pallas import tpu as pltpu
from jax.sharding import Mesh
from jax.sharding import PartitionSpec as P

highest = lax.Precision.HIGHEST
BS = 128
ROWS = 16
NX, NZ, NY, NC = 4, 8, 4, 2
COLS = 12
PER_STEP = 2
KB = 8
RB = 96
CAP = 18
GROUPS = NY * NC
SLOT_ROWS = CAP * BS
FO_ROWS = COLS * BS // GROUPS
CODE_ROWS = SLOT_ROWS + FO_ROWS
PART_ROWS = CODE_ROWS + 32
FINE = 256.0
CUT = 10 * BS


def shift(axis, size, step):
    pairs = [(i, (i + step) % size) for i in range(size)]
    return lambda value: lax.ppermute(value, axis, pairs)


def split_two(value):
    high = value.astype(jnp.bfloat16)
    low = (value - high.astype(jnp.float32)).astype(jnp.bfloat16)
    return high, low


def level_of(block):
    top = jnp.max(jnp.abs(block), axis=0, keepdims=True)
    return jnp.ceil(jnp.log2(jnp.maximum(top, 1e-30)) * FINE)


def encode(block, level):
    inverse = jnp.exp2(level * (-1.0 / FINE)) * 32700.0
    return jnp.floor(block * inverse + 0.5).astype(jnp.int32).astype(jnp.int16)


def decode(code, level):
    unit = jnp.exp2(level * (1.0 / FINE)) * (1.0 / 32700.0)
    return code.astype(jnp.int32).astype(jnp.float32) * unit


def main_kernel(
    counts, rows_ref, where_ref, place_ref, low_ref, weight_ref, factor_ref, up_ref, *rest
):
    arrays, rest = rest[: len(counts)], rest[len(counts) :]
    pieces = [ref.at[i] for ref, n in zip(arrays, counts) for i in range(n)]
    hidden_ref, send_ref, keep_ref, back_ref = rest[:4]
    tok, wide, low_two, codes, levels, sems = rest[4:]
    c = pl.program_id(0)
    tokens = NX * NZ * ROWS

    @pl.when(c == 0)
    def _():
        copies = [
            pltpu.make_async_copy(pieces[j], tok.at[place_ref[j]], sems.at[j])
            for j in range(NX * NZ)
        ]
        for copy in copies:
            copy.start()
        high, low = split_two(low_ref[...])
        low_two[:, :BS] = high
        low_two[:, BS:] = low
        wide[(KB + 1) * BS :, BS:] = jnp.zeros((BS, BS), jnp.bfloat16)
        back_ref[...] = jnp.zeros_like(back_ref)
        for copy in copies:
            copy.wait()

    for i in range(PER_STEP):
        col = c * PER_STEP + i
        here = slice(i * BS, (i + 1) * BS)
        for k in range(KB):
            high, low = split_two(weight_ref[i, k])
            wide[k * BS : (k + 1) * BS, :BS] = high
            wide[k * BS : (k + 1) * BS, BS:] = low
        f_high, f_low = split_two(factor_ref[:, here])
        wide[KB * BS : (KB + 1) * BS, :BS] = f_high
        wide[KB * BS : (KB + 1) * BS, BS:] = f_low
        wide[(KB + 1) * BS :, :BS] = f_high

        panel = jnp.concatenate(
            [tok[:, rows_ref[col * KB + k]].reshape(tokens, BS) for k in range(KB)]
            + [low_two[...]],
            axis=1,
        )
        both = jnp.dot(panel, wide[...], preferred_element_type=jnp.float32)
        v = both[:, :BS] + both[:, BS:]
        root = 0.7978845608028654
        square = v * v
        t = jnp.tanh(root * v * (1.0 + 0.044715 * square))
        half = 0.5 * (1.0 + t)
        hidden_ref[:, here] = (v * half).astype(jnp.bfloat16)
        slope = half + 0.5 * root * v * (1.0 - t * t) * (1.0 + 3.0 * 0.044715 * square)
        grad = up_ref[:, here].astype(jnp.float32) * slope

        g_high, g_low = split_two(grad)
        g_two = jnp.concatenate([g_high, g_low], axis=1)
        f_two = jnp.concatenate(
            [
                jnp.concatenate([f_high, f_high], axis=1),
                jnp.concatenate([f_low, jnp.zeros_like(f_low)], axis=1),
            ],
            axis=0,
        )
        back = lax.dot_general(
            g_two, f_two, (((1,), (1,)), ((), ())), preferred_element_type=jnp.float32
        )
        back_ref[...] += back[:, :BS] + back[:, BS:]

        grad_t = grad.T
        t_high, t_low = split_two(grad_t)
        gt_two = jnp.concatenate([t_high, t_low], axis=0)
        product = jnp.dot(gt_two, panel, preferred_element_type=jnp.float32)
        product = product[:BS] + product[BS:]
        for k in range(KB):
            block = product[:, k * BS : (k + 1) * BS]
            level = level_of(block)
            part = where_ref[0, col * KB + k]
            slot = where_ref[1, col * KB + k]
            codes[part, pl.ds(pl.multiple_of(slot * BS, BS), BS)] = encode(block, level)
            levels[part, pl.ds(slot, 1)] = level
        outer = product[:, KB * BS : (KB + 1) * BS] + product[:, (KB + 1) * BS :]
        for h in range(2):
            block = outer[h * 64 : (h + 1) * 64]
            level = level_of(block)
            part = where_ref[2, col * 2 + h]
            slot = where_ref[3, col * 2 + h]
            start = pl.multiple_of(SLOT_ROWS + slot * 64, 64)
            codes[part, pl.ds(start, 64)] = encode(block, level)
            levels[part, pl.ds(CAP + slot, 1)] = level

    @pl.when(c == COLS // PER_STEP - 1)
    def _():
        for part in range(2 * NY):
            codes[part, CODE_ROWS:] = levels[part].astype(jnp.int32).astype(jnp.int16)
        send = pltpu.make_async_copy(codes.at[pl.ds(0, NY)], send_ref, sems.at[0])
        keep = pltpu.make_async_copy(codes.at[pl.ds(NY, NY)], keep_ref, sems.at[1])
        send.start()
        keep.start()
        send.wait()
        keep.wait()


def blocks_of():
    spans = [(s * BS, BS, s) for s in range(CAP)]
    return spans + [(SLOT_ROWS + h * 64, 64, CAP + h) for h in range(FO_ROWS // 64)]


def pair_kernel(keep_ref, got_ref, out_ref):
    keep_levels = keep_ref[0, CODE_ROWS:].astype(jnp.int32).astype(jnp.float32)
    got_levels = got_ref[0, CODE_ROWS:].astype(jnp.int32).astype(jnp.float32)
    fresh = []
    for start, size, index in blocks_of():
        span = slice(start, start + size)
        total = decode(keep_ref[0, span], keep_levels[index : index + 1])
        total += decode(got_ref[0, span], got_levels[index : index + 1])
        level = level_of(total)
        out_ref[0, span] = encode(total, level)
        fresh.append(level)
    fresh.append(jnp.zeros((32 - len(fresh), BS), jnp.float32))
    fresh = jnp.concatenate(fresh, axis=0)
    out_ref[0, CODE_ROWS:] = fresh.astype(jnp.int32).astype(jnp.int16)


def levels_in(rows):
    return rows.astype(jnp.int32).astype(jnp.float32)


def relay_kernel(up_ref, down_ref, above_ref, below_ref, up_out, down_out):
    for own, got, out, first in (
        (up_ref, above_ref, up_out, True),
        (down_ref, below_ref, down_out, False),
    ):
        own_levels = levels_in(own[0, CODE_ROWS:])
        got_levels = levels_in(got[CUT:] if first else got[CODE_ROWS - CUT :])
        fresh = []
        for start, size, index in blocks_of():
            span = slice(start, start + size)
            level = own_levels[index : index + 1]
            if (start < CUT) == first:
                offset = start if first else start - CUT
                total = decode(own[0, span], level)
                total += decode(got[offset : offset + size], got_levels[index : index + 1])
                level = level_of(total)
                out[span] = encode(total, level)
            else:
                out[span] = own[0, span]
            fresh.append(level)
        fresh.append(jnp.zeros((32 - len(fresh), BS), jnp.float32))
        fresh = jnp.concatenate(fresh, axis=0)
        out[CODE_ROWS:] = fresh.astype(jnp.int32).astype(jnp.int16)


def relay(paired, above, below):
    one = lambda i: pl.BlockSpec((1, PART_ROWS, BS), lambda _: (i, 0, 0))
    flat = lambda rows: pl.BlockSpec((rows, BS), lambda _: (0, 0))
    return pl.pallas_call(
        relay_kernel,
        grid=(1,),
        in_specs=[one(1), one(3), flat(above.shape[0]), flat(below.shape[0])],
        out_specs=[flat(PART_ROWS)] * 2,
        out_shape=[jax.ShapeDtypeStruct((PART_ROWS, BS), jnp.int16)] * 2,
        compiler_params=pltpu.CompilerParams(vmem_limit_bytes=30 * 1024 * 1024),
        cost_estimate=pl.CostEstimate(
            flops=40_000_000, bytes_accessed=40_000_000, transcendentals=0
        ),
        name="relay",
    )(paired, paired, above, below)


def final_kernel(count_ref, own_ref, *refs):
    parts, (slots_ref, outer_ref) = refs[:2], refs[2:]
    levels = [levels_in(own_ref[0, CODE_ROWS:])] + [levels_in(r[CODE_ROWS:]) for r in parts]
    count = count_ref[0]
    for start, size, index in blocks_of():
        span = slice(start, start + size)
        total = decode(own_ref[0, span], levels[0][index : index + 1])
        for i in range(2):
            total += decode(parts[i][span], levels[i + 1][index : index + 1])
        if index < CAP:
            slots_ref[index] = jnp.where(index < count, total.T, 0.0)
        else:
            h = index - CAP
            outer_ref[:, h * 64 : (h + 1) * 64] = total.T


def in_kernel(cols_ref, back_ref, out_ref):
    total = NZ * NX * ROWS
    high, low = split_two(back_ref[...].reshape(total, BS).T)
    two = jnp.concatenate([high, low], axis=0)
    panel = jnp.concatenate(
        [cols_ref[:, j].reshape(total, BS) for j in range(cols_ref.shape[1])], axis=1
    )
    both = jnp.dot(two, panel, preferred_element_type=jnp.float32)
    out_ref[...] = (both[:BS] + both[BS:]).T.reshape(out_ref.shape)


def in_partial(cols, back_all):
    whole = pl.BlockSpec(memory_space=pltpu.VMEM)
    size = cols.shape[1] * BS // GROUPS
    return pl.pallas_call(
        in_kernel,
        in_specs=[whole, whole],
        out_specs=whole,
        out_shape=jax.ShapeDtypeStruct((GROUPS, size, BS), jnp.float32),
        compiler_params=pltpu.CompilerParams(vmem_limit_bytes=30 * 1024 * 1024),
        name="into",
    )(cols, back_all)


def gather_tokens(own):
    z_up, z_down = shift("z", NZ, 1), shift("z", NZ, -1)
    x_up, x_down = shift("x", NX, 1), shift("x", NX, -1)
    across = shift("x", NX, 2)
    held = {(0, 0): own[None]}
    held[0, 2] = across(own[None])
    for b in (0, 2):
        for a in (1, 2, 3):
            held[-a, b] = z_up(held[1 - a, b])
            held[a, b] = z_down(held[a - 1, b])
    held[4, 0] = z_up(held[-3, 0])
    held[4, 2] = z_down(held[3, 2])
    for a in (0, -1, 1, -2, 2, -3, 3, 4):
        for b, move in ((-1, x_up), (1, x_down)):
            if (a, b) in ((1, 1), (-1, -1)):
                held[a, b] = (z_down if a > 0 else z_up)(held[0, b])
            else:
                held[a, b] = move(held[a, 0])
    return list(held.values()), [[key] for key in held]


def per_device(tokens, block_weights, block_rows, block_owners, factor_in, factor_out, upstream):
    own = jnp.transpose(tokens.reshape(ROWS, RB, BS), (1, 0, 2))
    span = NX * NZ
    per = RB // span
    plane = ("z", "x")
    arrays, keys = gather_tokens(own)
    spread = lax.all_to_all(own.reshape(span, per, ROWS, BS), plane, 0, 0)
    factor = factor_in.reshape(per, BS, BS)
    partial = jnp.einsum(
        "sbtf,bfr->str", spread.astype(jnp.float32), factor, precision=highest
    )
    low_own = jnp.sum(lax.all_to_all(partial, plane, 0, 0), axis=0)
    low = lax.all_to_all(jnp.broadcast_to(low_own[None], (span, ROWS, BS)), plane, 0, 0)
    z, x = lax.axis_index("z"), lax.axis_index("x")
    y, core = lax.axis_index("y"), lax.axis_index("core")
    place = [((z + a) % NZ) * NX + (x + b) % NX for group in keys for a, b in group]
    place = jnp.stack(place).astype(jnp.int32)
    low = low.reshape(span * ROWS, BS)

    owners = block_owners.reshape(-1)
    count_all = owners.shape[0]
    marks = (owners[:, None] == jnp.arange(GROUPS, dtype=jnp.int32)[None, :]).astype(jnp.int32)
    before = (
        jnp.arange(count_all, dtype=jnp.int32)[:, None]
        > jnp.arange(count_all, dtype=jnp.int32)[None, :]
    ) & (owners[:, None] == owners[None, :])
    rank = jnp.sum(before.astype(jnp.int32), axis=1)

    def part_of(owner):
        turn = (owner // NC - y) % NY
        return turn + jnp.where(owner % NC == core, NY, 0)

    halves = jnp.arange(2 * COLS, dtype=jnp.int32)
    per_owner = FO_ROWS // 64
    pad = count_all - 2 * COLS
    where = jnp.stack(
        [
            part_of(owners),
            rank,
            jnp.pad(part_of(halves // per_owner), (0, pad)),
            jnp.pad(halves % per_owner, (0, pad)),
        ]
    ).astype(jnp.int32)
    counts = jnp.sum(marks, axis=0)
    mine = jnp.sum(
        jnp.where(jnp.arange(GROUPS) == y * NC + core, counts, 0), dtype=jnp.int32
    ).reshape(1)

    total = span * ROWS
    anywhere = pl.BlockSpec(memory_space=pl.ANY)
    hidden, send, keep, back = pl.pallas_call(
        functools.partial(main_kernel, [len(g) for g in keys]),
        grid_spec=pltpu.PrefetchScalarGridSpec(
            num_scalar_prefetch=3,
            grid=(COLS // PER_STEP,),
            in_specs=[
                pl.BlockSpec((total, BS), lambda c, *_: (0, 0)),
                pl.BlockSpec((PER_STEP, KB, BS, BS), lambda c, *_: (c, 0, 0, 0)),
                pl.BlockSpec((BS, PER_STEP * BS), lambda c, *_: (0, c)),
                pl.BlockSpec((total, PER_STEP * BS), lambda c, *_: (0, c)),
            ]
            + [anywhere] * len(arrays),
            out_specs=[
                pl.BlockSpec((total, PER_STEP * BS), lambda c, *_: (0, c)),
                anywhere,
                anywhere,
                pl.BlockSpec((total, BS), lambda c, *_: (0, 0)),
            ],
            scratch_shapes=[
                pltpu.VMEM((span, RB, ROWS, BS), jnp.bfloat16),
                pltpu.VMEM(((KB + 2) * BS, 2 * BS), jnp.bfloat16),
                pltpu.VMEM((total, 2 * BS), jnp.bfloat16),
                pltpu.VMEM((2 * NY, PART_ROWS, BS), jnp.int16),
                pltpu.VMEM((2 * NY, 32, BS), jnp.float32),
                pltpu.SemaphoreType.DMA((span,)),
            ],
        ),
        out_shape=[
            jax.ShapeDtypeStruct((total, COLS * BS), jnp.bfloat16),
            jax.ShapeDtypeStruct((NY, PART_ROWS, BS), jnp.int16),
            jax.ShapeDtypeStruct((NY, PART_ROWS, BS), jnp.int16),
            jax.ShapeDtypeStruct((total, BS), jnp.float32),
        ],
        compiler_params=pltpu.CompilerParams(vmem_limit_bytes=50 * 1024 * 1024),
        name="columns",
    )(
        block_rows.reshape(-1), where, place,
        low, block_weights, factor_out, upstream, *arrays,
    )

    got = shift("core", NC, 1)(send)
    back = lax.all_to_all(back.reshape(span, ROWS, BS), plane, 0, 0)
    paired = pl.pallas_call(
        pair_kernel,
        grid=(NY,),
        in_specs=[pl.BlockSpec((1, PART_ROWS, BS), lambda i: (i, 0, 0))] * 2,
        out_specs=pl.BlockSpec((1, PART_ROWS, BS), lambda i: (i, 0, 0)),
        out_shape=jax.ShapeDtypeStruct((NY, PART_ROWS, BS), jnp.int16),
        compiler_params=pltpu.CompilerParams(vmem_limit_bytes=50 * 1024 * 1024),
        name="pairs",
    )(keep, got)
    y_up, y_down = shift("y", NY, 1), shift("y", NY, -1)
    above = jnp.concatenate([paired[2, :CUT], paired[2, CODE_ROWS:]])
    below = paired[2, CUT:]
    parts = relay(paired, y_up(above), y_down(below))
    parts = [y_up(parts[0]), y_down(parts[1])]

    back, _ = lax.optimization_barrier((back, (above, below)))
    back_own = jnp.sum(back, axis=0)
    back_all = lax.all_to_all(
        jnp.broadcast_to(back_own[None], (span, ROWS, BS)), plane, 0, 0
    )
    in_part = in_partial(spread, back_all)
    in_grad = jnp.sum(lax.all_to_all(in_part, ("y", "core"), 0, 0), axis=0)

    whole = pl.BlockSpec(memory_space=pltpu.VMEM)
    slots, out_grad = pl.pallas_call(
        final_kernel,
        in_specs=[pl.BlockSpec(memory_space=pltpu.SMEM)] + [whole] * 3,
        out_specs=[whole, whole],
        out_shape=[
            jax.ShapeDtypeStruct((CAP, BS, BS), jnp.float32),
            jax.ShapeDtypeStruct((BS, FO_ROWS), jnp.float32),
        ],
        compiler_params=pltpu.CompilerParams(vmem_limit_bytes=50 * 1024 * 1024),
        cost_estimate=pl.CostEstimate(
            flops=10_000_000, bytes_accessed=16_000_000, transcendentals=0
        ),
        name="slots",
    )(mine, paired, *parts)
    return hidden, slots, in_grad, out_grad


def solution(mesh):
    split = Mesh(mesh.devices.reshape(NY, NC, NZ, NX), ("y", "core", "z", "x"))
    dp, mp = ("y", "core"), ("z", "x")
    return jax.shard_map(
        per_device,
        mesh=split,
        in_specs=(
            P(dp + mp, None),
            P(mp, None, None, None),
            P(mp, None),
            P(mp, None, None),
            P(mp, None),
            P(None, mp),
            P(dp, mp),
        ),
        out_specs=(
            P(dp, mp),
            P(mp + dp, None, None),
            P(mp + dp, None),
            P(None, mp + dp),
        ),
        check_vma=False,
    )
```

```python
import functools

import jax
import jax.numpy as jnp
from jax import lax
from jax.experimental import pallas as pl
from jax.experimental.pallas import tpu as pltpu
from jax.sharding import Mesh
from jax.sharding import PartitionSpec as P

highest = lax.Precision.HIGHEST
BS = 128
ROWS = 16
NX, NZ, NY, NC = 4, 8, 4, 2
COLS = 12
PER_STEP = 2
KB = 8
RB = 96
CAP = 18
GROUPS = NY * NC
SLOT_ROWS = CAP * BS
FO_ROWS = COLS * BS // GROUPS
CODE_ROWS = SLOT_ROWS + FO_ROWS
PART_ROWS = CODE_ROWS + 32
FINE = 256.0
CUT = 10 * BS


def shift(axis, size, step):
    pairs = [(i, (i + step) % size) for i in range(size)]
    return lambda value: lax.ppermute(value, axis, pairs)


def split_two(value):
    high = value.astype(jnp.bfloat16)
    low = (value - high.astype(jnp.float32)).astype(jnp.bfloat16)
    return high, low


def level_of(block):
    top = jnp.max(jnp.abs(block), axis=0, keepdims=True)
    return jnp.ceil(jnp.log2(jnp.maximum(top, 1e-30)) * FINE)


def encode(block, level):
    inverse = jnp.exp2(level * (-1.0 / FINE)) * 32700.0
    return jnp.floor(block * inverse + 0.5).astype(jnp.int32).astype(jnp.int16)


def decode(code, level):
    unit = jnp.exp2(level * (1.0 / FINE)) * (1.0 / 32700.0)
    return code.astype(jnp.int32).astype(jnp.float32) * unit


def main_kernel(
    counts, rows_ref, where_ref, place_ref, low_ref, weight_ref, factor_ref, up_ref, *rest
):
    arrays, rest = rest[: len(counts)], rest[len(counts) :]
    pieces = [ref.at[i] for ref, n in zip(arrays, counts) for i in range(n)]
    hidden_ref, send_ref, keep_ref, back_ref = rest[:4]
    tok, wide, low_two, codes, levels, sems = rest[4:]
    c = pl.program_id(0)
    tokens = NX * NZ * ROWS

    @pl.when(c == 0)
    def _():
        copies = [
            pltpu.make_async_copy(pieces[j], tok.at[place_ref[j]], sems.at[j])
            for j in range(NX * NZ)
        ]
        for copy in copies:
            copy.start()
        high, low = split_two(low_ref[...])
        low_two[:, :BS] = high
        low_two[:, BS:] = low
        wide[(KB + 1) * BS :, BS:] = jnp.zeros((BS, BS), jnp.bfloat16)
        back_ref[...] = jnp.zeros_like(back_ref)
        for copy in copies:
            copy.wait()

    for i in range(PER_STEP):
        col = c * PER_STEP + i
        here = slice(i * BS, (i + 1) * BS)
        for k in range(KB):
            high, low = split_two(weight_ref[i, k])
            wide[k * BS : (k + 1) * BS, :BS] = high
            wide[k * BS : (k + 1) * BS, BS:] = low
        f_high, f_low = split_two(factor_ref[:, here])
        wide[KB * BS : (KB + 1) * BS, :BS] = f_high
        wide[KB * BS : (KB + 1) * BS, BS:] = f_low
        wide[(KB + 1) * BS :, :BS] = f_high

        panel = jnp.concatenate(
            [tok[:, rows_ref[col * KB + k]].reshape(tokens, BS) for k in range(KB)]
            + [low_two[...]],
            axis=1,
        )
        both = jnp.dot(panel, wide[...], preferred_element_type=jnp.float32)
        v = both[:, :BS] + both[:, BS:]
        root = 0.7978845608028654
        square = v * v
        t = jnp.tanh(root * v * (1.0 + 0.044715 * square))
        half = 0.5 * (1.0 + t)
        hidden_ref[:, here] = (v * half).astype(jnp.bfloat16)
        slope = half + 0.5 * root * v * (1.0 - t * t) * (1.0 + 3.0 * 0.044715 * square)
        grad = up_ref[:, here].astype(jnp.float32) * slope

        g_high, g_low = split_two(grad)
        g_two = jnp.concatenate([g_high, g_low], axis=1)
        f_two = jnp.concatenate(
            [
                jnp.concatenate([f_high, f_high], axis=1),
                jnp.concatenate([f_low, jnp.zeros_like(f_low)], axis=1),
            ],
            axis=0,
        )
        back = lax.dot_general(
            g_two, f_two, (((1,), (1,)), ((), ())), preferred_element_type=jnp.float32
        )
        back_ref[...] += back[:, :BS] + back[:, BS:]

        grad_t = grad.T
        t_high, t_low = split_two(grad_t)
        gt_two = jnp.concatenate([t_high, t_low], axis=0)
        product = jnp.dot(gt_two, panel, preferred_element_type=jnp.float32)
        product = product[:BS] + product[BS:]
        for k in range(KB):
            block = product[:, k * BS : (k + 1) * BS]
            level = level_of(block)
            part = where_ref[0, col * KB + k]
            slot = where_ref[1, col * KB + k]
            codes[part, pl.ds(pl.multiple_of(slot * BS, BS), BS)] = encode(block, level)
            levels[part, pl.ds(slot, 1)] = level
        outer = product[:, KB * BS : (KB + 1) * BS] + product[:, (KB + 1) * BS :]
        for h in range(2):
            block = outer[h * 64 : (h + 1) * 64]
            level = level_of(block)
            part = where_ref[2, col * 2 + h]
            slot = where_ref[3, col * 2 + h]
            start = pl.multiple_of(SLOT_ROWS + slot * 64, 64)
            codes[part, pl.ds(start, 64)] = encode(block, level)
            levels[part, pl.ds(CAP + slot, 1)] = level

    @pl.when(c == COLS // PER_STEP - 1)
    def _():
        for part in range(2 * NY):
            codes[part, CODE_ROWS:] = levels[part].astype(jnp.int32).astype(jnp.int16)
        send = pltpu.make_async_copy(codes.at[pl.ds(0, NY)], send_ref, sems.at[0])
        keep = pltpu.make_async_copy(codes.at[pl.ds(NY, NY)], keep_ref, sems.at[1])
        send.start()
        keep.start()
        send.wait()
        keep.wait()


def blocks_of():
    spans = [(s * BS, BS, s) for s in range(CAP)]
    return spans + [(SLOT_ROWS + h * 64, 64, CAP + h) for h in range(FO_ROWS // 64)]


def pair_kernel(keep_ref, got_ref, out_ref):
    keep_levels = keep_ref[0, CODE_ROWS:].astype(jnp.int32).astype(jnp.float32)
    got_levels = got_ref[0, CODE_ROWS:].astype(jnp.int32).astype(jnp.float32)
    fresh = []
    for start, size, index in blocks_of():
        span = slice(start, start + size)
        total = decode(keep_ref[0, span], keep_levels[index : index + 1])
        total += decode(got_ref[0, span], got_levels[index : index + 1])
        level = level_of(total)
        out_ref[0, span] = encode(total, level)
        fresh.append(level)
    fresh.append(jnp.zeros((32 - len(fresh), BS), jnp.float32))
    fresh = jnp.concatenate(fresh, axis=0)
    out_ref[0, CODE_ROWS:] = fresh.astype(jnp.int32).astype(jnp.int16)


def levels_in(rows):
    return rows.astype(jnp.int32).astype(jnp.float32)


def relay_kernel(up_ref, down_ref, above_ref, below_ref, up_out, down_out):
    for own, got, out, first in (
        (up_ref, above_ref, up_out, True),
        (down_ref, below_ref, down_out, False),
    ):
        own_levels = levels_in(own[0, CODE_ROWS:])
        got_levels = levels_in(got[CUT:] if first else got[CODE_ROWS - CUT :])
        fresh = []
        for start, size, index in blocks_of():
            span = slice(start, start + size)
            level = own_levels[index : index + 1]
            if (start < CUT) == first:
                offset = start if first else start - CUT
                total = decode(own[0, span], level)
                total += decode(got[offset : offset + size], got_levels[index : index + 1])
                level = level_of(total)
                out[span] = encode(total, level)
            else:
                out[span] = own[0, span]
            fresh.append(level)
        fresh.append(jnp.zeros((32 - len(fresh), BS), jnp.float32))
        fresh = jnp.concatenate(fresh, axis=0)
        out[CODE_ROWS:] = fresh.astype(jnp.int32).astype(jnp.int16)


def relay(paired, above, below):
    one = lambda i: pl.BlockSpec((1, PART_ROWS, BS), lambda _: (i, 0, 0))
    flat = lambda rows: pl.BlockSpec((rows, BS), lambda _: (0, 0))
    return pl.pallas_call(
        relay_kernel,
        grid=(1,),
        in_specs=[one(1), one(3), flat(above.shape[0]), flat(below.shape[0])],
        out_specs=[flat(PART_ROWS)] * 2,
        out_shape=[jax.ShapeDtypeStruct((PART_ROWS, BS), jnp.int16)] * 2,
        compiler_params=pltpu.CompilerParams(vmem_limit_bytes=12 * 1024 * 1024),
        cost_estimate=pl.CostEstimate(
            flops=40_000_000, bytes_accessed=40_000_000, transcendentals=0
        ),
        name="relay",
    )(paired, paired, above, below)


def final_kernel(count_ref, own_ref, *refs):
    parts, (slots_ref, outer_ref) = refs[:2], refs[2:]
    levels = [levels_in(own_ref[0, CODE_ROWS:])] + [levels_in(r[CODE_ROWS:]) for r in parts]
    count = count_ref[0]
    for start, size, index in blocks_of():
        span = slice(start, start + size)
        total = decode(own_ref[0, span], levels[0][index : index + 1])
        for i in range(2):
            total += decode(parts[i][span], levels[i + 1][index : index + 1])
        if index < CAP:
            slots_ref[index] = jnp.where(index < count, total.T, 0.0)
        else:
            h = index - CAP
            outer_ref[:, h * 64 : (h + 1) * 64] = total.T


def in_kernel(cols_ref, back_ref, out_ref):
    total = NZ * NX * ROWS
    high, low = split_two(back_ref[...].reshape(total, BS).T)
    two = jnp.concatenate([high, low], axis=0)
    panel = jnp.concatenate(
        [cols_ref[:, j].reshape(total, BS) for j in range(cols_ref.shape[1])], axis=1
    )
    both = jnp.dot(two, panel, preferred_element_type=jnp.float32)
    out_ref[...] = (both[:BS] + both[BS:]).T.reshape(out_ref.shape)


def in_partial(cols, back_all):
    whole = pl.BlockSpec(memory_space=pltpu.VMEM)
    size = cols.shape[1] * BS // GROUPS
    return pl.pallas_call(
        in_kernel,
        in_specs=[whole, whole],
        out_specs=whole,
        out_shape=jax.ShapeDtypeStruct((GROUPS, size, BS), jnp.float32),
        compiler_params=pltpu.CompilerParams(vmem_limit_bytes=12 * 1024 * 1024),
        name="into",
    )(cols, back_all)


def gather_tokens(own):
    z_up, z_down = shift("z", NZ, 1), shift("z", NZ, -1)
    x_up, x_down = shift("x", NX, 1), shift("x", NX, -1)
    across = shift("x", NX, 2)
    held = {(0, 0): own[None]}
    held[0, 2] = across(own[None])
    for b in (0, 2):
        for a in (1, 2, 3):
            held[-a, b] = z_up(held[1 - a, b])
            held[a, b] = z_down(held[a - 1, b])
    held[4, 0] = z_up(held[-3, 0])
    held[4, 2] = z_down(held[3, 2])
    for a in (0, -1, 1, -2, 2, -3, 3, 4):
        for b, move in ((-1, x_up), (1, x_down)):
            if (a, b) in ((1, 1), (-1, -1)):
                held[a, b] = (z_down if a > 0 else z_up)(held[0, b])
            else:
                held[a, b] = move(held[a, 0])
    return list(held.values()), [[key] for key in held]


def per_device(tokens, block_weights, block_rows, block_owners, factor_in, factor_out, upstream):
    own = jnp.transpose(tokens.reshape(ROWS, RB, BS), (1, 0, 2))
    span = NX * NZ
    per = RB // span
    plane = ("z", "x")
    arrays, keys = gather_tokens(own)
    spread = lax.all_to_all(own.reshape(span, per, ROWS, BS), plane, 0, 0)
    factor = factor_in.reshape(per, BS, BS)
    partial = jnp.einsum(
        "sbtf,bfr->str", spread.astype(jnp.float32), factor, precision=highest
    )
    low_own = jnp.sum(lax.all_to_all(partial, plane, 0, 0), axis=0)
    low = lax.all_to_all(jnp.broadcast_to(low_own[None], (span, ROWS, BS)), plane, 0, 0)
    z, x = lax.axis_index("z"), lax.axis_index("x")
    y, core = lax.axis_index("y"), lax.axis_index("core")
    place = [((z + a) % NZ) * NX + (x + b) % NX for group in keys for a, b in group]
    place = jnp.stack(place).astype(jnp.int32)
    low = low.reshape(span * ROWS, BS)

    owners = block_owners.reshape(-1)
    count_all = owners.shape[0]
    marks = (owners[:, None] == jnp.arange(GROUPS, dtype=jnp.int32)[None, :]).astype(jnp.int32)
    before = (
        jnp.arange(count_all, dtype=jnp.int32)[:, None]
        > jnp.arange(count_all, dtype=jnp.int32)[None, :]
    ) & (owners[:, None] == owners[None, :])
    rank = jnp.sum(before.astype(jnp.int32), axis=1)

    def part_of(owner):
        turn = (owner // NC - y) % NY
        return turn + jnp.where(owner % NC == core, NY, 0)

    halves = jnp.arange(2 * COLS, dtype=jnp.int32)
    per_owner = FO_ROWS // 64
    pad = count_all - 2 * COLS
    where = jnp.stack(
        [
            part_of(owners),
            rank,
            jnp.pad(part_of(halves // per_owner), (0, pad)),
            jnp.pad(halves % per_owner, (0, pad)),
        ]
    ).astype(jnp.int32)
    counts = jnp.sum(marks, axis=0)
    mine = jnp.sum(
        jnp.where(jnp.arange(GROUPS) == y * NC + core, counts, 0), dtype=jnp.int32
    ).reshape(1)

    total = span * ROWS
    anywhere = pl.BlockSpec(memory_space=pl.ANY)
    hidden, send, keep, back = pl.pallas_call(
        functools.partial(main_kernel, [len(g) for g in keys]),
        grid_spec=pltpu.PrefetchScalarGridSpec(
            num_scalar_prefetch=3,
            grid=(COLS // PER_STEP,),
            in_specs=[
                pl.BlockSpec((total, BS), lambda c, *_: (0, 0)),
                pl.BlockSpec((PER_STEP, KB, BS, BS), lambda c, *_: (c, 0, 0, 0)),
                pl.BlockSpec((BS, PER_STEP * BS), lambda c, *_: (0, c)),
                pl.BlockSpec((total, PER_STEP * BS), lambda c, *_: (0, c)),
            ]
            + [anywhere] * len(arrays),
            out_specs=[
                pl.BlockSpec((total, PER_STEP * BS), lambda c, *_: (0, c)),
                anywhere,
                anywhere,
                pl.BlockSpec((total, BS), lambda c, *_: (0, 0)),
            ],
            scratch_shapes=[
                pltpu.VMEM((span, RB, ROWS, BS), jnp.bfloat16),
                pltpu.VMEM(((KB + 2) * BS, 2 * BS), jnp.bfloat16),
                pltpu.VMEM((total, 2 * BS), jnp.bfloat16),
                pltpu.VMEM((2 * NY, PART_ROWS, BS), jnp.int16),
                pltpu.VMEM((2 * NY, 32, BS), jnp.float32),
                pltpu.SemaphoreType.DMA((span,)),
            ],
        ),
        out_shape=[
            jax.ShapeDtypeStruct((total, COLS * BS), jnp.bfloat16),
            jax.ShapeDtypeStruct((NY, PART_ROWS, BS), jnp.int16),
            jax.ShapeDtypeStruct((NY, PART_ROWS, BS), jnp.int16),
            jax.ShapeDtypeStruct((total, BS), jnp.float32),
        ],
        compiler_params=pltpu.CompilerParams(vmem_limit_bytes=30 * 1024 * 1024),
        name="columns",
    )(
        block_rows.reshape(-1), where, place,
        low, block_weights, factor_out, upstream, *arrays,
    )

    got = shift("core", NC, 1)(send)
    back = lax.all_to_all(back.reshape(span, ROWS, BS), plane, 0, 0)
    paired = pl.pallas_call(
        pair_kernel,
        grid=(NY,),
        in_specs=[pl.BlockSpec((1, PART_ROWS, BS), lambda i: (i, 0, 0))] * 2,
        out_specs=pl.BlockSpec((1, PART_ROWS, BS), lambda i: (i, 0, 0)),
        out_shape=jax.ShapeDtypeStruct((NY, PART_ROWS, BS), jnp.int16),
        compiler_params=pltpu.CompilerParams(vmem_limit_bytes=12 * 1024 * 1024),
        name="pairs",
    )(keep, got)
    y_up, y_down = shift("y", NY, 1), shift("y", NY, -1)
    above = jnp.concatenate([paired[2, :CUT], paired[2, CODE_ROWS:]])
    below = paired[2, CUT:]
    parts = relay(paired, y_up(above), y_down(below))
    parts = [y_up(parts[0]), y_down(parts[1])]

    back, _ = lax.optimization_barrier((back, (above, below)))
    back_own = jnp.sum(back, axis=0)
    back_all = lax.all_to_all(
        jnp.broadcast_to(back_own[None], (span, ROWS, BS)), plane, 0, 0
    )
    in_part = in_partial(spread, back_all)
    in_grad = jnp.sum(lax.all_to_all(in_part, ("y", "core"), 0, 0), axis=0)

    whole = pl.BlockSpec(memory_space=pltpu.VMEM)
    slots, out_grad = pl.pallas_call(
        final_kernel,
        in_specs=[pl.BlockSpec(memory_space=pltpu.SMEM)] + [whole] * 3,
        out_specs=[whole, whole],
        out_shape=[
            jax.ShapeDtypeStruct((CAP, BS, BS), jnp.float32),
            jax.ShapeDtypeStruct((BS, FO_ROWS), jnp.float32),
        ],
        compiler_params=pltpu.CompilerParams(vmem_limit_bytes=16 * 1024 * 1024),
        cost_estimate=pl.CostEstimate(
            flops=10_000_000, bytes_accessed=16_000_000, transcendentals=0
        ),
        name="slots",
    )(mine, paired, *parts)
    return hidden, slots, in_grad, out_grad


def solution(mesh):
    split = Mesh(mesh.devices.reshape(NY, NC, NZ, NX), ("y", "core", "z", "x"))
    dp, mp = ("y", "core"), ("z", "x")
    return jax.shard_map(
        per_device,
        mesh=split,
        in_specs=(
            P(dp + mp, None),
            P(mp, None, None, None),
            P(mp, None),
            P(mp, None, None),
            P(mp, None),
            P(None, mp),
            P(dp, mp),
        ),
        out_specs=(
            P(dp, mp),
            P(mp + dp, None, None),
            P(mp + dp, None),
            P(None, mp + dp),
        ),
        check_vma=False,
    )
```

```python
import functools

import jax
import jax.numpy as jnp
from jax import lax
from jax.experimental import pallas as pl
from jax.experimental.pallas import tpu as pltpu
from jax.sharding import Mesh
from jax.sharding import PartitionSpec as P

highest = lax.Precision.HIGHEST
BS = 128
ROWS = 16
NX, NZ, NY, NC = 4, 8, 4, 2
COLS = 12
PER_STEP = 2
KB = 8
RB = 96
CAP = 18
GROUPS = NY * NC
SLOT_ROWS = CAP * BS
FO_ROWS = COLS * BS // GROUPS
CODE_ROWS = SLOT_ROWS + FO_ROWS
PART_ROWS = CODE_ROWS + 32
FINE = 256.0
CUT = 10 * BS


def shift(axis, size, step):
    pairs = [(i, (i + step) % size) for i in range(size)]
    return lambda value: lax.ppermute(value, axis, pairs)


def split_two(value):
    high = value.astype(jnp.bfloat16)
    low = (value - high.astype(jnp.float32)).astype(jnp.bfloat16)
    return high, low


def level_of(block):
    top = jnp.max(jnp.abs(block), axis=0, keepdims=True)
    return jnp.ceil(jnp.log2(jnp.maximum(top, 1e-30)) * FINE)


def encode(block, level):
    inverse = jnp.exp2(level * (-1.0 / FINE)) * 32700.0
    return jnp.floor(block * inverse + 0.5).astype(jnp.int32).astype(jnp.int16)


def decode(code, level):
    unit = jnp.exp2(level * (1.0 / FINE)) * (1.0 / 32700.0)
    return code.astype(jnp.int32).astype(jnp.float32) * unit


def main_kernel(
    counts, rows_ref, where_ref, place_ref, low_ref, weight_ref, factor_ref, up_ref, *rest
):
    arrays, rest = rest[: len(counts)], rest[len(counts) :]
    pieces = [ref.at[i] for ref, n in zip(arrays, counts) for i in range(n)]
    hidden_ref, send_ref, keep_ref, back_ref = rest[:4]
    tok, wide, low_two, codes, levels, sems = rest[4:]
    c = pl.program_id(0)
    tokens = NX * NZ * ROWS

    @pl.when(c == 0)
    def _():
        copies = [
            pltpu.make_async_copy(pieces[j], tok.at[place_ref[j]], sems.at[j])
            for j in range(NX * NZ)
        ]
        for copy in copies:
            copy.start()
        high, low = split_two(low_ref[...])
        low_two[:, :BS] = high
        low_two[:, BS:] = low
        wide[(KB + 1) * BS :, BS:] = jnp.zeros((BS, BS), jnp.bfloat16)
        back_ref[...] = jnp.zeros_like(back_ref)
        for copy in copies:
            copy.wait()

    for i in range(PER_STEP):
        col = c * PER_STEP + i
        here = slice(i * BS, (i + 1) * BS)
        for k in range(KB):
            high, low = split_two(weight_ref[i, k])
            wide[k * BS : (k + 1) * BS, :BS] = high
            wide[k * BS : (k + 1) * BS, BS:] = low
        f_high, f_low = split_two(factor_ref[:, here])
        wide[KB * BS : (KB + 1) * BS, :BS] = f_high
        wide[KB * BS : (KB + 1) * BS, BS:] = f_low
        wide[(KB + 1) * BS :, :BS] = f_high

        panel = jnp.concatenate(
            [tok[:, rows_ref[col * KB + k]].reshape(tokens, BS) for k in range(KB)]
            + [low_two[...]],
            axis=1,
        )
        both = jnp.dot(panel, wide[...], preferred_element_type=jnp.float32)
        v = both[:, :BS] + both[:, BS:]
        root = 0.7978845608028654
        square = v * v
        t = jnp.tanh(root * v * (1.0 + 0.044715 * square))
        half = 0.5 * (1.0 + t)
        hidden_ref[:, here] = (v * half).astype(jnp.bfloat16)
        slope = half + 0.5 * root * v * (1.0 - t * t) * (1.0 + 3.0 * 0.044715 * square)
        grad = up_ref[:, here].astype(jnp.float32) * slope

        g_high, g_low = split_two(grad)
        g_two = jnp.concatenate([g_high, g_low], axis=1)
        f_two = jnp.concatenate(
            [
                jnp.concatenate([f_high, f_high], axis=1),
                jnp.concatenate([f_low, jnp.zeros_like(f_low)], axis=1),
            ],
            axis=0,
        )
        back = lax.dot_general(
            g_two, f_two, (((1,), (1,)), ((), ())), preferred_element_type=jnp.float32
        )
        back_ref[...] += back[:, :BS] + back[:, BS:]

        grad_t = grad.T
        t_high, t_low = split_two(grad_t)
        gt_two = jnp.concatenate([t_high, t_low], axis=0)
        product = jnp.dot(gt_two, panel, preferred_element_type=jnp.float32)
        product = product[:BS] + product[BS:]
        for k in range(KB):
            block = product[:, k * BS : (k + 1) * BS]
            level = level_of(block)
            part = where_ref[0, col * KB + k]
            slot = where_ref[1, col * KB + k]
            codes[part, pl.ds(pl.multiple_of(slot * BS, BS), BS)] = encode(block, level)
            levels[part, pl.ds(slot, 1)] = level
        outer = product[:, KB * BS : (KB + 1) * BS] + product[:, (KB + 1) * BS :]
        for h in range(2):
            block = outer[h * 64 : (h + 1) * 64]
            level = level_of(block)
            part = where_ref[2, col * 2 + h]
            slot = where_ref[3, col * 2 + h]
            start = pl.multiple_of(SLOT_ROWS + slot * 64, 64)
            codes[part, pl.ds(start, 64)] = encode(block, level)
            levels[part, pl.ds(CAP + slot, 1)] = level

    @pl.when(c == COLS // PER_STEP - 1)
    def _():
        for part in range(2 * NY):
            codes[part, CODE_ROWS:] = levels[part].astype(jnp.int32).astype(jnp.int16)
        send = pltpu.make_async_copy(codes.at[pl.ds(0, NY)], send_ref, sems.at[0])
        keep = pltpu.make_async_copy(codes.at[pl.ds(NY, NY)], keep_ref, sems.at[1])
        send.start()
        keep.start()
        send.wait()
        keep.wait()


def blocks_of():
    spans = [(s * BS, BS, s) for s in range(CAP)]
    return spans + [(SLOT_ROWS + h * 64, 64, CAP + h) for h in range(FO_ROWS // 64)]


def pair_kernel(keep_ref, got_ref, out_ref):
    keep_levels = keep_ref[0, CODE_ROWS:].astype(jnp.int32).astype(jnp.float32)
    got_levels = got_ref[0, CODE_ROWS:].astype(jnp.int32).astype(jnp.float32)
    fresh = []
    for start, size, index in blocks_of():
        span = slice(start, start + size)
        total = decode(keep_ref[0, span], keep_levels[index : index + 1])
        total += decode(got_ref[0, span], got_levels[index : index + 1])
        level = level_of(total)
        out_ref[0, span] = encode(total, level)
        fresh.append(level)
    fresh.append(jnp.zeros((32 - len(fresh), BS), jnp.float32))
    fresh = jnp.concatenate(fresh, axis=0)
    out_ref[0, CODE_ROWS:] = fresh.astype(jnp.int32).astype(jnp.int16)


def levels_in(rows):
    return rows.astype(jnp.int32).astype(jnp.float32)


def relay_kernel(up_ref, down_ref, above_ref, below_ref, up_out, down_out):
    for own, got, out, first in (
        (up_ref, above_ref, up_out, True),
        (down_ref, below_ref, down_out, False),
    ):
        own_levels = levels_in(own[0, CODE_ROWS:])
        got_levels = levels_in(got[CUT:] if first else got[CODE_ROWS - CUT :])
        fresh = []
        for start, size, index in blocks_of():
            span = slice(start, start + size)
            level = own_levels[index : index + 1]
            if (start < CUT) == first:
                offset = start if first else start - CUT
                total = decode(own[0, span], level)
                total += decode(got[offset : offset + size], got_levels[index : index + 1])
                level = level_of(total)
                out[span] = encode(total, level)
            else:
                out[span] = own[0, span]
            fresh.append(level)
        fresh.append(jnp.zeros((32 - len(fresh), BS), jnp.float32))
        fresh = jnp.concatenate(fresh, axis=0)
        out[CODE_ROWS:] = fresh.astype(jnp.int32).astype(jnp.int16)


def relay(paired, above, below):
    one = lambda i: pl.BlockSpec((1, PART_ROWS, BS), lambda _: (i, 0, 0))
    flat = lambda rows: pl.BlockSpec((rows, BS), lambda _: (0, 0))
    return pl.pallas_call(
        relay_kernel,
        grid=(1,),
        in_specs=[one(1), one(3), flat(above.shape[0]), flat(below.shape[0])],
        out_specs=[flat(PART_ROWS)] * 2,
        out_shape=[jax.ShapeDtypeStruct((PART_ROWS, BS), jnp.int16)] * 2,
        compiler_params=pltpu.CompilerParams(vmem_limit_bytes=30 * 1024 * 1024),
        cost_estimate=pl.CostEstimate(
            flops=40_000_000, bytes_accessed=40_000_000, transcendentals=0
        ),
        name="relay",
    )(paired, paired, above, below)


def final_kernel(count_ref, own_ref, *refs):
    parts, (slots_ref, outer_ref) = refs[:2], refs[2:]
    levels = [levels_in(own_ref[0, CODE_ROWS:])] + [levels_in(r[CODE_ROWS:]) for r in parts]
    count = count_ref[0]
    for start, size, index in blocks_of():
        span = slice(start, start + size)
        total = decode(own_ref[0, span], levels[0][index : index + 1])
        for i in range(2):
            total += decode(parts[i][span], levels[i + 1][index : index + 1])
        if index < CAP:
            slots_ref[index] = jnp.where(index < count, total.T, 0.0)
        else:
            h = index - CAP
            outer_ref[h * 64 : (h + 1) * 64] = total


def in_kernel(cols_ref, back_ref, out_ref):
    total = NZ * NX * ROWS
    high, low = split_two(back_ref[...].reshape(total, BS).T)
    two = jnp.concatenate([high, low], axis=0)
    panel = jnp.concatenate(
        [cols_ref[:, j].reshape(total, BS) for j in range(cols_ref.shape[1])], axis=1
    )
    both = jnp.dot(two, panel, preferred_element_type=jnp.float32)
    out_ref[...] = (both[:BS] + both[BS:]).T.reshape(out_ref.shape)


def in_partial(cols, back_all):
    whole = pl.BlockSpec(memory_space=pltpu.VMEM)
    size = cols.shape[1] * BS // GROUPS
    return pl.pallas_call(
        in_kernel,
        in_specs=[whole, whole],
        out_specs=whole,
        out_shape=jax.ShapeDtypeStruct((GROUPS, size, BS), jnp.float32),
        compiler_params=pltpu.CompilerParams(vmem_limit_bytes=30 * 1024 * 1024),
        name="into",
    )(cols, back_all)


def gather_tokens(own, x):
    z_up, z_down = shift("z", NZ, 1), shift("z", NZ, -1)
    x_up, x_down = shift("x", NX, 1), shift("x", NX, -1)
    arrays, keys = [], []

    def around(a):
        copies = jnp.broadcast_to(held[a, 0], (NX,) + own.shape)
        row = lax.all_to_all(copies, "x", 0, 0)
        arrays.append(row)
        keys.append([(a, g - x) for g in range(NX)])
        return row

    held = {(0, 0): own[None]}
    row = around(0)
    for b in (-1, 1, 2):
        held[0, b] = lax.dynamic_slice_in_dim(row, lax.rem(x + b + NX, NX), 1, 0)
    for a in (1, 2, 3):
        for b in (0, 2):
            held[-a, b] = z_up(held[1 - a, b])
            held[a, b] = z_down(held[a - 1, b])
    held[4, 0] = z_up(held[-3, 0])
    for a in (-1, 1, -2, 2, -3, 3):
        for b, move in ((-1, x_up), (1, x_down)):
            if a == b:
                held[a, b] = (z_down if a > 0 else z_up)(held[0, b])
            else:
                held[a, b] = move(held[a, 0])
    around(4)
    for (a, b), value in held.items():
        if a not in (0, 4):
            arrays.append(value)
            keys.append([(a, b)])
    return arrays, keys


def per_device(tokens, block_weights, block_rows, block_owners, factor_in, factor_out, upstream):
    own = jnp.transpose(tokens.reshape(ROWS, RB, BS), (1, 0, 2))
    span = NX * NZ
    per = RB // span
    plane = ("z", "x")
    z, x = lax.axis_index("z"), lax.axis_index("x")
    arrays, keys = gather_tokens(own, x)
    spread = lax.all_to_all(own.reshape(span, per, ROWS, BS), plane, 0, 0)
    factor = factor_in.reshape(per, BS, BS)
    partial = jnp.einsum(
        "sbtf,bfr->str", spread.astype(jnp.float32), factor, precision=highest
    )
    low_own = jnp.sum(lax.all_to_all(partial, plane, 0, 0), axis=0)
    low = lax.all_to_all(jnp.broadcast_to(low_own[None], (span, ROWS, BS)), plane, 0, 0)
    y, core = lax.axis_index("y"), lax.axis_index("core")
    place = [((z + a) % NZ) * NX + (x + b + NX) % NX for group in keys for a, b in group]
    place = jnp.stack(place).astype(jnp.int32)
    low = low.reshape(span * ROWS, BS)

    owners = block_owners.reshape(-1)
    count_all = owners.shape[0]
    marks = (owners[:, None] == jnp.arange(GROUPS, dtype=jnp.int32)[None, :]).astype(jnp.int32)
    before = (
        jnp.arange(count_all, dtype=jnp.int32)[:, None]
        > jnp.arange(count_all, dtype=jnp.int32)[None, :]
    ) & (owners[:, None] == owners[None, :])
    rank = jnp.sum(before.astype(jnp.int32), axis=1)

    def part_of(owner):
        turn = (owner // NC - y) % NY
        return turn + jnp.where(owner % NC == core, NY, 0)

    halves = jnp.arange(2 * COLS, dtype=jnp.int32)
    per_owner = FO_ROWS // 64
    pad = count_all - 2 * COLS
    where = jnp.stack(
        [
            part_of(owners),
            rank,
            jnp.pad(part_of(halves // per_owner), (0, pad)),
            jnp.pad(halves % per_owner, (0, pad)),
        ]
    ).astype(jnp.int32)
    counts = jnp.sum(marks, axis=0)
    mine = jnp.sum(
        jnp.where(jnp.arange(GROUPS) == y * NC + core, counts, 0), dtype=jnp.int32
    ).reshape(1)

    total = span * ROWS
    anywhere = pl.BlockSpec(memory_space=pl.ANY)
    hidden, send, keep, back = pl.pallas_call(
        functools.partial(main_kernel, [len(g) for g in keys]),
        grid_spec=pltpu.PrefetchScalarGridSpec(
            num_scalar_prefetch=3,
            grid=(COLS // PER_STEP,),
            in_specs=[
                pl.BlockSpec((total, BS), lambda c, *_: (0, 0)),
                pl.BlockSpec((PER_STEP, KB, BS, BS), lambda c, *_: (c, 0, 0, 0)),
                pl.BlockSpec((BS, PER_STEP * BS), lambda c, *_: (0, c)),
                pl.BlockSpec((total, PER_STEP * BS), lambda c, *_: (0, c)),
            ]
            + [anywhere] * len(arrays),
            out_specs=[
                pl.BlockSpec((total, PER_STEP * BS), lambda c, *_: (0, c)),
                anywhere,
                anywhere,
                pl.BlockSpec((total, BS), lambda c, *_: (0, 0)),
            ],
            scratch_shapes=[
                pltpu.VMEM((span, RB, ROWS, BS), jnp.bfloat16),
                pltpu.VMEM(((KB + 2) * BS, 2 * BS), jnp.bfloat16),
                pltpu.VMEM((total, 2 * BS), jnp.bfloat16),
                pltpu.VMEM((2 * NY, PART_ROWS, BS), jnp.int16),
                pltpu.VMEM((2 * NY, 32, BS), jnp.float32),
                pltpu.SemaphoreType.DMA((span,)),
            ],
        ),
        out_shape=[
            jax.ShapeDtypeStruct((total, COLS * BS), jnp.bfloat16),
            jax.ShapeDtypeStruct((NY, PART_ROWS, BS), jnp.int16),
            jax.ShapeDtypeStruct((NY, PART_ROWS, BS), jnp.int16),
            jax.ShapeDtypeStruct((total, BS), jnp.float32),
        ],
        compiler_params=pltpu.CompilerParams(vmem_limit_bytes=50 * 1024 * 1024),
        name="columns",
    )(
        block_rows.reshape(-1), where, place,
        low, block_weights, factor_out, upstream, *arrays,
    )

    got = shift("core", NC, 1)(send)
    back = lax.all_to_all(back.reshape(span, ROWS, BS), plane, 0, 0)
    paired = pl.pallas_call(
        pair_kernel,
        grid=(NY,),
        in_specs=[pl.BlockSpec((1, PART_ROWS, BS), lambda i: (i, 0, 0))] * 2,
        out_specs=pl.BlockSpec((1, PART_ROWS, BS), lambda i: (i, 0, 0)),
        out_shape=jax.ShapeDtypeStruct((NY, PART_ROWS, BS), jnp.int16),
        compiler_params=pltpu.CompilerParams(vmem_limit_bytes=50 * 1024 * 1024),
        name="pairs",
    )(keep, got)
    y_up, y_down = shift("y", NY, 1), shift("y", NY, -1)
    above = jnp.concatenate([paired[2, :CUT], paired[2, CODE_ROWS:]])
    below = paired[2, CUT:]
    parts = relay(paired, y_up(above), y_down(below))
    parts = [y_up(parts[0]), y_down(parts[1])]

    back, _ = lax.optimization_barrier((back, (above, below)))
    back_own = jnp.sum(back, axis=0)
    back_all = lax.all_to_all(
        jnp.broadcast_to(back_own[None], (span, ROWS, BS)), plane, 0, 0
    )
    in_part = in_partial(spread, back_all)
    in_grad = jnp.sum(lax.all_to_all(in_part, ("y", "core"), 0, 0), axis=0)

    whole = pl.BlockSpec(memory_space=pltpu.VMEM)
    slots, out_grad = pl.pallas_call(
        final_kernel,
        in_specs=[pl.BlockSpec(memory_space=pltpu.SMEM)] + [whole] * 3,
        out_specs=[whole, whole],
        out_shape=[
            jax.ShapeDtypeStruct((CAP, BS, BS), jnp.float32),
            jax.ShapeDtypeStruct((FO_ROWS, BS), jnp.float32),
        ],
        compiler_params=pltpu.CompilerParams(vmem_limit_bytes=50 * 1024 * 1024),
        cost_estimate=pl.CostEstimate(
            flops=10_000_000, bytes_accessed=16_000_000, transcendentals=0
        ),
        name="slots",
    )(mine, paired, *parts)
    return hidden, slots, in_grad, out_grad.T


def solution(mesh):
    split = Mesh(mesh.devices.reshape(NY, NC, NZ, NX), ("y", "core", "z", "x"))
    dp, mp = ("y", "core"), ("z", "x")
    return jax.shard_map(
        per_device,
        mesh=split,
        in_specs=(
            P(dp + mp, None),
            P(mp, None, None, None),
            P(mp, None),
            P(mp, None, None),
            P(mp, None),
            P(None, mp),
            P(dp, mp),
        ),
        out_specs=(
            P(dp, mp),
            P(mp + dp, None, None),
            P(mp + dp, None),
            P(None, mp + dp),
        ),
        check_vma=False,
    )
```

```python
import functools

import jax
import jax.numpy as jnp
from jax import lax
from jax.experimental import pallas as pl
from jax.experimental.pallas import tpu as pltpu
from jax.sharding import Mesh
from jax.sharding import PartitionSpec as P

highest = lax.Precision.HIGHEST
BS = 128
ROWS = 16
NX, NZ, NY, NC = 4, 8, 4, 2
COLS = 12
PER_STEP = 2
KB = 8
RB = 96
CAP = 18
GROUPS = NY * NC
SLOT_ROWS = CAP * BS
FO_ROWS = COLS * BS // GROUPS
CODE_ROWS = SLOT_ROWS + FO_ROWS
PART_ROWS = CODE_ROWS + 32
FINE = 256.0
ORDER = (
    ("across", (0, 0), (0, 2)),
    ("z_up", (0, 0), (-1, 0)),
    ("z_up", (-1, 0), (-2, 0)),
    ("z_down", (0, 0), (1, 0)),
    ("z_down", (1, 0), (2, 0)),
    ("x_up", (1, 0), (1, -1)),
    ("z_up", (0, 2), (-1, 2)),
    ("x_down", (0, 0), (0, 1)),
    ("x_up", (0, 0), (0, -1)),
    ("x_down", (-1, 0), (-1, 1)),
    ("x_up", (2, 0), (2, -1)),
    ("z_down", (0, 2), (1, 2)),
    ("x_up", (-2, 0), (-2, -1)),
    ("z_down", (0, 1), (1, 1)),
    ("z_up", (-2, 0), (-3, 0)),
    ("z_down", (2, 0), (3, 0)),
    ("x_up", (3, 0), (3, -1)),
    ("x_down", (-2, 0), (-2, 1)),
    ("z_up", (0, -1), (-1, -1)),
    ("x_down", (-3, 0), (-3, 1)),
    ("x_up", (-3, 0), (-3, -1)),
    ("x_down", (2, 0), (2, 1)),
    ("z_up", (-1, 2), (-2, 2)),
    ("z_up", (-2, 2), (-3, 2)),
    ("z_down", (1, 2), (2, 2)),
    ("z_up", (-3, 0), (4, 0)),
    ("z_down", (2, 2), (3, 2)),
    ("x_down", (3, 0), (3, 1)),
    ("x_up", (4, 0), (4, -1)),
    ("x_down", (4, 0), (4, 1)),
    ("z_down", (3, 2), (4, 2)),
)
CUT = 10 * BS


def shift(axis, size, step):
    pairs = [(i, (i + step) % size) for i in range(size)]
    return lambda value: lax.ppermute(value, axis, pairs)


def split_two(value):
    high = value.astype(jnp.bfloat16)
    low = (value - high.astype(jnp.float32)).astype(jnp.bfloat16)
    return high, low


def level_of(block):
    top = jnp.max(jnp.abs(block), axis=0, keepdims=True)
    return jnp.ceil(jnp.log2(jnp.maximum(top, 1e-30)) * FINE)


def encode(block, level):
    inverse = jnp.exp2(level * (-1.0 / FINE)) * 32700.0
    return jnp.floor(block * inverse + 0.5).astype(jnp.int32).astype(jnp.int16)


def decode(code, level):
    unit = jnp.exp2(level * (1.0 / FINE)) * (1.0 / 32700.0)
    return code.astype(jnp.int32).astype(jnp.float32) * unit


def main_kernel(
    counts, rows_ref, where_ref, place_ref, low_ref, weight_ref, factor_ref, up_ref, *rest
):
    arrays, rest = rest[: len(counts)], rest[len(counts) :]
    pieces = [ref.at[i] for ref, n in zip(arrays, counts) for i in range(n)]
    hidden_ref, send_ref, keep_ref, back_ref = rest[:4]
    tok, wide, low_two, codes, levels, sems = rest[4:]
    c = pl.program_id(0)
    tokens = NX * NZ * ROWS

    @pl.when(c == 0)
    def _():
        copies = [
            pltpu.make_async_copy(pieces[j], tok.at[place_ref[j]], sems.at[j])
            for j in range(NX * NZ)
        ]
        for copy in copies:
            copy.start()
        high, low = split_two(low_ref[...])
        low_two[:, :BS] = high
        low_two[:, BS:] = low
        wide[(KB + 1) * BS :, BS:] = jnp.zeros((BS, BS), jnp.bfloat16)
        back_ref[...] = jnp.zeros_like(back_ref)
        for copy in copies:
            copy.wait()

    for i in range(PER_STEP):
        col = c * PER_STEP + i
        here = slice(i * BS, (i + 1) * BS)
        for k in range(KB):
            high, low = split_two(weight_ref[i, k])
            wide[k * BS : (k + 1) * BS, :BS] = high
            wide[k * BS : (k + 1) * BS, BS:] = low
        f_high, f_low = split_two(factor_ref[:, here])
        wide[KB * BS : (KB + 1) * BS, :BS] = f_high
        wide[KB * BS : (KB + 1) * BS, BS:] = f_low
        wide[(KB + 1) * BS :, :BS] = f_high

        panel = jnp.concatenate(
            [tok[:, rows_ref[col * KB + k]].reshape(tokens, BS) for k in range(KB)]
            + [low_two[...]],
            axis=1,
        )
        both = jnp.dot(panel, wide[...], preferred_element_type=jnp.float32)
        v = both[:, :BS] + both[:, BS:]
        root = 0.7978845608028654
        square = v * v
        t = jnp.tanh(root * v * (1.0 + 0.044715 * square))
        half = 0.5 * (1.0 + t)
        hidden_ref[:, here] = (v * half).astype(jnp.bfloat16)
        slope = half + 0.5 * root * v * (1.0 - t * t) * (1.0 + 3.0 * 0.044715 * square)
        grad = up_ref[:, here].astype(jnp.float32) * slope

        g_high, g_low = split_two(grad)
        g_two = jnp.concatenate([g_high, g_low], axis=1)
        f_two = jnp.concatenate(
            [
                jnp.concatenate([f_high, f_high], axis=1),
                jnp.concatenate([f_low, jnp.zeros_like(f_low)], axis=1),
            ],
            axis=0,
        )
        back = lax.dot_general(
            g_two, f_two, (((1,), (1,)), ((), ())), preferred_element_type=jnp.float32
        )
        back_ref[...] += back[:, :BS] + back[:, BS:]

        grad_t = grad.T
        t_high, t_low = split_two(grad_t)
        gt_two = jnp.concatenate([t_high, t_low], axis=0)
        product = jnp.dot(gt_two, panel, preferred_element_type=jnp.float32)
        product = product[:BS] + product[BS:]
        for k in range(KB):
            block = product[:, k * BS : (k + 1) * BS]
            level = level_of(block)
            part = where_ref[0, col * KB + k]
            slot = where_ref[1, col * KB + k]
            codes[part, pl.ds(pl.multiple_of(slot * BS, BS), BS)] = encode(block, level)
            levels[part, pl.ds(slot, 1)] = level
        outer = product[:, KB * BS : (KB + 1) * BS] + product[:, (KB + 1) * BS :]
        for h in range(2):
            block = outer[h * 64 : (h + 1) * 64]
            level = level_of(block)
            part = where_ref[2, col * 2 + h]
            slot = where_ref[3, col * 2 + h]
            start = pl.multiple_of(SLOT_ROWS + slot * 64, 64)
            codes[part, pl.ds(start, 64)] = encode(block, level)
            levels[part, pl.ds(CAP + slot, 1)] = level

    @pl.when(c == COLS // PER_STEP - 1)
    def _():
        for part in range(2 * NY):
            codes[part, CODE_ROWS:] = levels[part].astype(jnp.int32).astype(jnp.int16)
        send = pltpu.make_async_copy(codes.at[pl.ds(0, NY)], send_ref, sems.at[0])
        keep = pltpu.make_async_copy(codes.at[pl.ds(NY, NY)], keep_ref, sems.at[1])
        send.start()
        keep.start()
        send.wait()
        keep.wait()


def blocks_of():
    spans = [(s * BS, BS, s) for s in range(CAP)]
    return spans + [(SLOT_ROWS + h * 64, 64, CAP + h) for h in range(FO_ROWS // 64)]


def pair_kernel(keep_ref, got_ref, out_ref):
    keep_levels = keep_ref[0, CODE_ROWS:].astype(jnp.int32).astype(jnp.float32)
    got_levels = got_ref[0, CODE_ROWS:].astype(jnp.int32).astype(jnp.float32)
    fresh = []
    for start, size, index in blocks_of():
        span = slice(start, start + size)
        total = decode(keep_ref[0, span], keep_levels[index : index + 1])
        total += decode(got_ref[0, span], got_levels[index : index + 1])
        level = level_of(total)
        out_ref[0, span] = encode(total, level)
        fresh.append(level)
    fresh.append(jnp.zeros((32 - len(fresh), BS), jnp.float32))
    fresh = jnp.concatenate(fresh, axis=0)
    out_ref[0, CODE_ROWS:] = fresh.astype(jnp.int32).astype(jnp.int16)


def levels_in(rows):
    return rows.astype(jnp.int32).astype(jnp.float32)


def relay_kernel(up_ref, down_ref, above_ref, below_ref, up_out, down_out):
    for own, got, out, first in (
        (up_ref, above_ref, up_out, True),
        (down_ref, below_ref, down_out, False),
    ):
        own_levels = levels_in(own[0, CODE_ROWS:])
        got_levels = levels_in(got[CUT:] if first else got[CODE_ROWS - CUT :])
        fresh = []
        for start, size, index in blocks_of():
            span = slice(start, start + size)
            level = own_levels[index : index + 1]
            if (start < CUT) == first:
                offset = start if first else start - CUT
                total = decode(own[0, span], level)
                total += decode(got[offset : offset + size], got_levels[index : index + 1])
                level = level_of(total)
                out[span] = encode(total, level)
            else:
                out[span] = own[0, span]
            fresh.append(level)
        fresh.append(jnp.zeros((32 - len(fresh), BS), jnp.float32))
        fresh = jnp.concatenate(fresh, axis=0)
        out[CODE_ROWS:] = fresh.astype(jnp.int32).astype(jnp.int16)


def relay(paired, above, below):
    one = lambda i: pl.BlockSpec((1, PART_ROWS, BS), lambda _: (i, 0, 0))
    flat = lambda rows: pl.BlockSpec((rows, BS), lambda _: (0, 0))
    return pl.pallas_call(
        relay_kernel,
        grid=(1,),
        in_specs=[one(1), one(3), flat(above.shape[0]), flat(below.shape[0])],
        out_specs=[flat(PART_ROWS)] * 2,
        out_shape=[jax.ShapeDtypeStruct((PART_ROWS, BS), jnp.int16)] * 2,
        compiler_params=pltpu.CompilerParams(vmem_limit_bytes=30 * 1024 * 1024),
        cost_estimate=pl.CostEstimate(
            flops=40_000_000, bytes_accessed=40_000_000, transcendentals=0
        ),
        name="relay",
    )(paired, paired, above, below)


def final_kernel(count_ref, own_ref, *refs):
    parts, (slots_ref, outer_ref) = refs[:2], refs[2:]
    levels = [levels_in(own_ref[0, CODE_ROWS:])] + [levels_in(r[CODE_ROWS:]) for r in parts]
    count = count_ref[0]
    for start, size, index in blocks_of():
        span = slice(start, start + size)
        total = decode(own_ref[0, span], levels[0][index : index + 1])
        for i in range(2):
            total += decode(parts[i][span], levels[i + 1][index : index + 1])
        if index < CAP:
            slots_ref[index] = jnp.where(index < count, total.T, 0.0)
        else:
            h = index - CAP
            outer_ref[h * 64 : (h + 1) * 64] = total


def in_kernel(cols_ref, back_ref, out_ref):
    total = NZ * NX * ROWS
    high, low = split_two(back_ref[...].reshape(total, BS).T)
    two = jnp.concatenate([high, low], axis=0)
    panel = jnp.concatenate(
        [cols_ref[:, j].reshape(total, BS) for j in range(cols_ref.shape[1])], axis=1
    )
    both = jnp.dot(two, panel, preferred_element_type=jnp.float32)
    out_ref[...] = (both[:BS] + both[BS:]).T.reshape(out_ref.shape)


def in_partial(cols, back_all):
    whole = pl.BlockSpec(memory_space=pltpu.VMEM)
    size = cols.shape[1] * BS // GROUPS
    return pl.pallas_call(
        in_kernel,
        in_specs=[whole, whole],
        out_specs=whole,
        out_shape=jax.ShapeDtypeStruct((GROUPS, size, BS), jnp.float32),
        compiler_params=pltpu.CompilerParams(vmem_limit_bytes=30 * 1024 * 1024),
        name="into",
    )(cols, back_all)


def gather_tokens(own):
    moves = {
        "z_up": shift("z", NZ, 1),
        "z_down": shift("z", NZ, -1),
        "x_up": shift("x", NX, 1),
        "x_down": shift("x", NX, -1),
        "across": shift("x", NX, 2),
    }
    held = {(0, 0): own[None]}
    for name, source, target in ORDER:
        held[target] = moves[name](held[source])
    return list(held.values()), [[key] for key in held]


def per_device(tokens, block_weights, block_rows, block_owners, factor_in, factor_out, upstream):
    own = jnp.transpose(tokens.reshape(ROWS, RB, BS), (1, 0, 2))
    span = NX * NZ
    per = RB // span
    plane = ("z", "x")
    arrays, keys = gather_tokens(own)
    spread = lax.all_to_all(own.reshape(span, per, ROWS, BS), plane, 0, 0)
    factor = factor_in.reshape(per, BS, BS)
    partial = jnp.einsum(
        "sbtf,bfr->str", spread.astype(jnp.float32), factor, precision=highest
    )
    low_own = jnp.sum(lax.all_to_all(partial, plane, 0, 0), axis=0)
    low = lax.all_to_all(jnp.broadcast_to(low_own[None], (span, ROWS, BS)), plane, 0, 0)
    z, x = lax.axis_index("z"), lax.axis_index("x")
    y, core = lax.axis_index("y"), lax.axis_index("core")
    place = [((z + a) % NZ) * NX + (x + b) % NX for group in keys for a, b in group]
    place = jnp.stack(place).astype(jnp.int32)
    low = low.reshape(span * ROWS, BS)

    owners = block_owners.reshape(-1)
    count_all = owners.shape[0]
    marks = (owners[:, None] == jnp.arange(GROUPS, dtype=jnp.int32)[None, :]).astype(jnp.int32)
    before = (
        jnp.arange(count_all, dtype=jnp.int32)[:, None]
        > jnp.arange(count_all, dtype=jnp.int32)[None, :]
    ) & (owners[:, None] == owners[None, :])
    rank = jnp.sum(before.astype(jnp.int32), axis=1)

    def part_of(owner):
        turn = (owner // NC - y) % NY
        return turn + jnp.where(owner % NC == core, NY, 0)

    halves = jnp.arange(2 * COLS, dtype=jnp.int32)
    per_owner = FO_ROWS // 64
    pad = count_all - 2 * COLS
    where = jnp.stack(
        [
            part_of(owners),
            rank,
            jnp.pad(part_of(halves // per_owner), (0, pad)),
            jnp.pad(halves % per_owner, (0, pad)),
        ]
    ).astype(jnp.int32)
    counts = jnp.sum(marks, axis=0)
    mine = jnp.sum(
        jnp.where(jnp.arange(GROUPS) == y * NC + core, counts, 0), dtype=jnp.int32
    ).reshape(1)

    total = span * ROWS
    anywhere = pl.BlockSpec(memory_space=pl.ANY)
    hidden, send, keep, back = pl.pallas_call(
        functools.partial(main_kernel, [len(g) for g in keys]),
        grid_spec=pltpu.PrefetchScalarGridSpec(
            num_scalar_prefetch=3,
            grid=(COLS // PER_STEP,),
            in_specs=[
                pl.BlockSpec((total, BS), lambda c, *_: (0, 0)),
                pl.BlockSpec((PER_STEP, KB, BS, BS), lambda c, *_: (c, 0, 0, 0)),
                pl.BlockSpec((BS, PER_STEP * BS), lambda c, *_: (0, c)),
                pl.BlockSpec((total, PER_STEP * BS), lambda c, *_: (0, c)),
            ]
            + [anywhere] * len(arrays),
            out_specs=[
                pl.BlockSpec((total, PER_STEP * BS), lambda c, *_: (0, c)),
                anywhere,
                anywhere,
                pl.BlockSpec((total, BS), lambda c, *_: (0, 0)),
            ],
            scratch_shapes=[
                pltpu.VMEM((span, RB, ROWS, BS), jnp.bfloat16),
                pltpu.VMEM(((KB + 2) * BS, 2 * BS), jnp.bfloat16),
                pltpu.VMEM((total, 2 * BS), jnp.bfloat16),
                pltpu.VMEM((2 * NY, PART_ROWS, BS), jnp.int16),
                pltpu.VMEM((2 * NY, 32, BS), jnp.float32),
                pltpu.SemaphoreType.DMA((span,)),
            ],
        ),
        out_shape=[
            jax.ShapeDtypeStruct((total, COLS * BS), jnp.bfloat16),
            jax.ShapeDtypeStruct((NY, PART_ROWS, BS), jnp.int16),
            jax.ShapeDtypeStruct((NY, PART_ROWS, BS), jnp.int16),
            jax.ShapeDtypeStruct((total, BS), jnp.float32),
        ],
        compiler_params=pltpu.CompilerParams(vmem_limit_bytes=50 * 1024 * 1024),
        name="columns",
    )(
        block_rows.reshape(-1), where, place,
        low, block_weights, factor_out, upstream, *arrays,
    )

    got = shift("core", NC, 1)(send)
    back = lax.all_to_all(back.reshape(span, ROWS, BS), plane, 0, 0)
    paired = pl.pallas_call(
        pair_kernel,
        grid=(NY,),
        in_specs=[pl.BlockSpec((1, PART_ROWS, BS), lambda i: (i, 0, 0))] * 2,
        out_specs=pl.BlockSpec((1, PART_ROWS, BS), lambda i: (i, 0, 0)),
        out_shape=jax.ShapeDtypeStruct((NY, PART_ROWS, BS), jnp.int16),
        compiler_params=pltpu.CompilerParams(vmem_limit_bytes=50 * 1024 * 1024),
        name="pairs",
    )(keep, got)
    y_up, y_down = shift("y", NY, 1), shift("y", NY, -1)
    above = jnp.concatenate([paired[2, :CUT], paired[2, CODE_ROWS:]])
    below = paired[2, CUT:]
    parts = relay(paired, y_up(above), y_down(below))
    parts = [y_up(parts[0]), y_down(parts[1])]

    back, _ = lax.optimization_barrier((back, (above, below)))
    back_own = jnp.sum(back, axis=0)
    back_all = lax.all_to_all(
        jnp.broadcast_to(back_own[None], (span, ROWS, BS)), plane, 0, 0
    )
    in_part = in_partial(spread, back_all)
    in_grad = jnp.sum(lax.all_to_all(in_part, ("y", "core"), 0, 0), axis=0)

    whole = pl.BlockSpec(memory_space=pltpu.VMEM)
    slots, out_grad = pl.pallas_call(
        final_kernel,
        in_specs=[pl.BlockSpec(memory_space=pltpu.SMEM)] + [whole] * 3,
        out_specs=[whole, whole],
        out_shape=[
            jax.ShapeDtypeStruct((CAP, BS, BS), jnp.float32),
            jax.ShapeDtypeStruct((FO_ROWS, BS), jnp.float32),
        ],
        compiler_params=pltpu.CompilerParams(vmem_limit_bytes=50 * 1024 * 1024),
        cost_estimate=pl.CostEstimate(
            flops=10_000_000, bytes_accessed=16_000_000, transcendentals=0
        ),
        name="slots",
    )(mine, paired, *parts)
    return hidden, slots, in_grad, out_grad.T


def solution(mesh):
    split = Mesh(mesh.devices.reshape(NY, NC, NZ, NX), ("y", "core", "z", "x"))
    dp, mp = ("y", "core"), ("z", "x")
    return jax.shard_map(
        per_device,
        mesh=split,
        in_specs=(
            P(dp + mp, None),
            P(mp, None, None, None),
            P(mp, None),
            P(mp, None, None),
            P(mp, None),
            P(None, mp),
            P(dp, mp),
        ),
        out_specs=(
            P(dp, mp),
            P(mp + dp, None, None),
            P(mp + dp, None),
            P(None, mp + dp),
        ),
        check_vma=False,
    )
```

```python
import functools

import jax
import jax.numpy as jnp
from jax import lax
from jax.experimental import pallas as pl
from jax.experimental.pallas import tpu as pltpu
from jax.sharding import Mesh
from jax.sharding import PartitionSpec as P

highest = lax.Precision.HIGHEST
BS = 128
ROWS = 16
NX, NZ, NY, NC = 4, 8, 4, 2
COLS = 12
PER_STEP = 2
KB = 8
RB = 96
CAP = 18
GROUPS = NY * NC
SLOT_ROWS = CAP * BS
FO_ROWS = COLS * BS // GROUPS
CODE_ROWS = SLOT_ROWS + FO_ROWS
PART_ROWS = CODE_ROWS + 32
FINE = 256.0
ORDER = (
    ("across", (0, 0), (0, 2)),
    ("z_up", (0, 0), (-1, 0)),
    ("z_up", (-1, 0), (-2, 0)),
    ("z_down", (0, 0), (1, 0)),
    ("z_down", (1, 0), (2, 0)),
    ("x_up", (1, 0), (1, -1)),
    ("z_up", (0, 2), (-1, 2)),
    ("x_down", (0, 0), (0, 1)),
    ("x_up", (0, 0), (0, -1)),
    ("x_down", (-1, 0), (-1, 1)),
    ("x_up", (2, 0), (2, -1)),
    ("z_down", (0, 2), (1, 2)),
    ("x_up", (-2, 0), (-2, -1)),
    ("z_down", (0, 1), (1, 1)),
    ("z_up", (-2, 0), (-3, 0)),
    ("z_down", (2, 0), (3, 0)),
    ("x_up", (3, 0), (3, -1)),
    ("x_down", (-2, 0), (-2, 1)),
    ("z_up", (0, -1), (-1, -1)),
    ("x_down", (-3, 0), (-3, 1)),
    ("x_up", (-3, 0), (-3, -1)),
    ("x_down", (2, 0), (2, 1)),
    ("z_up", (-1, 2), (-2, 2)),
    ("z_up", (-2, 2), (-3, 2)),
    ("z_down", (1, 2), (2, 2)),
    ("z_up", (-3, 0), (4, 0)),
    ("z_down", (2, 2), (3, 2)),
    ("x_down", (3, 0), (3, 1)),
    ("x_up", (4, 0), (4, -1)),
    ("x_down", (4, 0), (4, 1)),
    ("z_down", (3, 2), (4, 2)),
)
CUT = 10 * BS


def shift(axis, size, step):
    pairs = [(i, (i + step) % size) for i in range(size)]
    return lambda value: lax.ppermute(value, axis, pairs)


def split_two(value):
    high = value.astype(jnp.bfloat16)
    low = (value - high.astype(jnp.float32)).astype(jnp.bfloat16)
    return high, low


def level_of(block):
    top = jnp.max(jnp.abs(block), axis=0, keepdims=True)
    return jnp.ceil(jnp.log2(jnp.maximum(top, 1e-30)) * FINE)


def encode(block, level):
    inverse = jnp.exp2(level * (-1.0 / FINE)) * 32700.0
    return jnp.floor(block * inverse + 0.5).astype(jnp.int32).astype(jnp.int16)


def decode(code, level):
    unit = jnp.exp2(level * (1.0 / FINE)) * (1.0 / 32700.0)
    return code.astype(jnp.int32).astype(jnp.float32) * unit


def main_kernel(
    counts, rows_ref, where_ref, place_ref, low_ref, weight_ref, factor_ref, up_ref, *rest
):
    arrays, rest = rest[: len(counts)], rest[len(counts) :]
    pieces = [ref.at[i] for ref, n in zip(arrays, counts) for i in range(n)]
    hidden_ref, send_ref, keep_ref, back_ref = rest[:4]
    tok, wide, low_two, codes, levels, sems = rest[4:]
    c = pl.program_id(0)
    tokens = NX * NZ * ROWS

    @pl.when(c == 0)
    def _():
        copies = [
            pltpu.make_async_copy(pieces[j], tok.at[place_ref[j]], sems.at[j])
            for j in range(NX * NZ)
        ]
        for copy in copies:
            copy.start()
        high, low = split_two(low_ref[...])
        low_two[:, :BS] = high
        low_two[:, BS:] = low
        wide[(KB + 1) * BS :, BS:] = jnp.zeros((BS, BS), jnp.bfloat16)
        back_ref[...] = jnp.zeros_like(back_ref)
        for copy in copies:
            copy.wait()

    for i in range(PER_STEP):
        col = c * PER_STEP + i
        here = slice(i * BS, (i + 1) * BS)
        for k in range(KB):
            high, low = split_two(weight_ref[i, k])
            wide[k * BS : (k + 1) * BS, :BS] = high
            wide[k * BS : (k + 1) * BS, BS:] = low
        f_high, f_low = split_two(factor_ref[:, here])
        wide[KB * BS : (KB + 1) * BS, :BS] = f_high
        wide[KB * BS : (KB + 1) * BS, BS:] = f_low
        wide[(KB + 1) * BS :, :BS] = f_high

        panel = jnp.concatenate(
            [tok[:, rows_ref[col * KB + k]].reshape(tokens, BS) for k in range(KB)]
            + [low_two[...]],
            axis=1,
        )
        both = jnp.dot(panel, wide[...], preferred_element_type=jnp.float32)
        v = both[:, :BS] + both[:, BS:]
        root = 0.7978845608028654
        square = v * v
        t = jnp.tanh(root * v * (1.0 + 0.044715 * square))
        half = 0.5 * (1.0 + t)
        hidden_ref[:, here] = (v * half).astype(jnp.bfloat16)
        slope = half + 0.5 * root * v * (1.0 - t * t) * (1.0 + 3.0 * 0.044715 * square)
        grad = up_ref[:, here].astype(jnp.float32) * slope

        g_high, g_low = split_two(grad)
        g_two = jnp.concatenate([g_high, g_low], axis=1)
        f_two = jnp.concatenate(
            [
                jnp.concatenate([f_high, f_high], axis=1),
                jnp.concatenate([f_low, jnp.zeros_like(f_low)], axis=1),
            ],
            axis=0,
        )
        back = lax.dot_general(
            g_two, f_two, (((1,), (1,)), ((), ())), preferred_element_type=jnp.float32
        )
        back_ref[...] += back[:, :BS] + back[:, BS:]

        grad_t = grad.T
        t_high, t_low = split_two(grad_t)
        gt_two = jnp.concatenate([t_high, t_low], axis=0)
        product = jnp.dot(gt_two, panel, preferred_element_type=jnp.float32)
        product = product[:BS] + product[BS:]
        for k in range(KB):
            block = product[:, k * BS : (k + 1) * BS]
            level = level_of(block)
            part = where_ref[0, col * KB + k]
            slot = where_ref[1, col * KB + k]
            codes[part, pl.ds(pl.multiple_of(slot * BS, BS), BS)] = encode(block, level)
            levels[part, pl.ds(slot, 1)] = level
        outer = product[:, KB * BS : (KB + 1) * BS] + product[:, (KB + 1) * BS :]
        for h in range(2):
            block = outer[h * 64 : (h + 1) * 64]
            level = level_of(block)
            part = where_ref[2, col * 2 + h]
            slot = where_ref[3, col * 2 + h]
            start = pl.multiple_of(SLOT_ROWS + slot * 64, 64)
            codes[part, pl.ds(start, 64)] = encode(block, level)
            levels[part, pl.ds(CAP + slot, 1)] = level

    @pl.when(c == COLS // PER_STEP - 1)
    def _():
        for part in range(2 * NY):
            codes[part, CODE_ROWS:] = levels[part].astype(jnp.int32).astype(jnp.int16)
        send = pltpu.make_async_copy(codes.at[pl.ds(0, NY)], send_ref, sems.at[0])
        keep = pltpu.make_async_copy(codes.at[pl.ds(NY, NY)], keep_ref, sems.at[1])
        send.start()
        keep.start()
        send.wait()
        keep.wait()


def blocks_of():
    spans = [(s * BS, BS, s) for s in range(CAP)]
    return spans + [(SLOT_ROWS + h * 64, 64, CAP + h) for h in range(FO_ROWS // 64)]


def pair_kernel(keep_ref, got_ref, out_ref, above_ref, below_ref):
    keep_levels = keep_ref[0, CODE_ROWS:].astype(jnp.int32).astype(jnp.float32)
    got_levels = got_ref[0, CODE_ROWS:].astype(jnp.int32).astype(jnp.float32)
    fresh = []
    for start, size, index in blocks_of():
        span = slice(start, start + size)
        total = decode(keep_ref[0, span], keep_levels[index : index + 1])
        total += decode(got_ref[0, span], got_levels[index : index + 1])
        level = level_of(total)
        out_ref[0, span] = encode(total, level)
        fresh.append(level)
    fresh.append(jnp.zeros((32 - len(fresh), BS), jnp.float32))
    fresh = jnp.concatenate(fresh, axis=0)
    out_ref[0, CODE_ROWS:] = fresh.astype(jnp.int32).astype(jnp.int16)

    @pl.when(pl.program_id(0) == 2)
    def _():
        above_ref[:CUT] = out_ref[0, :CUT]
        above_ref[CUT:] = out_ref[0, CODE_ROWS:]
        below_ref[...] = out_ref[0, CUT:]


def levels_in(rows):
    return rows.astype(jnp.int32).astype(jnp.float32)


def relay_kernel(up_ref, down_ref, above_ref, below_ref, up_out, down_out):
    for own, got, out, first in (
        (up_ref, above_ref, up_out, True),
        (down_ref, below_ref, down_out, False),
    ):
        own_levels = levels_in(own[0, CODE_ROWS:])
        got_levels = levels_in(got[CUT:] if first else got[CODE_ROWS - CUT :])
        fresh = []
        for start, size, index in blocks_of():
            span = slice(start, start + size)
            level = own_levels[index : index + 1]
            if (start < CUT) == first:
                offset = start if first else start - CUT
                total = decode(own[0, span], level)
                total += decode(got[offset : offset + size], got_levels[index : index + 1])
                level = level_of(total)
                out[span] = encode(total, level)
            else:
                out[span] = own[0, span]
            fresh.append(level)
        fresh.append(jnp.zeros((32 - len(fresh), BS), jnp.float32))
        fresh = jnp.concatenate(fresh, axis=0)
        out[CODE_ROWS:] = fresh.astype(jnp.int32).astype(jnp.int16)


def relay(paired, above, below):
    one = lambda i: pl.BlockSpec((1, PART_ROWS, BS), lambda _: (i, 0, 0))
    flat = lambda rows: pl.BlockSpec((rows, BS), lambda _: (0, 0))
    return pl.pallas_call(
        relay_kernel,
        grid=(1,),
        in_specs=[one(1), one(3), flat(above.shape[0]), flat(below.shape[0])],
        out_specs=[flat(PART_ROWS)] * 2,
        out_shape=[jax.ShapeDtypeStruct((PART_ROWS, BS), jnp.int16)] * 2,
        compiler_params=pltpu.CompilerParams(vmem_limit_bytes=30 * 1024 * 1024),
        cost_estimate=pl.CostEstimate(
            flops=40_000_000, bytes_accessed=40_000_000, transcendentals=0
        ),
        name="relay",
    )(paired, paired, above, below)


def final_kernel(count_ref, own_ref, *refs):
    parts, (slots_ref, outer_ref) = refs[:2], refs[2:]
    levels = [levels_in(own_ref[0, CODE_ROWS:])] + [levels_in(r[CODE_ROWS:]) for r in parts]
    count = count_ref[0]
    for start, size, index in blocks_of():
        span = slice(start, start + size)
        total = decode(own_ref[0, span], levels[0][index : index + 1])
        for i in range(2):
            total += decode(parts[i][span], levels[i + 1][index : index + 1])
        if index < CAP:
            slots_ref[index] = jnp.where(index < count, total.T, 0.0)
        else:
            h = index - CAP
            outer_ref[h * 64 : (h + 1) * 64] = total


def in_kernel(cols_ref, back_ref, out_ref):
    total = NZ * NX * ROWS
    high, low = split_two(back_ref[...].reshape(total, BS).T)
    two = jnp.concatenate([high, low], axis=0)
    panel = jnp.concatenate(
        [cols_ref[:, j].reshape(total, BS) for j in range(cols_ref.shape[1])], axis=1
    )
    both = jnp.dot(two, panel, preferred_element_type=jnp.float32)
    out_ref[...] = (both[:BS] + both[BS:]).T.reshape(out_ref.shape)


def in_partial(cols, back_all):
    whole = pl.BlockSpec(memory_space=pltpu.VMEM)
    size = cols.shape[1] * BS // GROUPS
    return pl.pallas_call(
        in_kernel,
        in_specs=[whole, whole],
        out_specs=whole,
        out_shape=jax.ShapeDtypeStruct((GROUPS, size, BS), jnp.float32),
        compiler_params=pltpu.CompilerParams(vmem_limit_bytes=30 * 1024 * 1024),
        name="into",
    )(cols, back_all)


def gather_tokens(own):
    moves = {
        "z_up": shift("z", NZ, 1),
        "z_down": shift("z", NZ, -1),
        "x_up": shift("x", NX, 1),
        "x_down": shift("x", NX, -1),
        "across": shift("x", NX, 2),
    }
    held = {(0, 0): own[None]}
    for name, source, target in ORDER:
        held[target] = moves[name](held[source])
    return list(held.values()), [[key] for key in held]


def per_device(tokens, block_weights, block_rows, block_owners, factor_in, factor_out, upstream):
    own = jnp.transpose(tokens.reshape(ROWS, RB, BS), (1, 0, 2))
    span = NX * NZ
    per = RB // span
    plane = ("z", "x")
    arrays, keys = gather_tokens(own)
    spread = lax.all_to_all(own.reshape(span, per, ROWS, BS), plane, 0, 0)
    factor = factor_in.reshape(per, BS, BS)
    partial = jnp.einsum(
        "sbtf,bfr->str", spread.astype(jnp.float32), factor, precision=highest
    )
    low_own = jnp.sum(lax.all_to_all(partial, plane, 0, 0), axis=0)
    low = lax.all_to_all(jnp.broadcast_to(low_own[None], (span, ROWS, BS)), plane, 0, 0)
    z, x = lax.axis_index("z"), lax.axis_index("x")
    y, core = lax.axis_index("y"), lax.axis_index("core")
    place = [((z + a) % NZ) * NX + (x + b) % NX for group in keys for a, b in group]
    place = jnp.stack(place).astype(jnp.int32)
    low = low.reshape(span * ROWS, BS)

    owners = block_owners.reshape(-1)
    count_all = owners.shape[0]
    marks = (owners[:, None] == jnp.arange(GROUPS, dtype=jnp.int32)[None, :]).astype(jnp.int32)
    before = (
        jnp.arange(count_all, dtype=jnp.int32)[:, None]
        > jnp.arange(count_all, dtype=jnp.int32)[None, :]
    ) & (owners[:, None] == owners[None, :])
    rank = jnp.sum(before.astype(jnp.int32), axis=1)

    def part_of(owner):
        turn = (owner // NC - y) % NY
        return turn + jnp.where(owner % NC == core, NY, 0)

    halves = jnp.arange(2 * COLS, dtype=jnp.int32)
    per_owner = FO_ROWS // 64
    pad = count_all - 2 * COLS
    where = jnp.stack(
        [
            part_of(owners),
            rank,
            jnp.pad(part_of(halves // per_owner), (0, pad)),
            jnp.pad(halves % per_owner, (0, pad)),
        ]
    ).astype(jnp.int32)
    counts = jnp.sum(marks, axis=0)
    mine = jnp.sum(
        jnp.where(jnp.arange(GROUPS) == y * NC + core, counts, 0), dtype=jnp.int32
    ).reshape(1)

    total = span * ROWS
    anywhere = pl.BlockSpec(memory_space=pl.ANY)
    hidden, send, keep, back = pl.pallas_call(
        functools.partial(main_kernel, [len(g) for g in keys]),
        grid_spec=pltpu.PrefetchScalarGridSpec(
            num_scalar_prefetch=3,
            grid=(COLS // PER_STEP,),
            in_specs=[
                pl.BlockSpec((total, BS), lambda c, *_: (0, 0)),
                pl.BlockSpec((PER_STEP, KB, BS, BS), lambda c, *_: (c, 0, 0, 0)),
                pl.BlockSpec((BS, PER_STEP * BS), lambda c, *_: (0, c)),
                pl.BlockSpec((total, PER_STEP * BS), lambda c, *_: (0, c)),
            ]
            + [anywhere] * len(arrays),
            out_specs=[
                pl.BlockSpec((total, PER_STEP * BS), lambda c, *_: (0, c)),
                anywhere,
                anywhere,
                pl.BlockSpec((total, BS), lambda c, *_: (0, 0)),
            ],
            scratch_shapes=[
                pltpu.VMEM((span, RB, ROWS, BS), jnp.bfloat16),
                pltpu.VMEM(((KB + 2) * BS, 2 * BS), jnp.bfloat16),
                pltpu.VMEM((total, 2 * BS), jnp.bfloat16),
                pltpu.VMEM((2 * NY, PART_ROWS, BS), jnp.int16),
                pltpu.VMEM((2 * NY, 32, BS), jnp.float32),
                pltpu.SemaphoreType.DMA((span,)),
            ],
        ),
        out_shape=[
            jax.ShapeDtypeStruct((total, COLS * BS), jnp.bfloat16),
            jax.ShapeDtypeStruct((NY, PART_ROWS, BS), jnp.int16),
            jax.ShapeDtypeStruct((NY, PART_ROWS, BS), jnp.int16),
            jax.ShapeDtypeStruct((total, BS), jnp.float32),
        ],
        compiler_params=pltpu.CompilerParams(vmem_limit_bytes=50 * 1024 * 1024),
        name="columns",
    )(
        block_rows.reshape(-1), where, place,
        low, block_weights, factor_out, upstream, *arrays,
    )

    got = shift("core", NC, 1)(send)
    back = lax.all_to_all(back.reshape(span, ROWS, BS), plane, 0, 0)
    flat = lambda rows: pl.BlockSpec((rows, BS), lambda i: (0, 0))
    heights = (CUT + PART_ROWS - CODE_ROWS, PART_ROWS - CUT)
    paired, above, below = pl.pallas_call(
        pair_kernel,
        grid=(NY,),
        in_specs=[pl.BlockSpec((1, PART_ROWS, BS), lambda i: (i, 0, 0))] * 2,
        out_specs=[pl.BlockSpec((1, PART_ROWS, BS), lambda i: (i, 0, 0))]
        + [flat(rows) for rows in heights],
        out_shape=[jax.ShapeDtypeStruct((NY, PART_ROWS, BS), jnp.int16)]
        + [jax.ShapeDtypeStruct((rows, BS), jnp.int16) for rows in heights],
        compiler_params=pltpu.CompilerParams(vmem_limit_bytes=50 * 1024 * 1024),
        name="pairs",
    )(keep, got)
    y_up, y_down = shift("y", NY, 1), shift("y", NY, -1)
    parts = relay(paired, y_up(above), y_down(below))
    parts = [y_up(parts[0]), y_down(parts[1])]

    back, _ = lax.optimization_barrier((back, (above, below)))
    back_own = jnp.sum(back, axis=0)
    back_all = lax.all_to_all(
        jnp.broadcast_to(back_own[None], (span, ROWS, BS)), plane, 0, 0
    )
    in_part = in_partial(spread, back_all)
    in_grad = jnp.sum(lax.all_to_all(in_part, ("y", "core"), 0, 0), axis=0)

    whole = pl.BlockSpec(memory_space=pltpu.VMEM)
    slots, out_grad = pl.pallas_call(
        final_kernel,
        in_specs=[pl.BlockSpec(memory_space=pltpu.SMEM)] + [whole] * 3,
        out_specs=[whole, whole],
        out_shape=[
            jax.ShapeDtypeStruct((CAP, BS, BS), jnp.float32),
            jax.ShapeDtypeStruct((FO_ROWS, BS), jnp.float32),
        ],
        compiler_params=pltpu.CompilerParams(vmem_limit_bytes=50 * 1024 * 1024),
        cost_estimate=pl.CostEstimate(
            flops=10_000_000, bytes_accessed=16_000_000, transcendentals=0
        ),
        name="slots",
    )(mine, paired, *parts)
    return hidden, slots, in_grad, out_grad.T


def solution(mesh):
    split = Mesh(mesh.devices.reshape(NY, NC, NZ, NX), ("y", "core", "z", "x"))
    dp, mp = ("y", "core"), ("z", "x")
    return jax.shard_map(
        per_device,
        mesh=split,
        in_specs=(
            P(dp + mp, None),
            P(mp, None, None, None),
            P(mp, None),
            P(mp, None, None),
            P(mp, None),
            P(None, mp),
            P(dp, mp),
        ),
        out_specs=(
            P(dp, mp),
            P(mp + dp, None, None),
            P(mp + dp, None),
            P(None, mp + dp),
        ),
        check_vma=False,
    )
```
